128 devices in a mesh: rep: 16 (over z, y_lo, core), shard: 8 (over x, y_hi).
Axes of the slice: x: 4, y: 4 (y_hi: 2, y_lo: 2; y = y_hi * 2 + y_lo), z: 4, core: 2. Of those that a mesh axis runs over, the one named last changes fastest.
Arguments:
- tokens: bfloat16 [32768, 1024], P(('rep', 'shard')), may hold values from -24 to 24
- cotangent: bfloat16 [32768, 1024], P(('rep', 'shard')), may hold values from -6 to 6
- segment_ids: int32 [128, 256], P(('rep', 'shard')), may hold values from 0 to 2, as said below
- positions: int32 [128, 256], P(('rep', 'shard')), may hold values from 0 to 506, as said below
- master_qkv: float32 [1024, 4096], P('shard'), may hold values from -0.1875 to 0.1875
- master_out: float32 [2048, 1024], P('shard'), may hold values from -0.5 to 0.5
- master_gate_up: float32 [1024, 6144], P('shard'), may hold values from -0.1875 to 0.1875
- master_down: float32 [3072, 1024], P('shard'), may hold values from -0.109375 to 0.109375
- master_gains: float32 [2304], P('shard'), may hold values from 0.5 to 1.5
- first_qkv: float32 [1024, 4096], P('shard'), may hold values from -128 to 128
- first_out: float32 [2048, 1024], P('shard'), may hold values from -32 to 32
- first_gate_up: float32 [1024, 6144], P('shard'), may hold values from -48 to 48
- first_down: float32 [3072, 1024], P('shard'), may hold values from -64 to 64
- first_gains: float32 [2304], P('shard'), may hold values from -128 to 128
- second_qkv: float32 [1024, 4096], P('shard'), may hold values from 32.768 to 131.072
- second_out: float32 [2048, 1024], P('shard'), may hold values from 2.94912 to 11.79648
- second_gate_up: float32 [1024, 6144], P('shard'), may hold values from 5.24288 to 20.97152
- second_down: float32 [3072, 1024], P('shard'), may hold values from 11.79648 to 47.18592
- second_gains: float32 [2304], P('shard'), may hold values from 32.768 to 131.072
Outputs:
- activations: bfloat16 [32768, 1024], P(('rep', 'shard'))
- input_grad: bfloat16 [32768, 1024], P(('rep', 'shard'))
- new_master_qkv: float32 [1024, 4096], P('shard')
- new_master_out: float32 [2048, 1024], P('shard')
- new_master_gate_up: float32 [1024, 6144], P('shard')
- new_master_down: float32 [3072, 1024], P('shard')
- new_master_gains: float32 [2304], P('shard')
- new_first_qkv: float32 [1024, 4096], P('shard')
- new_first_out: float32 [2048, 1024], P('shard')
- new_first_gate_up: float32 [1024, 6144], P('shard')
- new_first_down: float32 [3072, 1024], P('shard')
- new_first_gains: float32 [2304], P('shard')
- new_second_qkv: float32 [1024, 4096], P('shard')
- new_second_out: float32 [2048, 1024], P('shard')
- new_second_gate_up: float32 [1024, 6144], P('shard')
- new_second_down: float32 [3072, 1024], P('shard')
- new_second_gains: float32 [2304], P('shard')
The draws below stay inside these ranges and needn't reach their ends.
Inputs may be any that keep to these rules, and one draw needn't show every extreme that they name: `segment_ids`: each row holds 3 documents, numbered from 0 and never falling along the row, each of one token or more. Within each document positions are 0 at its first token and rise by 1 or 2 from one token to the next; in one sequence the first document holds 254 tokens and rises by 2 throughout.
All inputs are finite; a program needn't handle non-finite values.
Results may differ from the reference program's by a relative error of at most 0.024.
Values may be sent and summed in bfloat16 or wider, within the bound.
A program may use at most 320 MiB of HBM per device.

```python
import math
import jax
import jax.numpy as jnp
from jax import lax

D = 1024
HEADS = 16
KV_HEADS = 8
HD = 128
FF = 3072
TOK_DEV = 256
DOCS = 3
STEP = 10
SEQS = 128
TOKENS = 32768
Q_WIDTH = 2048
KV_WIDTH = 1024
GAINS = 2304


def document_layout(key):
    chosen = jax.random.randint(jax.random.fold_in(key, 7), (), 0, SEQS)
    places = jnp.arange(TOK_DEV)
    packed_cuts = (TOK_DEV - DOCS + 1 + jnp.arange(DOCS - 1)).astype(jnp.int32)

    def one_row(row_key, special):
        order = jax.random.permutation(row_key, TOK_DEV - 1) + 1
        cuts = jnp.sort(order[:DOCS - 1]).astype(jnp.int32)
        cuts = jnp.where(special, packed_cuts, cuts)
        passed = cuts[:, None] <= places[None, :]
        segment = jnp.sum(passed.astype(jnp.int32), axis=0)
        start = jnp.max(jnp.where(passed, cuts[:, None], 0), axis=0)
        return (segment.astype(jnp.int32), start.astype(jnp.int32))
    rows = jnp.arange(SEQS) == chosen
    segment, start = jax.vmap(one_row)(jax.random.split(key, SEQS), rows)
    return (segment, start, rows)


def draw_segment_ids(key, part):
    segment, start, rows = document_layout(key)
    return segment


def draw_positions(key, part):
    segment, start, rows = document_layout(key)
    key = jax.random.fold_in(key, 5)
    strides = jax.random.randint(key, (SEQS, TOK_DEV), 1, 3)
    strides = jnp.where(rows[:, None], 2, strides).astype(jnp.int32)
    running = jnp.cumsum(strides, axis=1)
    first = jnp.take_along_axis(running, start, axis=1)
    return (running - first).astype(jnp.int32)


def spiked(values, own_key, source, target, blocks, factor):
    owner, partner = [(jnp.arange(values.shape[axis_at]) // (values.shape[axis_at] // blocks)).reshape([-1 if axis == axis_at else 1 for axis in range(values.ndim)]) for axis_at in (source, target)]
    chosen = jax.random.permutation(own_key, blocks)[partner]
    strong = (owner == chosen) | (owner == (partner + blocks // 2) % blocks)
    return jnp.where(strong, factor * values, values)


def shard_levels(own_key, dims, shards, least, top_value):
    level, own = 1.0, jax.random.fold_in(own_key, 6)
    for axis_at, shards_of in shards:
        steps = jnp.exp(jax.random.uniform(jax.random.fold_in(own, axis_at), (shards_of,), jnp.float32, least / len(shards), top_value / len(shards)))
        level = level * jnp.repeat(steps, dims[axis_at] // shards_of).reshape([-1 if axis == axis_at else 1 for axis in range(len(dims))])
    return level


def scatter_about(own_key, extent, deviation, limit, cuts=(), dtype=jnp.bfloat16):
    array = deviation * jax.random.normal(own_key, extent, jnp.float32)
    if cuts:
        array = array * shard_levels(own_key, extent, cuts, -0.22, 0.18)
    return jnp.clip(array, -limit, limit).astype(dtype)


def gaussian_with(own_key, dims, spread, reach, pieces, heavy, kind=jnp.bfloat16):
    drawn = spread * jax.random.normal(own_key, dims, jnp.float32)
    if pieces:
        drawn = drawn * shard_levels(own_key, dims, pieces, -0.22, 0.18)
    return jnp.clip(spiked(drawn, jax.random.fold_in(own_key, 3), *heavy), -reach, reach).astype(kind)


def setup_inputs(seed: int = 0) -> dict:
    key_of = jax.random.split(jax.random.key(seed), 20)
    return {
        "tokens": gaussian_with(key_of[0], (TOKENS, D), 1.0, 24.0, ((0, 128),), (0, 1, 128, 5.5)),
        "cotangent": scatter_about(key_of[1], (TOKENS, D), 1.0, 6.0, ((0, 128),)),
        "segment_ids": draw_segment_ids(jax.random.fold_in(key_of[19], 71), 0),
        "positions": draw_positions(jax.random.fold_in(key_of[19], 71), 0),
        "master_qkv": scatter_about(key_of[4], (D, Q_WIDTH + 2 * KV_WIDTH), D ** -0.5, 0.1875, ((0, 8),), jnp.float32),
        "master_out": scatter_about(key_of[5], (Q_WIDTH, D), (Q_WIDTH // 16) ** -0.5, 0.5, ((0, 8),), jnp.float32),
        "master_gate_up": scatter_about(key_of[6], (D, 2 * FF), D ** -0.5, 0.1875, ((0, 8),), jnp.float32),
        "master_down": scatter_about(key_of[7], (FF, D), FF ** -0.5, 0.109375, ((0, 8),), jnp.float32),
        "master_gains": jnp.clip(1.0 + 0.1 * jax.random.normal(key_of[8], (GAINS,), jnp.float32), 0.5, 1.5),
        "first_qkv": scatter_about(key_of[9], (D, Q_WIDTH + 2 * KV_WIDTH), (0.11 * TOKENS ** 0.5), 128.0, ((0, 8),), jnp.float32),
        "first_out": scatter_about(key_of[10], (Q_WIDTH, D), (0.033 * TOKENS ** 0.5), 32.0, ((0, 8),), jnp.float32),
        "first_gate_up": scatter_about(key_of[11], (D, 2 * FF), (0.044 * TOKENS ** 0.5), 48.0, ((0, 8),), jnp.float32),
        "first_down": scatter_about(key_of[12], (FF, D), (0.066 * TOKENS ** 0.5), 64.0, ((0, 8),), jnp.float32),
        "first_gains": scatter_about(key_of[13], (GAINS,), (0.11 * TOKENS ** 0.5), 128.0, ((0, 8),), jnp.float32),
        "second_qkv": jnp.clip(jnp.exp(math.log(131.072) - 1.3862944 * jax.random.uniform(key_of[14], (D, Q_WIDTH + 2 * KV_WIDTH), jnp.float32) ** shard_levels(key_of[14], (D, Q_WIDTH + 2 * KV_WIDTH), ((0, 8),), -0.2, 0.2)), 32.768, 131.072),
        "second_out": jnp.clip(jnp.exp(math.log(11.79648) - 1.3862944 * jax.random.uniform(key_of[15], (Q_WIDTH, D), jnp.float32) ** shard_levels(key_of[15], (Q_WIDTH, D), ((0, 8),), -0.2, 0.2)), 2.94912, 11.79648),
        "second_gate_up": jnp.clip(jnp.exp(math.log(20.97152) - 1.3862944 * jax.random.uniform(key_of[16], (D, 2 * FF), jnp.float32) ** shard_levels(key_of[16], (D, 2 * FF), ((0, 8),), -0.2, 0.2)), 5.24288, 20.97152),
        "second_down": jnp.clip(jnp.exp(math.log(47.18592) - 1.3862944 * jax.random.uniform(key_of[17], (FF, D), jnp.float32) ** shard_levels(key_of[17], (FF, D), ((0, 8),), -0.2, 0.2)), 11.79648, 47.18592),
        "second_gains": jnp.clip(jnp.exp(math.log(131.072) - 1.3862944 * jax.random.uniform(key_of[18], (GAINS,), jnp.float32) ** shard_levels(key_of[18], (GAINS,), ((0, 8),), -0.2, 0.2)), 32.768, 131.072),
    }


@jax.custom_vjp
def low(v):
    return lax.optimization_barrier(v.astype(jnp.bfloat16)).astype(jnp.float32)

@jax.custom_vjp
def low_back(v):
    return v

def low_keep(v):
    return (low(v), None)

def low_pass(kept, grad):
    return (grad,)

def back_keep(v):
    return (v, None)

def back_low(kept, grad):
    return (low(grad),)
low.defvjp(low_keep, low_pass)
low_back.defvjp(back_keep, back_low)

def normed(values, gain):
    return values * lax.rsqrt(lax.optimization_barrier(jnp.mean(values * values, axis=-1, keepdims=True)) + 1e-06) * gain

def turned(values):
    middle = values.shape[-1] // 2
    return jnp.concatenate([-values[..., middle:], values[..., :middle]], axis=-1)

def rotate(values, cosine, sine):
    return values * cosine + turned(values) * sine

def rope_tables(positions):
    freq = jnp.exp(jnp.arange(HD // 2).astype(jnp.float32) * (-2.0 * math.log(1000000.0) / HD))
    angle = positions.astype(jnp.float32)[..., None] * freq
    cosine = jnp.cos(angle)
    sine = jnp.sin(angle)
    return (jnp.concatenate([cosine, cosine], axis=-1), jnp.concatenate([sine, sine], axis=-1))

def matmul(left, right):
    return jnp.einsum('...d,de->...e', left, right, precision=lax.Precision.HIGHEST)

def forward(inputs, segments, positions, w_qkv, w_out, w_gate_up, w_down, gains):
    groups, length = segments.shape
    share = HEADS // KV_HEADS
    gain_in = gains[:D]
    gain_mid = gains[D:2 * D]
    gain_query = gains[2 * D:2 * D + HD]
    gain_key = gains[2 * D + HD:]
    hidden_in = low(normed(inputs, gain_in))
    project = low_back(matmul(hidden_in, w_qkv))
    queries = project[..., :Q_WIDTH].reshape(groups, length, KV_HEADS, share, HD)
    keys_raw = project[..., Q_WIDTH:Q_WIDTH + KV_WIDTH].reshape(groups, length, KV_HEADS, HD)
    values_raw = project[..., Q_WIDTH + KV_WIDTH:].reshape(groups, length, KV_HEADS, HD)
    cosine, sine = rope_tables(positions)
    rotated_q = low(rotate(normed(queries, gain_query), cosine[:, :, None, None, :], sine[:, :, None, None, :]))
    rotated_k = low(rotate(normed(keys_raw, gain_key), cosine[:, :, None, :], sine[:, :, None, :]))
    values = low(values_raw)
    scores = low_back(jnp.einsum('gtkrd,gskd->gkrts', rotated_q, rotated_k, precision=lax.Precision.HIGHEST)) * HD ** (-0.5)
    places = jnp.arange(length)
    allowed = (places[None, :] <= places[:, None])[None] & (segments[:, :, None] == segments[:, None, :])
    scores = jnp.where(allowed[:, None, None], scores, -1e+30)
    top = lax.optimization_barrier(jnp.max(scores, axis=-1, keepdims=True))
    expo = jnp.exp(scores - top)
    probs = low(expo / lax.optimization_barrier(jnp.sum(expo, axis=-1, keepdims=True)))
    mixed = jnp.einsum('gkrts,gskd->gtkrd', probs, values, precision=lax.Precision.HIGHEST)
    mixed = low_back(low(mixed.reshape(groups, length, Q_WIDTH)))
    middle = inputs + low_back(matmul(mixed, w_out))
    hidden_mid = low(normed(middle, gain_mid))
    gate_up = low_back(matmul(hidden_mid, w_gate_up))
    active = low(jax.nn.silu(gate_up[..., :FF]) * gate_up[..., FF:])
    return middle + low_back(matmul(active, w_down))

def adamw_step(master, first, second, gradient, rate, decay):
    first_new = 0.9 * first + 0.1 * gradient
    second_new = 0.999 * second + 0.001 * gradient * gradient
    direction = first_new / (1.0 - 0.9 ** STEP) / (jnp.sqrt(second_new / (1.0 - 0.999 ** STEP)) + 1e-08)
    return (master - rate * (direction + decay * master), first_new, second_new)

def reference(tokens, cotangent, segment_ids, positions, master_qkv, master_out, master_gate_up, master_down, master_gains, first_qkv, first_out, first_gate_up, first_down, first_gains, second_qkv, second_out, second_gate_up, second_down, second_gains):
    masters = (master_qkv, master_out, master_gate_up, master_down, master_gains)
    weights = tuple((master.astype(jnp.bfloat16).astype(jnp.float32) for master in masters))
    sequences = segment_ids.shape[0]
    group = min(sequences, max(1, 4096 // TOK_DEV))
    count = sequences // group

    def one_group(totals, block):
        token_block, back_block, segment_block, position_block = block

        def apply(inputs, *params):
            return forward(inputs, segment_block, position_block, *params)
        result, pull = jax.vjp(apply, token_block.astype(jnp.float32), *weights)
        grads = pull(back_block.astype(jnp.float32))
        totals = tuple((total + piece for total, piece in zip(totals, grads[1:])))
        return (totals, (result.astype(jnp.bfloat16), grads[0].astype(jnp.bfloat16)))
    zeros = tuple((jnp.zeros_like(weight) for weight in weights))
    blocks = (tokens.reshape(count, group, TOK_DEV, D), cotangent.reshape(count, group, TOK_DEV, D), segment_ids.reshape(count, group, TOK_DEV), positions.reshape(count, group, TOK_DEV))
    totals, (results, backs) = lax.scan(one_group, zeros, blocks)
    activations = results.reshape(TOKENS, D)
    input_grad = backs.reshape(TOKENS, D)
    firsts = (first_qkv, first_out, first_gate_up, first_down, first_gains)
    seconds = (second_qkv, second_out, second_gate_up, second_down, second_gains)
    rates = (0.05, 0.05, 0.05, 0.05, 0.4)
    decays = (0.1, 0.1, 0.1, 0.1, 0.0)
    updated = [adamw_step(masters[index], firsts[index], seconds[index], totals[index], rates[index], decays[index]) for index in range(5)]
    return (activations, input_grad, updated[0][0], updated[1][0], updated[2][0], updated[3][0], updated[4][0], updated[0][1], updated[1][1], updated[2][1], updated[3][1], updated[4][1], updated[0][2], updated[1][2], updated[2][2], updated[3][2], updated[4][2])
```

```python
import math

import jax
import jax.numpy as jnp
from jax import lax
from jax.experimental import pallas as pl
from jax.experimental.pallas import tpu as pltpu
from jax.sharding import PartitionSpec as P

D = 1024
HEADS = 16
KV_HEADS = 8
HD = 128
FF = 3072
STEP = 10
Q_WIDTH = 2048
KV_WIDTH = 1024
TOK = 256
F32 = jnp.float32
BF16 = jnp.bfloat16
EPS = 1e-06
SCALE = HD ** (-0.5)

QKV0, OUT0, GAIN0, GU0, DN0, WCOLS = 0, 2048, 3072, 3200, 6272, 7808
G_OUT, G_GAIN, G_DN, G_COLS = 0, 1024, 1152, 2688
S_QKV, S_GU = 2688, 4736
ROTATIONS = (("x", "y", "z"), ("y", "z", "x"), ("z", "x", "y"))


def dot(left, right):
    return jnp.dot(left, right, preferred_element_type=F32)


def dot_nt(left, right):
    return lax.dot_general(left, right, (((1,), (1,)), ((), ())), preferred_element_type=F32)


def dot_tn(left, right):
    return lax.dot_general(left, right, (((0,), (0,)), ((), ())), preferred_element_type=F32)


def lanes(start, size, step=128):
    return pl.ds(start if isinstance(start, int) else pl.multiple_of(start, step), size)


def coordinates():
    rep = lax.axis_index("rep")
    shard = lax.axis_index("shard")
    return {
        "x": shard // 2,
        "y": (shard % 2) * 2 + (rep // 2) % 2,
        "z": rep // 4,
        "c": rep % 2,
    }


def device(at):
    return {"rep": at["z"] * 4 + (at["y"] % 2) * 2 + at["c"], "shard": at["x"] * 2 + at["y"] // 2}


def moved(me, axis, by):
    return {**me, axis: (me[axis] + by + 4) % 4}


def view(ref, select, offset, size):
    where = tuple(select.get(axis, slice(None)) for axis in "xyz")
    return ref.at[where + (slice(None), lanes(offset, size))]


def layer_kernel(
    tokens,
    cotangent,
    tables,
    bias,
    piece,
    activations,
    input_grad,
    summed,
    weights,
    grads,
    other_weights,
    got_far,
    got_near,
    got_two,
    got_three,
    toks,
    cots,
    rope,
    mask,
    hidden,
    raw,
    rotated,
    vals,
    mixed,
    part,
    got_part,
    got_down,
    middle,
    hidden_mid,
    gate_up,
    active,
    branch,
    turned_lhs,
    out_low,
    gains_acc,
    local_sem,
    send_sem,
    recv_sem,
):
    me = coordinates()
    c = me["c"]
    sib = 1 - c
    x, y, z = me["x"], me["y"], me["z"]
    sibling = device({**me, "c": sib})
    used = [0]

    class Transfer:
        def __init__(self, source, there, here, target):
            self.index = used[0]
            used[0] += 1
            self.source, self.there, self.here, self.target = source, there, here, target
            self.copy(source, there).start()

        def copy(self, source, there):
            return pltpu.make_async_remote_copy(
                src_ref=source,
                dst_ref=there,
                send_sem=send_sem.at[self.index],
                recv_sem=recv_sem.at[self.index],
                device_id=self.target,
                device_id_type=pl.DeviceIdType.MESH,
            )

        def arrived(self):
            self.copy(self.here, self.here).wait_recv()

        def sent(self):
            self.copy(self.source, self.there).wait_send()

    pending = []

    def send(source, there, here, target):
        transfer = Transfer(source, there, here, target)
        pending.append(transfer)
        return transfer

    def flush():
        while pending:
            pending.pop(0).sent()

    def arrive(transfers):
        for transfer in transfers:
            transfer.arrived()

    own = view(weights, {"x": x, "y": y, "z": z}, 0, WCOLS)
    inward = [
        (tokens, toks.at[c]),
        (cotangent, cots.at[c]),
        (tables, rope.at[c]),
        (bias, mask.at[c]),
        (piece, own),
    ]
    for index, (source, target) in enumerate(inward):
        pltpu.make_async_copy(source, target, local_sem.at[index]).start()

    barrier = pltpu.get_barrier_semaphore()
    friends = [sibling] + [device(moved(me, axis, by)) for axis in "xyz" for by in (1, 2, 3)]
    for friend in friends:
        pl.semaphore_signal(barrier, inc=1, device_id=friend, device_id_type=pl.DeviceIdType.MESH)
    for index, (source, target) in enumerate(inward):
        pltpu.make_async_copy(source, target, local_sem.at[index]).wait()
    pl.semaphore_wait(barrier, len(friends))

    def gather_one(rotation, offset, size):
        first, second, third = rotation
        source = view(weights, {"x": x, "y": y, "z": z}, offset, size)
        out = []
        for by in (1, 2, 3):
            here = view(weights, {**{"x": x, "y": y, "z": z}, third: (me[third] - by + 4) % 4}, offset, size)
            out.append(send(source, source, here, device(moved(me, third, by))))
        return out

    def gather_two(rotation, offset, size):
        first, second, third = rotation
        source = view(weights, {first: me[first], second: me[second]}, offset, size)
        out = []
        for by in (1, 2, 3):
            here = view(weights, {first: me[first], second: (me[second] - by + 4) % 4}, offset, size)
            out.append(send(source, source, here, device(moved(me, second, by))))
        return out

    def gather_three(rotation, offset, size):
        first = rotation[0]
        source = view(weights, {first: me[first]}, offset, size)
        out = []
        for by in (1, 3):
            here = view(weights, {first: (me[first] - by + 4) % 4}, offset, size)
            out.append(send(source, source, here, device(moved(me, first, by))))
        return out

    def gather_four(rotation, offset, size):
        first, second = rotation[0], rotation[1]
        out = []
        for by, half in ((1, 0), (3, 1)):
            rows = pl.ds(2 * half, 2)
            source = view(weights, {first: (me[first] - by + 4) % 4, second: rows}, offset, size)
            here = view(weights, {first: (me[first] + 2) % 4, second: rows}, offset, size)
            out.append(send(source, source, here, device(moved(me, first, by))))
        return out

    chunks = (((0, 1024), (1024, 1024), (2048, 1152)), ((GU0, 1536), (GU0 + 1536, 1536), (DN0, 1536)))
    steps = (gather_one, gather_two, gather_three, gather_four)
    flying = [[None] * 3 for _ in chunks]

    def pump(chunk, step):
        for index, rotation in enumerate(ROTATIONS):
            if step:
                arrive(flying[chunk][index])
            if step < 4:
                flying[chunk][index] = steps[step](rotation, *chunks[chunk][index])

    pump(0, 0)
    early = [
        send(toks.at[c], toks.at[c], toks.at[sib], sibling),
        send(rope.at[c], rope.at[c], rope.at[sib], sibling),
        send(mask.at[c], mask.at[c], mask.at[sib], sibling),
        send(cots.at[c], cots.at[c], cots.at[sib], sibling),
    ]
    pump(1, 0)
    pump(0, 1)
    pump(1, 1)
    pump(0, 2)
    pump(1, 2)
    arrive(early)
    pump(0, 3)
    pump(0, 4)

    def to_other(offset, size, at):
        return send(
            view(weights, {"x": pl.ds(2 * sib, 2)}, offset, size),
            view(other_weights, {}, at, size),
            view(other_weights, {}, at, size),
            sibling,
        )

    other_out = to_other(OUT0, 1024, 0)

    def weight(offset, size):
        return weights[:, :, :, :, lanes(offset, size)].reshape(1024, size)

    def weight_rows(row, offset, size):
        return weights[row, :, :, :, lanes(offset, size)].reshape(256, size)

    def weight_own(offset, size):
        return weights[pl.ds(2 * c, 2), :, :, :, lanes(offset, size)].reshape(512, size)

    def weight_other(offset, size):
        return other_weights[:, :, :, :, lanes(offset, size)].reshape(512, size)

    gain_rows = jnp.zeros((16, 128), F32)
    head_rows = jnp.zeros((16, 128), F32)
    for part_x in range(4):
        for part_y in (0, 2):
            gain_rows += weights[part_x, part_y, 0, :, pl.ds(GAIN0, 128)].astype(F32)
            head_rows += weights[part_x, part_y, 1, :, pl.ds(GAIN0, 128)].astype(F32)
    gain_in = jnp.concatenate([gain_rows[i : i + 1] for i in range(8)], axis=1)
    gain_mid = jnp.concatenate([gain_rows[i : i + 1] for i in range(8, 16)], axis=1)
    gain_query = head_rows[0:1]
    gain_key = head_rows[1:2]

    def unit_of(values):
        scale = lax.rsqrt(jnp.mean(values * values, axis=-1, keepdims=True) + EPS)
        return values * scale, scale

    def norm_back(upstream, gain, unit, scale):
        pushed = upstream * gain
        inner = jnp.mean(pushed * unit, axis=-1, keepdims=True)
        return scale * (pushed - unit * inner)

    for b in range(2):
        unit, _ = unit_of(toks[b].astype(F32))
        hidden[b] = (unit * gain_in).astype(BF16)

    def all_hidden():
        return hidden[...].reshape(512, 1024)

    def project_heads(t, carry):
        values = dot(all_hidden(), weight(QKV0 + t * 256, 256))
        raw[:, lanes(t * 256, 256)] = values.astype(BF16)
        gain = jnp.where(t < 4, gain_query, gain_key)
        cosine = rope[:, :, 0:128].reshape(512, 128)
        sine = rope[:, :, 128:256].reshape(512, 128)
        for h in range(2):
            unit, _ = unit_of(values[:, h * 128 : (h + 1) * 128])
            normal = unit * gain
            rotated[2 * t + h] = (normal * cosine + pltpu.roll(normal, 64, 1) * sine).astype(BF16)
        return carry

    lax.fori_loop(0, 6, project_heads, 0)

    def project_values(t, carry):
        values = dot(all_hidden(), weight(QKV0 + 1536 + t * 256, 256)).astype(BF16)
        vals[2 * t] = values[:, :128]
        vals[2 * t + 1] = values[:, 128:]
        return carry

    lax.fori_loop(0, 2, project_values, 0)

    def probabilities(b, g):
        rows = pl.ds(pl.multiple_of(b * 256, 256), 256)
        query = rotated[pl.ds(2 * g, 2), rows, :].reshape(512, 128)
        key = rotated[8 + g, rows, :]
        scores = dot_nt(query, key).reshape(2, 256, 256) * SCALE + mask[b][None]
        scores = scores.reshape(512, 256)
        expo = jnp.exp(scores - jnp.max(scores, axis=-1, keepdims=True))
        probs = expo / jnp.sum(expo, axis=-1, keepdims=True)
        return rows, query, key, vals[g, rows, :], probs

    def attend(step, carry):
        b, g = step // 4, step % 4
        rows, query, key, value, probs = probabilities(b, g)
        result = dot(probs.astype(BF16), value).astype(BF16)
        for h in range(2):
            mixed[h, rows, lanes(g * 128, 128)] = result[h * 256 : (h + 1) * 256]
        return carry

    lax.fori_loop(0, 8, attend, 0)

    pump(1, 3)
    arrive([other_out])

    def two_parts(values, columns):
        part[0, :, columns] = values[:256]
        part[1, :, columns] = values[256:]

    def project_out(t, carry):
        values = dot(mixed[c], weight_own(OUT0 + t * 256, 256)) + dot(
            mixed[sib], weight_other(t * 256, 256)
        )
        two_parts(values, lanes(t * 256, 256))
        return carry

    lax.fori_loop(0, 4, project_out, 0)
    across = send(part.at[sib], got_part, got_part, sibling)
    across.arrived()
    middle[...] = toks[c].astype(F32) + part[c] + got_part[...]
    unit_mid, _ = unit_of(middle[...])
    hidden_mid[c] = (unit_mid * gain_mid).astype(BF16)
    across_mid = send(hidden_mid.at[c], hidden_mid.at[c], hidden_mid.at[sib], sibling)
    across.sent()
    pending.remove(across)
    pump(1, 4)
    other_down = to_other(DN0, 1536, 1024)
    arrive([across_mid])

    def all_mid():
        return hidden_mid[...].reshape(512, 1024)

    def feed_forward(t, carry):
        gate = dot(all_mid(), weight(GU0 + t * 256, 256))
        up = dot(all_mid(), weight(GU0 + 1536 + t * 256, 256))
        gate_up[:, lanes(t * 256, 256)] = gate.astype(BF16)
        gate_up[:, lanes(1536 + t * 256, 256)] = up.astype(BF16)
        result = (gate * jax.nn.sigmoid(gate) * up).astype(BF16)
        for h in range(2):
            block = 2 * t + h
            active[block % 3, :, lanes((block // 3) * 128, 128)] = result[:, h * 128 : (h + 1) * 128]
        return carry

    lax.fori_loop(0, 6, feed_forward, 0)

    plans = (
        ((grads, G_DN, 512), (grads, G_DN + 512, 512), (grads, G_DN + 1024, 512)),
        ((weights, GU0, 1024), (weights, GU0 + 1024, 1024), (weights, GU0 + 2048, 1024)),
        ((weights, QKV0, 1024), (weights, QKV0 + 1024, 1024), (grads, G_OUT, 1152)),
    )
    landing, at = {}, 0
    for unit in range(3):
        for index in range(3):
            landing[unit, index] = at
            at += plans[unit][index][2]

    def piece_column(ref, offset):
        if ref is grads:
            return offset
        return S_GU + offset - GU0 if offset >= GU0 else S_QKV + offset - QKV0

    def remaining(rotation):
        return [axis for axis in "xyz" if axis != rotation[0]]

    def add_blocks(blocks, target, size, shape):
        count = math.prod(shape)

        def body(k, carry):
            where = []
            left = k
            for extent in reversed(shape):
                where.insert(0, left % extent)
                left = left // extent
            total = blocks[0](where)
            for block in blocks[1:]:
                total = total + block(where)
            target(where, total.astype(BF16))
            return carry

        if count == 1:
            body(0, 0)
        else:
            lax.fori_loop(0, count, body, 0)

    def reader(ref, offset, size, locate):
        return lambda where: ref[locate(where) + (slice(None), lanes(offset, size))].astype(F32)

    def writer(ref, offset, size, locate):
        def store(where, value):
            ref[locate(where) + (slice(None), lanes(offset, size))] = value

        return store

    sums = {}

    def reduce_one(unit, index):
        ref, offset, size = plans[unit][index]
        rotation = ROTATIONS[index]
        first, other = rotation[0], remaining(rotation)[0]
        at = landing[unit, index]
        sums[unit, index, 1] = [
            send(
                view(ref, {first: (me[first] + 2) % 4, other: pl.ds(2 * half, 2)}, offset, size),
                got_far.at[half, :, :, :, lanes(at, size)],
                got_far.at[half, :, :, :, lanes(at, size)],
                device(moved(me, first, by)),
            )
            for by, half in ((1, 0), (3, 1))
        ]

    def reduce_two(unit, index):
        ref, offset, size = plans[unit][index]
        rotation = ROTATIONS[index]
        first, (other, last) = rotation[0], remaining(rotation)
        at = landing[unit, index]
        arrive(sums[unit, index, 1])
        out = []
        for by, half in ((1, 0), (3, 1)):
            block = (me[first] + by) % 4

            def locate(where, block=block, half=half):
                spot = {first: block, other: where[0] + 2 * half, last: where[1]}
                return tuple(spot[axis] for axis in "xyz")

            add_blocks(
                [
                    reader(ref, offset, size, locate),
                    reader(got_far, at, size, lambda where, half=half: (half, where[0], where[1])),
                ],
                writer(ref, offset, size, locate),
                size,
                (2, 4),
            )
            out.append(
                send(
                    view(ref, {first: block}, offset, size),
                    got_near.at[half, :, :, :, lanes(at, size)],
                    got_near.at[half, :, :, :, lanes(at, size)],
                    device(moved(me, first, by)),
                )
            )
        sums[unit, index, 2] = out

    def reduce_three(unit, index):
        ref, offset, size = plans[unit][index]
        rotation = ROTATIONS[index]
        first, second, third = rotation
        other, last = remaining(rotation)
        at = landing[unit, index]
        arrive(sums[unit, index, 2])

        def locate(where):
            spot = {first: me[first], other: where[0], last: where[1]}
            return tuple(spot[axis] for axis in "xyz")

        add_blocks(
            [reader(ref, offset, size, locate)]
            + [
                reader(got_near, at, size, lambda where, half=half: (half, where[0], where[1]))
                for half in range(2)
            ],
            writer(ref, offset, size, locate),
            size,
            (4, 4),
        )
        sums[unit, index, 3] = [
            send(
                view(ref, {first: me[first], second: (me[second] + by) % 4}, offset, size),
                got_two.at[by - 1, :, :, lanes(at, size)],
                got_two.at[by - 1, :, :, lanes(at, size)],
                device(moved(me, second, by)),
            )
            for by in (1, 2, 3)
        ]

    def reduce_four(unit, index):
        ref, offset, size = plans[unit][index]
        first, second, third = ROTATIONS[index]
        at = landing[unit, index]
        arrive(sums[unit, index, 3])

        def locate(where):
            spot = {first: me[first], second: me[second], third: where[0]}
            return tuple(spot[axis] for axis in "xyz")

        add_blocks(
            [reader(ref, offset, size, locate)]
            + [reader(got_two, at, size, lambda where, by=by: (by, where[0])) for by in range(3)],
            writer(ref, offset, size, locate),
            size,
            (4,),
        )
        sums[unit, index, 4] = [
            send(
                view(ref, {first: me[first], second: me[second], third: (me[third] + by) % 4}, offset, size),
                got_three.at[by - 1, :, lanes(at, size)],
                got_three.at[by - 1, :, lanes(at, size)],
                device(moved(me, third, by)),
            )
            for by in (1, 2, 3)
        ]

    y_low = y % 2
    z_first = (2, 0, 2)
    local_count = [len(inward)]
    local_pending = []

    def reduce_five(unit, index):
        ref, offset, size = plans[unit][index]
        at = landing[unit, index]
        arrive(sums[unit, index, 4])
        here = (x, y, z)
        add_blocks(
            [reader(ref, offset, size, lambda where: here)]
            + [reader(got_three, at, size, lambda where, by=by: (by,)) for by in range(3)],
            writer(ref, offset, size, lambda where: here),
            size,
            (1,),
        )
        source = ref.at[x, y, z, :, lanes(offset, size)]
        column = lanes(piece_column(ref, offset), size)
        copy = pltpu.make_async_copy(
            source, summed.at[c, y_low, z, :, column], local_sem.at[local_count[0]]
        )
        local_count[0] += 1
        copy.start()
        local_pending.append(copy)
        there = summed.at[c, y_low, z, :, column]
        beside = device({**me, "y": y + 1 - 2 * y_low})
        if index == z_first[unit]:
            sums[unit, index, 5] = [
                send(source, there, summed.at[c, y_low, (z - by + 4) % 4, :, column], device(moved(me, "z", by)))
                for by in (1, 2, 3)
            ]
        else:
            sums[unit, index, 5] = [send(source, there, summed.at[c, 1 - y_low, z, :, column], beside)]

    def reduce_six(unit, index):
        ref, offset, size = plans[unit][index]
        arrive(sums[unit, index, 5])
        column = lanes(piece_column(ref, offset), size)
        beside = device({**me, "y": y + 1 - 2 * y_low})
        if index == z_first[unit]:
            source = summed.at[c, y_low, :, :, column]
            sums[unit, index, 6] = [send(source, source, summed.at[c, 1 - y_low, :, :, column], beside)]
        else:
            source = summed.at[c, :, z, :, column]
            sums[unit, index, 6] = [
                send(source, source, summed.at[c, :, (z - by + 4) % 4, :, column], device(moved(me, "z", by)))
                for by in (1, 2, 3)
            ]

    def reduce_seven(unit, index):
        ref, offset, size = plans[unit][index]
        arrive(sums[unit, index, 6])
        column = lanes(piece_column(ref, offset), size)
        source = summed.at[c, :, :, :, column]
        sums[unit, index, 7] = [send(source, source, summed.at[sib, :, :, :, column], sibling)]

    stages = (reduce_one, reduce_two, reduce_three, reduce_four, reduce_five, reduce_six, reduce_seven)

    def reduce(unit, stage):
        if stage == 4:
            while local_pending:
                local_pending.pop().wait()
        if stage == 5:
            while local_pending:
                local_pending.pop().wait()
        for index in range(3):
            stages[stage](unit, index)

    arrive([other_down])
    flush()

    def all_cots():
        return cots[...].reshape(512, 1024)

    def cot_half(half):
        return cots[:, :, lanes(half * 512, 512, 512)].reshape(512, 512)

    def grads_own(offset, size, values):
        grads[pl.ds(2 * c, 2), :, :, :, lanes(offset, size)] = values.astype(BF16).reshape(2, 4, 4, 16, size)

    def grads_other(offset, size, values):
        weights[pl.ds(2 * sib, 2), :, :, :, lanes(offset, size)] = values.astype(BF16).reshape(2, 4, 4, 16, size)

    for t in range(2):
        values = dot_tn(active[2 * c], cots[:, :, t * 512 : (t + 1) * 512].reshape(512, 512))
        grads_own(G_DN + t * 512, 512, values)
    for t in range(2):
        values = dot_tn(active[2 * sib], cots[:, :, t * 512 : (t + 1) * 512].reshape(512, 512))
        grads_other(DN0 + t * 512, 512, values)
    grads_own(G_DN + 1024, 512, dot_tn(active[1], cot_half(c)))
    grads_other(DN0 + 1024, 512, dot_tn(active[1], cot_half(sib)))
    down_grads = send(
        view(weights, {"x": pl.ds(2 * sib, 2)}, DN0, 1536),
        view(grads, {"x": pl.ds(2 * c, 2)}, G_DN, 1536),
        view(grads, {"x": pl.ds(2 * sib, 2)}, G_DN, 1536),
        sibling,
    )

    def back_active(kind, q):
        if kind == 0:
            group = 2 * c
            values = dot_nt(all_cots(), weight_rows(2 * c + q, DN0, 1024))
        elif kind == 1:
            group = 2 * sib
            values = dot_nt(all_cots(), other_weights[q, :, :, :, 1024:2048].reshape(256, 1024))
        else:
            group = 1
            values = dot_nt(cot_half(c), weight_rows(2 * c + q, DN0 + 1024, 512)) + dot_nt(
                cot_half(sib), other_weights[q, :, :, :, 2048:2560].reshape(256, 512)
            )
        for h in range(2):
            block = 3 * (2 * q + h) + group
            pulled = values[:, h * 128 : (h + 1) * 128]
            gate = gate_up[:, lanes(block * 128, 128)].astype(F32)
            up = gate_up[:, lanes(1536 + block * 128, 128)].astype(F32)
            sigma = jax.nn.sigmoid(gate)
            back_gate = pulled * up * sigma * (1.0 + gate * (1.0 - sigma))
            gate_up[:, lanes(block * 128, 128)] = back_gate.astype(BF16)
            gate_up[:, lanes(1536 + block * 128, 128)] = (pulled * gate * sigma).astype(BF16)

    def down_back(q, carry):
        for kind in range(3):
            back_active(kind, q)
        return carry

    lax.fori_loop(0, 2, down_back, 0)
    arrive([down_grads])
    reduce(0, 0)

    def back_mid(row, carry):
        values = dot_nt(gate_up[...], weight_rows(row, GU0, 3072))
        two_parts(values, lanes(row * 256, 256))
        return carry

    lax.fori_loop(0, 4, back_mid, 0)
    across = send(part.at[sib], got_part, got_part, sibling)
    turned_lhs[...] = all_mid().T

    def gate_up_grads(t, carry):
        values = dot(turned_lhs[...], gate_up[:, lanes(t * 256, 256)])
        weights[:, :, :, :, lanes(GU0 + t * 256, 256)] = values.astype(BF16).reshape(4, 4, 4, 16, 256)
        return carry

    lax.fori_loop(0, 12, gate_up_grads, 0)
    reduce(1, 0)
    reduce(0, 1)
    arrive([across])
    back = part[c] + got_part[...]
    unit_mid, scale_mid = unit_of(middle[...])
    gains_acc[1:2, :] = jnp.sum(back * unit_mid, axis=0, keepdims=True)
    back_middle = cots[c].astype(F32) + norm_back(back, gain_mid, unit_mid, scale_mid)
    branch[c] = back_middle.astype(BF16)
    across.sent()
    pending.remove(across)
    across_branch = send(branch.at[c], branch.at[c], branch.at[sib], sibling)

    down_rows = lambda t: (
        dot(active[2 * c], weight_own(DN0 + t * 256, 256))
        + dot(active[2 * sib], weight_other(1024 + t * 256, 256))
    )
    for t in range(4):
        values = down_rows(t)
        two_parts(values, pl.ds(t * 256, 256))
    for half, load in ((c, lambda: weight_own(DN0 + 1024, 512)), (sib, lambda: weight_other(2048, 512))):
        values = dot(active[1], load())
        columns = lanes(half * 512, 512, 512)
        part[0, :, columns] += values[:256]
        part[1, :, columns] += values[256:]
    across_down = send(part.at[sib], got_down, got_down, sibling)
    across_down.arrived()
    out_low[...] = (middle[...] + part[c] + got_down[...]).astype(BF16)
    across_down.sent()
    pending.remove(across_down)
    copy_out = pltpu.make_async_copy(out_low, activations, local_sem.at[0])
    copy_out.start()
    middle[...] = back_middle
    arrive([across_branch])
    reduce(1, 1)
    reduce(0, 2)

    def all_branch():
        return branch[...].reshape(512, 1024)

    for t in range(2):
        columns = slice(t * 512, (t + 1) * 512)
        grads_own(G_OUT + t * 512, 512, dot_tn(mixed[c], branch[:, :, columns].reshape(512, 512)))
    for t in range(2):
        columns = slice(t * 512, (t + 1) * 512)
        grads_other(OUT0 + t * 512, 512, dot_tn(mixed[sib], branch[:, :, columns].reshape(512, 512)))
    out_grads = send(
        view(weights, {"x": pl.ds(2 * sib, 2)}, OUT0, 1024),
        view(grads, {"x": pl.ds(2 * c, 2)}, G_OUT, 1024),
        view(grads, {"x": pl.ds(2 * sib, 2)}, G_OUT, 1024),
        sibling,
    )
    mixed[c] = dot_nt(all_branch(), weight_own(OUT0, 1024)).astype(BF16)
    mixed[sib] = dot_nt(all_branch(), weight_other(0, 1024)).astype(BF16)
    gains_acc[2:3, :] = jnp.zeros((1, 1024), F32)

    def attend_back(step, carry):
        b, g = step // 4, step % 4
        rows, query, key, value, probs = probabilities(b, g)
        pulled = jnp.concatenate([mixed[h, rows, lanes(g * 128, 128)] for h in range(2)], axis=0)
        back_probs = dot_nt(pulled, value)
        inner = jnp.sum(probs * back_probs, axis=-1, keepdims=True)
        back_scores = (probs * (back_probs - inner) * SCALE).astype(BF16)
        back_query = dot(back_scores, key)
        back_key = dot_tn(back_scores, query)
        back_value = dot_tn(probs.astype(BF16), pulled)
        cosine = rope[b, :, 0:128]
        sine = rope[b, :, 128:256]

        def through(upstream, column, gain):
            unit, scale = unit_of(raw[rows, lanes(column, 128)].astype(F32))
            plain = upstream * cosine - pltpu.roll(upstream, 64, 1) * sine
            gate_up[rows, lanes(column, 128)] = norm_back(plain, gain, unit, scale).astype(BF16)
            return jnp.sum(plain * unit, axis=0, keepdims=True)

        for h in range(2):
            gains_acc[2:3, 0:128] += through(
                back_query[h * 256 : (h + 1) * 256], (2 * g + h) * 128, gain_query
            )
        gains_acc[2:3, 128:256] += through(back_key, 1024 + g * 128, gain_key)
        gate_up[rows, lanes(1536 + g * 128, 128)] = back_value.astype(BF16)
        return carry

    lax.fori_loop(0, 8, attend_back, 0)
    reduce(1, 2)
    reduce(0, 3)

    def back_in(row, carry):
        values = dot_nt(gate_up[:, 0:2048], weight_rows(row, QKV0, 2048))
        two_parts(values, lanes(row * 256, 256))
        return carry

    lax.fori_loop(0, 4, back_in, 0)
    across = send(part.at[sib], got_part, got_part, sibling)
    turned_lhs[...] = all_hidden().T

    def qkv_grads(t, carry):
        values = dot(turned_lhs[...], gate_up[:, lanes(t * 256, 256)])
        weights[:, :, :, :, lanes(QKV0 + t * 256, 256)] = values.astype(BF16).reshape(4, 4, 4, 16, 256)
        return carry

    lax.fori_loop(0, 8, qkv_grads, 0)
    arrive([across])
    back = part[c] + got_part[...]
    unit_in, scale_in = unit_of(toks[c].astype(F32))
    gains_acc[0:1, :] = jnp.sum(back * unit_in, axis=0, keepdims=True)
    pltpu.make_async_copy(out_low, activations, local_sem.at[0]).wait()
    out_low[...] = (middle[...] + norm_back(back, gain_in, unit_in, scale_in)).astype(BF16)
    copy_out = pltpu.make_async_copy(out_low, input_grad, local_sem.at[1])
    copy_out.start()

    low = jnp.concatenate(
        [gains_acc[r : r + 1, i * 128 : (i + 1) * 128] for r in range(2) for i in range(8)], axis=0
    ).astype(BF16)
    high = jnp.concatenate(
        [gains_acc[2:3, 0:128], gains_acc[2:3, 128:256], jnp.zeros((14, 128), F32)], axis=0
    ).astype(BF16)
    grads[:, :, :, :, G_GAIN : G_GAIN + 128] = jnp.zeros((4, 4, 4, 16, 128), BF16)
    for part_x in range(4):
        for part_y in (0, 2):
            grads[part_x, part_y, 0, :, G_GAIN : G_GAIN + 128] = low
            grads[part_x, part_y, 1, :, G_GAIN : G_GAIN + 128] = high
    arrive([out_grads])
    reduce(2, 0)
    reduce(0, 4)
    reduce(1, 3)
    reduce(0, 5)
    reduce(2, 1)
    reduce(1, 4)
    reduce(0, 6)
    reduce(2, 2)
    reduce(1, 5)
    reduce(2, 3)
    reduce(1, 6)
    reduce(2, 4)
    reduce(2, 5)
    reduce(2, 6)
    for unit in range(3):
        for index in range(3):
            arrive(sums[unit, index, 7])
    copy_out.wait()
    flush()


TRANSFERS = 256


def run_layer(tokens, cotangent, tables, bias, piece):
    anywhere = pl.BlockSpec(memory_space=pl.ANY)
    vmem = pltpu.VMEM
    return pl.pallas_call(
        layer_kernel,
        out_shape=(
            jax.ShapeDtypeStruct((TOK, D), BF16),
            jax.ShapeDtypeStruct((TOK, D), BF16),
            jax.ShapeDtypeStruct((2, 2, 4, 16, WCOLS), BF16),
        ),
        in_specs=[anywhere] * 5,
        out_specs=(anywhere,) * 3,
        scratch_shapes=[
            vmem((4, 4, 4, 16, WCOLS), BF16),
            vmem((4, 4, 4, 16, G_COLS), BF16),
            vmem((2, 4, 4, 16, 2560), BF16),
            vmem((2, 2, 4, 16, WCOLS), BF16),
            vmem((2, 4, 4, 16, WCOLS), BF16),
            vmem((3, 4, 16, WCOLS), BF16),
            vmem((3, 16, WCOLS), BF16),
            vmem((2, TOK, D), BF16),
            vmem((2, TOK, D), BF16),
            vmem((2, TOK, 256), F32),
            vmem((2, TOK, TOK), F32),
            vmem((2, TOK, D), BF16),
            vmem((2 * TOK, 1536), BF16),
            vmem((12, 2 * TOK, HD), BF16),
            vmem((4, 2 * TOK, HD), BF16),
            vmem((2, 2 * TOK, 512), BF16),
            vmem((2, TOK, D), F32),
            vmem((TOK, D), F32),
            vmem((TOK, D), F32),
            vmem((TOK, D), F32),
            vmem((2, TOK, D), BF16),
            vmem((2 * TOK, 3072), BF16),
            vmem((3, 2 * TOK, 512), BF16),
            vmem((2, TOK, D), BF16),
            vmem((D, 2 * TOK), BF16),
            vmem((TOK, D), BF16),
            vmem((8, D), F32),
            pltpu.SemaphoreType.DMA((24,)),
            pltpu.SemaphoreType.DMA((TRANSFERS,)),
            pltpu.SemaphoreType.DMA((TRANSFERS,)),
        ],
        compiler_params=pltpu.CompilerParams(
            collective_id=0, has_side_effects=True, vmem_limit_bytes=64 * 2**20
        ),
        cost_estimate=pl.CostEstimate(flops=26 * 10**9, bytes_accessed=10**7, transcendentals=10**6),
    )(tokens, cotangent, tables, bias, piece)


def adamw(master, first, second, gradient, rate, decay):
    first_new = 0.9 * first + 0.1 * gradient
    second_new = 0.999 * second + 0.001 * gradient * gradient
    direction = first_new / (1.0 - 0.9**STEP) / (jnp.sqrt(second_new / (1.0 - 0.999**STEP)) + 1e-08)
    return (master - rate * (direction + decay * master), first_new, second_new)


def per_device(
    tokens,
    cotangent,
    segment_ids,
    positions,
    master_qkv,
    master_out,
    master_gate_up,
    master_down,
    master_gains,
    first_qkv,
    first_out,
    first_gate_up,
    first_down,
    first_gains,
    second_qkv,
    second_out,
    second_gate_up,
    second_down,
    second_gains,
):
    me = coordinates()
    c = me["c"]
    shard = lax.axis_index("shard")
    order = (me["y"] % 2) * 4 + me["z"]
    row = 16 * order

    def half(array, offset, size):
        return lax.dynamic_slice(array, (row, offset + c * size), (16, size))

    down = lax.dynamic_slice(master_down.reshape(3, 128, D), (0, row, 0), (3, 16, D))
    whole = jnp.where(c == 0, down[0], down[2])
    shared = jnp.where(c == 0, down[1][:, :512], down[1][:, 512:])
    out = lax.dynamic_slice(master_out.reshape(2, 128, D), (c, row, 0), (1, 16, D))[0]
    spread = lax.dynamic_update_slice(jnp.zeros((32 * 128,), F32), master_gains, (288 * shard,))
    spread = jnp.concatenate([spread.reshape(2, 16, 128), jnp.zeros((6, 16, 128), F32)], axis=0)
    gains = lax.dynamic_slice(spread, (order, 0, 0), (1, 16, 128))[0]
    piece = jnp.concatenate(
        [
            half(master_qkv, 0, 1024),
            half(master_qkv, 2048, 512),
            half(master_qkv, 3072, 512),
            out,
            gains,
            half(master_gate_up, 0, 1536),
            half(master_gate_up, 3072, 1536),
            whole,
            shared,
        ],
        axis=1,
    ).astype(BF16)

    freq = jnp.exp(jnp.arange(HD // 2).astype(F32) * (-2.0 * math.log(1000000.0) / HD))
    angle = positions[0].astype(F32)[:, None] * freq
    cosine = jnp.cos(angle)
    sine = jnp.sin(angle)
    tables = jnp.concatenate([cosine, cosine, -sine, sine], axis=-1)
    segments = segment_ids[0]
    places = jnp.arange(TOK)
    allowed = (places[None, :] <= places[:, None]) & (segments[:, None] == segments[None, :])
    bias = jnp.where(allowed, 0.0, -1e30).astype(F32)

    activations, input_grad, summed = run_layer(tokens, cotangent, tables, bias, piece)
    summed = summed.reshape(2, 128, WCOLS)

    gradient = summed.astype(F32)
    g0, g1 = gradient[0], gradient[1]
    grad_qkv = jnp.concatenate(
        [
            g0[:, S_QKV : S_QKV + 1024],
            g1[:, S_QKV : S_QKV + 1024],
            g0[:, S_QKV + 1024 : S_QKV + 1536],
            g1[:, S_QKV + 1024 : S_QKV + 1536],
            g0[:, S_QKV + 1536 : S_QKV + 2048],
            g1[:, S_QKV + 1536 : S_QKV + 2048],
        ],
        axis=1,
    )
    grad_out = jnp.concatenate([g0[:, :1024], g1[:, :1024]], axis=0)
    grad_gate_up = jnp.concatenate(
        [
            g0[:, S_GU : S_GU + 1536],
            g1[:, S_GU : S_GU + 1536],
            g0[:, S_GU + 1536 :],
            g1[:, S_GU + 1536 :],
        ],
        axis=1,
    )
    grad_down = jnp.concatenate(
        [
            g0[:, G_DN : G_DN + 1024],
            jnp.concatenate([g0[:, G_DN + 1024 : G_DN + 1536], g1[:, G_DN + 1024 : G_DN + 1536]], axis=1),
            g1[:, G_DN : G_DN + 1024],
        ],
        axis=0,
    )
    gain_rows = (g0[:32, G_GAIN : G_GAIN + 128] + g1[:32, G_GAIN : G_GAIN + 128]).reshape(-1)
    grad_gains = lax.dynamic_slice(gain_rows, (288 * shard,), (288,))
    updated = [
        adamw(master_qkv, first_qkv, second_qkv, grad_qkv, 0.05, 0.1),
        adamw(master_out, first_out, second_out, grad_out, 0.05, 0.1),
        adamw(master_gate_up, first_gate_up, second_gate_up, grad_gate_up, 0.05, 0.1),
        adamw(master_down, first_down, second_down, grad_down, 0.05, 0.1),
        adamw(master_gains, first_gains, second_gains, grad_gains, 0.4, 0.0),
    ]
    return (
        activations,
        input_grad,
        *(new[0] for new in updated),
        *(new[1] for new in updated),
        *(new[2] for new in updated),
    )


def solution(mesh):
    rows = P(("rep", "shard"), None)
    state = (P("shard", None),) * 4 + (P("shard"),)
    return jax.shard_map(
        per_device,
        mesh=mesh,
        in_specs=(rows,) * 4 + state * 3,
        out_specs=(rows,) * 2 + state * 3,
        check_vma=False,
    )
```

```python
import math

import jax
import jax.numpy as jnp
from jax import lax
from jax.experimental import pallas as pl
from jax.experimental.pallas import tpu as pltpu
from jax.sharding import PartitionSpec as P

D = 1024
HEADS = 16
KV_HEADS = 8
HD = 128
FF = 3072
STEP = 10
Q_WIDTH = 2048
KV_WIDTH = 1024
TOK = 256
F32 = jnp.float32
BF16 = jnp.bfloat16
EPS = 1e-06
SCALE = HD ** (-0.5)

QKV0, GAIN0, OUT0, GU0, DN0, WCOLS = 0, 2048, 2176, 3200, 6272, 7808
G_OUT, G_DN, G_COLS = 0, 1024, 2560
S_GU, S_QKV, S_GAIN, S_DN, S_OUT, S_COLS = 0, 3072, 5120, 5632, 7168, 8192
LOG2E = 1.4426950408889634
ROTATIONS = (("x", "y", "z"), ("y", "z", "x"), ("z", "x", "y"))

SCHEDULE = {
    "start": ("W0", "W1", "W2"),
    "early": ("W0", "W0", "W1", "W0", "W1", "W2"),
    "attend": ("W1",),
    "mid": ("W2",),
    "feed1": ("W2",),
    "active0": ("G0",),
    "mid1": ("G0",),
    "gu1": ("G1",),
    "output": ("G0",),
    "mixed": ("G2",),
    "attend0": ("G1", "G3", "G0"),
    "query": ("G2",),
    "key": ("G1",),
    "in": ("G3", "G4", "G0"),
    "end": tuple("G" + unit for unit in "25136402561342536142536456"),
}


def dot(left, right):
    return jnp.dot(left, right, preferred_element_type=F32)


def dot_nt(left, right):
    return lax.dot_general(left, right, (((1,), (1,)), ((), ())), preferred_element_type=F32)


def dot_tn(left, right):
    return lax.dot_general(left, right, (((0,), (0,)), ((), ())), preferred_element_type=F32)


def lanes(start, size, step=128):
    return pl.ds(start if isinstance(start, int) else pl.multiple_of(start, step), size)


def coordinates():
    rep = lax.axis_index("rep")
    shard = lax.axis_index("shard")
    return {
        "x": shard // 2,
        "y": (shard % 2) * 2 + (rep // 2) % 2,
        "z": rep // 4,
        "c": rep % 2,
    }


def device(at):
    return {"rep": at["z"] * 4 + (at["y"] % 2) * 2 + at["c"], "shard": at["x"] * 2 + at["y"] // 2}


def moved(me, axis, by):
    return {**me, axis: (me[axis] + by + 4) % 4}


def view(ref, select, offset, size):
    where = tuple(select.get(axis, slice(None)) for axis in "xyz")
    return ref.at[where + (slice(None), lanes(offset, size))]


def layer_kernel(
    tokens,
    cotangent,
    tables,
    segments,
    gains,
    master_qkv,
    master_out,
    master_gate_up,
    master_down,
    activations,
    input_grad,
    summed,
    weights,
    grads,
    other_weights,
    got_far,
    got_near,
    got_two,
    got_three,
    toks,
    cots,
    rope,
    mask,
    mask_turned,
    hidden,
    raw,
    rotated,
    vals,
    mixed,
    part,
    got_part,
    got_down,
    middle,
    hidden_mid,
    gate_up,
    active,
    branch,
    turned_lhs,
    spare,
    gains_acc,
    local_sem,
    send_sem,
    recv_sem,
):
    me = coordinates()
    c = me["c"]
    sib = 1 - c
    x, y, z = me["x"], me["y"], me["z"]
    sibling = device({**me, "c": sib})
    used = [0]

    class Transfer:
        def __init__(self, source, there, here, target):
            self.index = used[0]
            used[0] += 1
            self.source, self.there, self.here, self.target = source, there, here, target
            self.copy(source, there).start()

        def copy(self, source, there):
            return pltpu.make_async_remote_copy(
                src_ref=source,
                dst_ref=there,
                send_sem=send_sem.at[self.index],
                recv_sem=recv_sem.at[self.index],
                device_id=self.target,
                device_id_type=pl.DeviceIdType.MESH,
            )

        def arrived(self):
            self.copy(self.here, self.here).wait_recv()

        def sent(self):
            self.copy(self.source, self.there).wait_send()

    pending = []

    def send(source, there, here, target):
        transfer = Transfer(source, there, here, target)
        pending.append(transfer)
        return transfer

    def flush():
        while pending:
            pending.pop(0).sent()

    def arrive(transfers):
        for transfer in transfers:
            transfer.arrived()

    row = 16 * ((y % 2) * 4 + z)

    def rows_of(ref, first, offset, size):
        return ref.at[pl.ds(pl.multiple_of(first, 16), 16), lanes(offset, size)]

    groups = [
        (rows_of(master_qkv, row, c * 1024, 1024), QKV0, 1024),
        (rows_of(master_qkv, row, 2048 + c * 512, 512), QKV0 + 1024, 512),
        (rows_of(master_qkv, row, 3072 + c * 512, 512), QKV0 + 1536, 512),
        (rows_of(master_out, c * 128 + row, 0, 1024), OUT0, 1024),
        (rows_of(master_gate_up, row, c * 1536, 768), GU0, 768),
        (rows_of(master_gate_up, row, 3072 + c * 1536, 768), GU0 + 768, 768),
        (rows_of(master_gate_up, row, c * 1536 + 768, 768), GU0 + 1536, 768),
        (rows_of(master_gate_up, row, 3072 + c * 1536 + 768, 768), GU0 + 2304, 768),
        (rows_of(master_down, c * 256 + row, 0, 1024), DN0, 1024),
        (rows_of(master_down, 128 + row, c * 512, 512), DN0 + 1024, 512),
    ]
    inward = [
        (source, got_part.at[pl.ds(16 * index, 16), pl.ds(0, size)])
        for index, (source, offset, size) in enumerate(groups)
    ]
    inward += [(gains, got_part.at[pl.ds(160, 16), pl.ds(0, 128)])]
    first_inward = len(inward)
    inward += [
        (tables, got_down.at[:, pl.ds(0, 128)]),
        (segments, got_down.at[pl.ds(0, 8), pl.ds(128, 256)]),
        (tokens, toks.at[c]),
        (cotangent, cots.at[c]),
    ]
    inward = [pltpu.make_async_copy(*pair, local_sem.at[index]) for index, pair in enumerate(inward)]

    barrier = pltpu.get_barrier_semaphore()
    across_y = {**me, "y": y + 1 - 2 * (y % 2)}
    friends = [sibling] + [device(moved(me, axis, by)) for axis in "xyz" for by in (1, 2, 3)]
    friends += [device(moved(across_y, "z", by)) for by in (1, 2, 3)]
    for friend in friends:
        pl.semaphore_signal(barrier, inc=1, device_id=friend, device_id_type=pl.DeviceIdType.MESH)
    for copy in inward:
        copy.start()
    for copy in inward[:first_inward]:
        copy.wait()
    for index, (source, offset, size) in enumerate(groups):
        rows16 = got_part[16 * index : 16 * index + 16, 0:size]
        weights[x, y, z, :, offset : offset + size] = rows16.astype(BF16)
    weights[x, y, z, :, GAIN0 : GAIN0 + 128] = got_part[160:176, 0:128].astype(BF16)
    pl.semaphore_wait(barrier, len(friends))

    def gather_one(rotation, offset, size):
        first, second, third = rotation
        source = view(weights, {"x": x, "y": y, "z": z}, offset, size)
        out = []
        for by in (1, 2, 3):
            here = view(weights, {**{"x": x, "y": y, "z": z}, third: (me[third] - by + 4) % 4}, offset, size)
            out.append(send(source, source, here, device(moved(me, third, by))))
        return out

    def gather_two(rotation, offset, size):
        first, second, third = rotation
        source = view(weights, {first: me[first], second: me[second]}, offset, size)
        out = []
        for by in (1, 2, 3):
            here = view(weights, {first: me[first], second: (me[second] - by + 4) % 4}, offset, size)
            out.append(send(source, source, here, device(moved(me, second, by))))
        return out

    def gather_three(rotation, offset, size):
        first = rotation[0]
        source = view(weights, {first: me[first]}, offset, size)
        out = []
        for by in (1, 3):
            here = view(weights, {first: (me[first] - by + 4) % 4}, offset, size)
            out.append(send(source, source, here, device(moved(me, first, by))))
        return out

    def gather_four(rotation, offset, size):
        first, second = rotation[0], rotation[1]
        out = []
        for by, half in ((1, 0), (3, 1)):
            rows = pl.ds(2 * half, 2)
            source = view(weights, {first: (me[first] - by + 4) % 4, second: rows}, offset, size)
            here = view(weights, {first: (me[first] + 2) % 4, second: rows}, offset, size)
            out.append(send(source, source, here, device(moved(me, first, by))))
        return out

    chunks = (
        ((0, 1152), (1152, 1024), (OUT0, 1024)),
        ((GU0, 1024), (GU0 + 1024, 1024), (GU0 + 2048, 1024)),
        ((DN0, 512), (DN0 + 512, 512), (DN0 + 1024, 512)),
    )
    steps = (gather_one, gather_two, gather_three, gather_four)
    flying = [[None] * 3 for _ in chunks]

    w_step = [0] * len(chunks)
    g_stage = [0] * 7

    def pump(chunk):
        step = w_step[chunk]
        w_step[chunk] += 1
        for index, rotation in enumerate(ROTATIONS):
            if step:
                arrive(flying[chunk][index])
            if step < 4:
                flying[chunk][index] = steps[step](rotation, *chunks[chunk][index])

    def gathered(chunk):
        while w_step[chunk] < 5:
            pump(chunk)

    def exchange(name):
        for item in SCHEDULE.get(name, ()):
            (pump if item[0] == "W" else reduce)(int(item[1]))

    exchange("start")
    for copy in inward[first_inward:]:
        copy.wait()
    wave = got_down[:, 0:128]
    rope[c, :, 0:128] = jnp.concatenate([wave[:, :64], wave[:, :64]], axis=1)
    rope[c, :, 128:256] = jnp.concatenate([-wave[:, 64:], wave[:, 64:]], axis=1)
    across_segments = jnp.broadcast_to(got_down[0:1, 128:384], (256, 256))
    same = across_segments == across_segments.T
    earlier = lax.broadcasted_iota(jnp.int32, (256, 256), 1) <= lax.broadcasted_iota(
        jnp.int32, (256, 256), 0
    )
    mask[c] = jnp.where(same & earlier, 0.0, -1e30).astype(BF16)
    early = [
        send(toks.at[c], toks.at[c], toks.at[sib], sibling),
        send(rope.at[c], rope.at[c], rope.at[sib], sibling),
        send(mask.at[c], mask.at[c], mask.at[sib], sibling),
        send(cots.at[c], cots.at[c], cots.at[sib], sibling),
    ]
    exchange("early")
    arrive(early)
    for b in range(2):
        mask_turned[b] = mask[b].astype(F32).T.astype(BF16)
    exchange("late")
    gathered(0)

    def to_other(offset, size, at):
        return send(
            view(weights, {"x": pl.ds(2 * sib, 2)}, offset, size),
            view(other_weights, {}, at, size),
            view(other_weights, {}, at, size),
            sibling,
        )

    other_out = to_other(OUT0, 1024, 0)

    def weight(offset, size):
        return weights[:, :, :, :, lanes(offset, size)].reshape(1024, size)

    def weight_rows(row, offset, size):
        return weights[row, :, :, :, lanes(offset, size)].reshape(256, size)

    def weight_own(offset, size):
        return weights[pl.ds(2 * c, 2), :, :, :, lanes(offset, size)].reshape(512, size)

    def weight_other(offset, size):
        return other_weights[:, :, :, :, lanes(offset, size)].reshape(512, size)

    gain_rows = jnp.zeros((16, 128), F32)
    head_rows = jnp.zeros((16, 128), F32)
    for part_x in range(4):
        for part_y in (0, 2):
            gain_rows += weights[part_x, part_y, 0, :, pl.ds(GAIN0, 128)].astype(F32)
            head_rows += weights[part_x, part_y, 1, :, pl.ds(GAIN0, 128)].astype(F32)
    gain_in = jnp.concatenate([gain_rows[i : i + 1] for i in range(8)], axis=1)
    gain_mid = jnp.concatenate([gain_rows[i : i + 1] for i in range(8, 16)], axis=1)
    gain_query = head_rows[0:1]
    gain_key = head_rows[1:2]

    def unit_of(values):
        scale = lax.rsqrt(jnp.mean(values * values, axis=-1, keepdims=True) + EPS)
        return values * scale, scale

    def norm_back(upstream, gain, unit, scale):
        pushed = upstream * gain
        inner = jnp.mean(pushed * unit, axis=-1, keepdims=True)
        return scale * (pushed - unit * inner)

    for b in range(2):
        unit, _ = unit_of(toks[b].astype(F32))
        hidden[b] = (unit * gain_in).astype(BF16)

    def all_hidden():
        return hidden[...].reshape(512, 1024)

    mean_of = jnp.full((128, 128), 1.0 / 128, BF16)

    def head_mean(values):
        return dot(values.astype(BF16), mean_of)

    def project_heads(t, carry):
        values = dot(all_hidden(), weight(QKV0 + t * 256, 256))
        raw[:, lanes(t * 256, 256)] = values.astype(BF16)
        gain = jnp.where(t < 4, gain_query, gain_key)
        cosine = rope[:, :, 0:128].reshape(512, 128)
        sine = rope[:, :, 128:256].reshape(512, 128)
        for h in range(2):
            head = values[:, h * 128 : (h + 1) * 128]
            normal = head * lax.rsqrt(head_mean(head * head) + EPS) * gain
            rotated[2 * t + h] = (normal * cosine + pltpu.roll(normal, 64, 1) * sine).astype(BF16)
        return carry

    lax.fori_loop(0, 6, project_heads, 0)

    def project_values(t, carry):
        values = dot(all_hidden(), weight(QKV0 + 1536 + t * 256, 256)).astype(BF16)
        vals[2 * t] = values[:, :128]
        vals[2 * t + 1] = values[:, 128:]
        return carry

    lax.fori_loop(0, 2, project_values, 0)
    exchange("project")

    def heads_of(b, g):
        rows = pl.ds(pl.multiple_of(b * 256, 256), 256)
        query = rotated[pl.ds(2 * g, 2), rows, :].reshape(512, 128)
        return rows, query, rotated[8 + g, rows, :], vals[g, rows, :]

    def attend(step, carry):
        b, g = step // 4, step % 4
        rows, query, key, value = heads_of(b, g)
        scores = dot_nt(query, key).reshape(2, 256, 256) * (SCALE * LOG2E) + mask[b].astype(F32)[None]
        expo = jnp.exp2(scores).reshape(512, 256).astype(BF16)
        result = dot(expo, jnp.concatenate([value, jnp.ones((256, 128), BF16)], axis=1))
        result = (result[:, :128] / result[:, 128:]).astype(BF16)
        for h in range(2):
            mixed[h, rows, lanes(g * 128, 128)] = result[h * 256 : (h + 1) * 256]
        return carry

    lax.fori_loop(0, 8, attend, 0)

    exchange("attend")
    arrive([other_out])

    def two_parts(values, columns):
        part[0, :, columns] = values[:256]
        part[1, :, columns] = values[256:]

    def project_out(t, carry):
        values = dot(mixed[c], weight_own(OUT0 + t * 256, 256)) + dot(
            mixed[sib], weight_other(t * 256, 256)
        )
        two_parts(values, lanes(t * 256, 256))
        return carry

    lax.fori_loop(0, 4, project_out, 0)
    exchange("projected")
    across = send(part.at[sib], got_part, got_part, sibling)
    across.arrived()
    middle[...] = toks[c].astype(F32) + part[c] + got_part[...]
    unit_mid, _ = unit_of(middle[...])
    hidden_mid[c] = (unit_mid * gain_mid).astype(BF16)
    across_mid = send(hidden_mid.at[c], hidden_mid.at[c], hidden_mid.at[sib], sibling)
    across.sent()
    pending.remove(across)
    exchange("mid")
    gathered(1)
    arrive([across_mid])

    def all_mid():
        return hidden_mid[...].reshape(512, 1024)

    def feed_forward(t, carry):
        column = (t // 3) * 1536 + (t % 3) * 256
        gate = dot(all_mid(), weight(GU0 + column, 256))
        up = dot(all_mid(), weight(GU0 + column + 768, 256))
        gate_up[:, lanes(column, 256)] = gate.astype(BF16)
        gate_up[:, lanes(column + 768, 256)] = up.astype(BF16)
        result = (gate * jax.nn.sigmoid(gate) * up).astype(BF16)
        for h in range(2):
            block = 2 * t + h
            active[block % 3, :, lanes((block // 3) * 128, 128)] = result[:, h * 128 : (h + 1) * 128]
        return carry

    lax.fori_loop(0, 3, feed_forward, 0)
    exchange("feed0")
    lax.fori_loop(3, 6, feed_forward, 0)
    exchange("feed1")

    def unit_of_parts(ref, offset, sizes, column):
        parts = []
        for size in sizes:
            parts.append((ref, offset, size, column))
            offset, column = offset + size, column + size
        return parts

    plans = (
        unit_of_parts(grads, G_DN, (512, 512, 512), S_DN),
        unit_of_parts(weights, GU0, (512, 512, 512), S_GU),
        unit_of_parts(weights, GU0 + 1536, (512, 512, 512), S_GU + 1536),
        unit_of_parts(grads, G_OUT, (384, 384, 256), S_OUT),
        unit_of_parts(weights, OUT0, (384, 384, 256), S_QKV),
        unit_of_parts(weights, DN0, (384, 384, 256), S_QKV + 1024),
        unit_of_parts(weights, DN0 + 1024, (128,), S_GAIN),
    )
    UNITS = len(plans)
    landing, at = {}, 0
    for unit in range(UNITS):
        for index in range(len(plans[unit])):
            landing[unit, index] = at
            at += plans[unit][index][2]

    def remaining(rotation):
        return [axis for axis in "xyz" if axis != rotation[0]]

    def add_blocks(blocks, target, size, shape):
        count = math.prod(shape)

        def body(k, carry):
            where = []
            left = k
            for extent in reversed(shape):
                where.insert(0, left % extent)
                left = left // extent
            total = blocks[0](where)
            for block in blocks[1:]:
                total = total + block(where)
            target(where, total.astype(BF16))
            return carry

        if count == 1:
            body(0, 0)
        else:
            lax.fori_loop(0, count, body, 0)

    def reader(ref, offset, size, locate):
        return lambda where: ref[locate(where) + (slice(None), lanes(offset, size))].astype(F32)

    def writer(ref, offset, size, locate):
        def store(where, value):
            ref[locate(where) + (slice(None), lanes(offset, size))] = value

        return store

    sums = {}

    def reduce_one(unit, index):
        ref, offset, size, to = plans[unit][index]
        rotation = ROTATIONS[index]
        first, other = rotation[0], remaining(rotation)[0]
        at = landing[unit, index]
        sums[unit, index, 1] = [
            send(
                view(ref, {first: (me[first] + 2) % 4, other: pl.ds(2 * half, 2)}, offset, size),
                got_far.at[half, :, :, :, lanes(at, size)],
                got_far.at[half, :, :, :, lanes(at, size)],
                device(moved(me, first, by)),
            )
            for by, half in ((1, 0), (3, 1))
        ]

    def reduce_two(unit, index):
        ref, offset, size, to = plans[unit][index]
        rotation = ROTATIONS[index]
        first, (other, last) = rotation[0], remaining(rotation)
        at = landing[unit, index]
        arrive(sums[unit, index, 1])
        out = []
        for by, half in ((1, 0), (3, 1)):
            block = (me[first] + by) % 4

            def locate(where, block=block, half=half):
                spot = {first: block, other: where[0] + 2 * half, last: where[1]}
                return tuple(spot[axis] for axis in "xyz")

            add_blocks(
                [
                    reader(ref, offset, size, locate),
                    reader(got_far, at, size, lambda where, half=half: (half, where[0], where[1])),
                ],
                writer(ref, offset, size, locate),
                size,
                (2, 4),
            )
            out.append(
                send(
                    view(ref, {first: block}, offset, size),
                    got_near.at[half, :, :, :, lanes(at, size)],
                    got_near.at[half, :, :, :, lanes(at, size)],
                    device(moved(me, first, by)),
                )
            )
        sums[unit, index, 2] = out

    def reduce_three(unit, index):
        ref, offset, size, to = plans[unit][index]
        rotation = ROTATIONS[index]
        first, second, third = rotation
        other, last = remaining(rotation)
        at = landing[unit, index]
        arrive(sums[unit, index, 2])

        def locate(where):
            spot = {first: me[first], other: where[0], last: where[1]}
            return tuple(spot[axis] for axis in "xyz")

        add_blocks(
            [reader(ref, offset, size, locate)]
            + [
                reader(got_near, at, size, lambda where, half=half: (half, where[0], where[1]))
                for half in range(2)
            ],
            writer(ref, offset, size, locate),
            size,
            (4, 4),
        )
        sums[unit, index, 3] = [
            send(
                view(ref, {first: me[first], second: (me[second] + by) % 4}, offset, size),
                got_two.at[by - 1, :, :, lanes(at, size)],
                got_two.at[by - 1, :, :, lanes(at, size)],
                device(moved(me, second, by)),
            )
            for by in (1, 2, 3)
        ]

    def reduce_four(unit, index):
        ref, offset, size, to = plans[unit][index]
        first, second, third = ROTATIONS[index]
        at = landing[unit, index]
        arrive(sums[unit, index, 3])

        def locate(where):
            spot = {first: me[first], second: me[second], third: where[0]}
            return tuple(spot[axis] for axis in "xyz")

        add_blocks(
            [reader(ref, offset, size, locate)]
            + [reader(got_two, at, size, lambda where, by=by: (by, where[0])) for by in range(3)],
            writer(ref, offset, size, locate),
            size,
            (4,),
        )
        sums[unit, index, 4] = [
            send(
                view(ref, {first: me[first], second: me[second], third: (me[third] + by) % 4}, offset, size),
                got_three.at[by - 1, :, lanes(at, size)],
                got_three.at[by - 1, :, lanes(at, size)],
                device(moved(me, third, by)),
            )
            for by in (1, 2, 3)
        ]

    y_low = y % 2
    ways = ("yz", "yz", "zy", "yz", "all", "all", "all")
    local_count = [len(inward)]
    local_pending = {}

    def whole(unit):
        ref, offset, _, to = plans[unit][0]
        size = sum(part[2] for part in plans[unit])
        return ref.at[x, y, z, :, lanes(offset, size)], lanes(to, size)

    def along_z(unit, number, source, there, here):
        sums[unit, number] = [
            send(source, there, here((z - by + 4) % 4), device(moved(me, "z", by))) for by in (1, 2, 3)
        ]

    def reduce_five(unit):
        for index in range(len(plans[unit])):
            ref, offset, size, to = plans[unit][index]
            at = landing[unit, index]
            arrive(sums[unit, index, 4])
            here = (x, y, z)
            add_blocks(
                [reader(ref, offset, size, lambda where: here)]
                + [reader(got_three, at, size, lambda where, by=by: (by,)) for by in range(3)],
                writer(ref, offset, size, lambda where: here),
                size,
                (1,),
            )
        source, column = whole(unit)
        there = summed.at[c, y_low, z, :, column]
        local_pending[unit] = pltpu.make_async_copy(source, there, local_sem.at[local_count[0]])
        local_count[0] += 1
        local_pending[unit].start()
        if ways[unit] != "yz":
            along_z(unit, 5, source, there, lambda at_z: summed.at[c, y_low, at_z, :, column])
        if ways[unit] == "yz":
            sums[unit, 5] = [send(source, there, summed.at[c, 1 - y_low, z, :, column], device(across_y))]
        if ways[unit] == "all":
            sums[unit, 5] += [
                send(
                    source,
                    there,
                    summed.at[c, 1 - y_low, (z - by + 4) % 4, :, column],
                    device(moved(across_y, "z", by)),
                )
                for by in range(4)
            ]

    def reduce_six(unit):
        if ways[unit] == "all":
            return
        source, column = whole(unit)
        arrive(sums[unit, 5])
        local_pending.pop(unit).wait()
        if ways[unit] == "zy":
            source = summed.at[c, y_low, :, :, column]
            sums[unit, 6] = [send(source, source, summed.at[c, 1 - y_low, :, :, column], device(across_y))]
        else:
            source = summed.at[c, :, z, :, column]
            along_z(unit, 6, source, source, lambda at_z: summed.at[c, :, at_z, :, column])

    def reduce_seven(unit):
        if ways[unit] == "all":
            arrive(sums[unit, 5])
            local_pending.pop(unit).wait()
        else:
            arrive(sums[unit, 6])
        source, column = whole(unit)
        source = summed.at[c, :, :, :, column]
        sums[unit, 7] = [send(source, source, summed.at[sib, :, :, :, column], sibling)]

    stages = (reduce_one, reduce_two, reduce_three, reduce_four, reduce_five, reduce_six, reduce_seven)

    def reduce(unit):
        stage = g_stage[unit]
        g_stage[unit] += 2 if stage == 4 and ways[unit] == "all" else 1
        if stage >= 4:
            stages[stage](unit)
        else:
            for index in range(len(plans[unit])):
                stages[stage](unit, index)

    def all_cots():
        return cots[...].reshape(512, 1024)

    def cot_half(half):
        return cots[:, :, lanes(half * 512, 512, 512)].reshape(512, 512)

    def grads_own(offset, size, values):
        grads[pl.ds(2 * c, 2), :, :, :, lanes(offset, size)] = values.astype(BF16).reshape(2, 4, 4, 16, size)

    def grads_other(offset, size, values):
        weights[pl.ds(2 * sib, 2), :, :, :, lanes(offset, size)] = values.astype(BF16).reshape(2, 4, 4, 16, size)

    def turned(values, t):
        turned_lhs[pl.ds(2 * t, 2)] = values.astype(BF16).reshape(2, 4, 4, 16, 512)

    for t in range(2):
        columns = slice(t * 512, (t + 1) * 512)
        turned(dot_tn(active[2 * sib], cots[:, :, columns].reshape(512, 512)), t)
    spare[...] = dot_tn(active[1], cot_half(sib)).astype(BF16).reshape(2, 4, 4, 16, 512)
    to_sibling = [
        send(source, view(grads, {"x": pl.ds(2 * c, 2)}, at, 512), view(grads, {"x": pl.ds(2 * sib, 2)}, at, 512), sibling)
        for source, at in (
            (turned_lhs.at[0:2], G_DN),
            (turned_lhs.at[2:4], G_DN + 512),
            (spare, G_DN + 1024),
        )
    ]
    for t in range(2):
        values = dot_tn(active[2 * c], cots[:, :, t * 512 : (t + 1) * 512].reshape(512, 512))
        grads_own(G_DN + t * 512, 512, values)
    grads_own(G_DN + 1024, 512, dot_tn(active[1], cot_half(c)))
    exchange("down")
    arrive(to_sibling)
    reduce(0)
    gathered(2)
    other_down = to_other(DN0, 1536, 1024)
    flush()
    turned_lhs[...] = all_mid().T.reshape(4, 4, 4, 16, 512)
    arrive([other_down])

    def left():
        return turned_lhs[...].reshape(1024, 512)

    def back_active(kind, q):
        if kind == 0:
            group = 2 * c
            values = dot_nt(all_cots(), weight_rows(2 * c + q, DN0, 1024))
        elif kind == 1:
            group = 2 * sib
            values = dot_nt(all_cots(), other_weights[q, :, :, :, 1024:2048].reshape(256, 1024))
        else:
            group = 1
            values = dot_nt(cot_half(c), weight_rows(2 * c + q, DN0 + 1024, 512)) + dot_nt(
                cot_half(sib), other_weights[q, :, :, :, 2048:2560].reshape(256, 512)
            )
        for h in range(2):
            column = q * 1536 + (3 * h + group) * 128
            pulled = values[:, h * 128 : (h + 1) * 128]
            gate = gate_up[:, lanes(column, 128)].astype(F32)
            up = gate_up[:, lanes(column + 768, 128)].astype(F32)
            sigma = jax.nn.sigmoid(gate)
            back_gate = pulled * up * sigma * (1.0 + gate * (1.0 - sigma))
            gate_up[:, lanes(column, 128)] = back_gate.astype(BF16)
            gate_up[:, lanes(column + 768, 128)] = (pulled * gate * sigma).astype(BF16)

    def back_mid(half):
        def body(row, carry):
            values = dot_nt(
                gate_up[:, half * 1536 : (half + 1) * 1536], weight_rows(row, GU0 + half * 1536, 1536)
            )
            columns = lanes(row * 256, 256)
            if half == 0:
                two_parts(values, columns)
            else:
                part[0, :, columns] += values[:256]
                part[1, :, columns] += values[256:]
            return carry

        lax.fori_loop(0, 4, body, 0)

    def gate_up_grads(half):
        def body(t, carry):
            column = half * 1536 + t * 256
            values = dot(left(), gate_up[:, lanes(column, 256)])
            weights[:, :, :, :, lanes(GU0 + column, 256)] = values.astype(BF16).reshape(4, 4, 4, 16, 256)
            return carry

        lax.fori_loop(0, 6, body, 0)

    for kind in range(3):
        back_active(kind, 0)
    exchange("active0")
    back_mid(0)
    gate_up_grads(0)
    reduce(1)
    exchange("gu0")
    for kind in range(3):
        back_active(kind, 1)
    exchange("active1")
    back_mid(1)
    exchange("mid1")
    across = send(part.at[sib], got_part, got_part, sibling)
    gate_up_grads(1)
    reduce(2)
    exchange("gu1")
    arrive([across])
    back = part[c] + got_part[...]
    unit_mid, scale_mid = unit_of(middle[...])
    gains_acc[1:2, :] = jnp.sum(back * unit_mid, axis=0, keepdims=True)
    back_middle = cots[c].astype(F32) + norm_back(back, gain_mid, unit_mid, scale_mid)
    branch[c] = back_middle.astype(BF16)
    across.sent()
    pending.remove(across)
    across_branch = send(branch.at[c], branch.at[c], branch.at[sib], sibling)
    cots[c] = (back_middle - branch[c].astype(F32)).astype(BF16)

    down_rows = lambda t: (
        dot(active[2 * c], weight_own(DN0 + t * 256, 256))
        + dot(active[2 * sib], weight_other(1024 + t * 256, 256))
    )
    for t in range(4):
        values = down_rows(t)
        two_parts(values, pl.ds(t * 256, 256))
    for half, load in ((c, lambda: weight_own(DN0 + 1024, 512)), (sib, lambda: weight_other(2048, 512))):
        values = dot(active[1], load())
        columns = lanes(half * 512, 512, 512)
        part[0, :, columns] += values[:256]
        part[1, :, columns] += values[256:]
    across_down = send(part.at[sib], got_down, got_down, sibling)
    middle[...] += part[c]
    exchange("output")
    arrive([across_branch])

    def all_branch():
        return branch[...].reshape(512, 1024)

    for t in range(2):
        columns = slice(t * 512, (t + 1) * 512)
        turned(dot_tn(mixed[sib], branch[:, :, columns].reshape(512, 512)), t)
    to_sibling = [
        send(
            turned_lhs.at[2 * t : 2 * t + 2],
            view(grads, {"x": pl.ds(2 * c, 2)}, G_OUT + t * 512, 512),
            view(grads, {"x": pl.ds(2 * sib, 2)}, G_OUT + t * 512, 512),
            sibling,
        )
        for t in range(2)
    ]
    for t in range(2):
        columns = slice(t * 512, (t + 1) * 512)
        grads_own(G_OUT + t * 512, 512, dot_tn(mixed[c], branch[:, :, columns].reshape(512, 512)))
    mixed_back = (
        dot_nt(all_branch(), weight_own(OUT0, 1024)).astype(BF16),
        dot_nt(all_branch(), weight_other(0, 1024)).astype(BF16),
    )
    for h, values in ((c, mixed_back[0]), (sib, mixed_back[1])):
        hidden_mid[h, :, 0:512] = values[:256]
        hidden_mid[h, :, 512:1024] = values[256:]
    arrive(to_sibling)
    reduce(3)
    exchange("mixed")
    gains_acc[2:3, :] = jnp.zeros((1, 1024), F32)

    def attend_back(step, carry):
        b, g = step // 4, step % 4
        rows, query, key, value = heads_of(b, g)
        column = lanes(b * 512 + g * 128, 128)
        pulled = jnp.concatenate([hidden_mid[h, :, column] for h in range(2)], axis=0)
        bias = mask_turned[b].astype(F32)
        scores = dot_nt(key, query) * (SCALE * LOG2E) + jnp.concatenate([bias, bias], axis=1)
        expo = jnp.exp2(scores)
        probs = expo * (1.0 / jnp.sum(expo, axis=0, keepdims=True))
        back_probs = dot_nt(value, pulled)
        inner = jnp.sum(probs * back_probs, axis=0, keepdims=True)
        back_scores = (probs * (back_probs - inner) * SCALE).astype(BF16)
        back_query = dot_tn(back_scores, key)
        back_key = dot(back_scores, query)
        back_value = dot(probs.astype(BF16), pulled)
        cosine = rope[b, :, 0:128]
        sine = rope[b, :, 128:256]

        def through(upstream, column, gain):
            values = raw[rows, lanes(column, 128)].astype(F32)
            scale = lax.rsqrt(head_mean(values * values) + EPS)
            unit = values * scale
            plain = upstream * cosine - pltpu.roll(upstream, 64, 1) * sine
            term = plain * unit
            pushed = plain * gain
            result = scale * (pushed - unit * head_mean(term * gain))
            gate_up[rows, lanes(column, 128)] = result.astype(BF16)
            return jnp.sum(term, axis=0, keepdims=True)

        for h in range(2):
            gains_acc[2:3, 0:128] += through(
                back_query[h * 256 : (h + 1) * 256], (2 * g + h) * 128, gain_query
            )
        gains_acc[2:3, 128:256] += through(back_key, 1024 + g * 128, gain_key)
        gate_up[rows, lanes(1536 + g * 128, 128)] = back_value.astype(BF16)
        return carry

    lax.fori_loop(0, 4, attend_back, 0)
    exchange("attend0")
    lax.fori_loop(4, 8, attend_back, 0)
    exchange("attend1")
    for transfer in to_sibling:
        transfer.sent()
        pending.remove(transfer)
    turned_lhs[...] = all_hidden().T.reshape(4, 4, 4, 16, 512)

    def qkv_grads(t, carry):
        values = dot(left(), gate_up[:, lanes(t * 256, 256)])
        column = t * 256 + jnp.where(t < 4, OUT0, DN0 - 1024)
        weights[:, :, :, :, lanes(column, 256)] = values.astype(BF16).reshape(4, 4, 4, 16, 256)
        return carry

    lax.fori_loop(0, 4, qkv_grads, 0)
    reduce(4)
    exchange("query")
    lax.fori_loop(4, 8, qkv_grads, 0)
    reduce(5)
    exchange("key")
    across_down.sent()
    pending.remove(across_down)

    def back_in(row, carry):
        values = dot_nt(gate_up[:, 0:2048], weight_rows(row, QKV0, 2048))
        two_parts(values, lanes(row * 256, 256))
        return carry

    lax.fori_loop(0, 4, back_in, 0)
    across = send(part.at[sib], got_part, got_part, sibling)
    across_down.arrived()
    hidden_mid[c] = (middle[...] + got_down[...]).astype(BF16)
    copy_out = pltpu.make_async_copy(hidden_mid.at[c], activations, local_sem.at[0])
    copy_out.start()
    exchange("in")
    arrive([across])
    back = part[c] + got_part[...]
    unit_in, scale_in = unit_of(toks[c].astype(F32))
    gains_acc[0:1, :] = jnp.sum(back * unit_in, axis=0, keepdims=True)
    back_middle = branch[c].astype(F32) + cots[c].astype(F32)
    hidden_mid[sib] = (back_middle + norm_back(back, gain_in, unit_in, scale_in)).astype(BF16)
    copy_in = pltpu.make_async_copy(hidden_mid.at[sib], input_grad, local_sem.at[1])
    copy_in.start()

    low = jnp.concatenate(
        [gains_acc[r : r + 1, i * 128 : (i + 1) * 128] for r in range(2) for i in range(8)], axis=0
    ).astype(BF16)
    high = jnp.concatenate(
        [gains_acc[2:3, 0:128], gains_acc[2:3, 128:256], jnp.zeros((14, 128), F32)], axis=0
    ).astype(BF16)
    gains_at = slice(DN0 + 1024, DN0 + 1152)
    weights[:, :, :, :, gains_at] = jnp.zeros((4, 4, 4, 16, 128), BF16)
    for part_x in range(4):
        for part_y in (0, 2):
            weights[part_x, part_y, 0, :, gains_at] = low
            weights[part_x, part_y, 1, :, gains_at] = high
    reduce(6)
    exchange("end")
    assert g_stage == [7] * UNITS, g_stage
    for unit in range(UNITS):
        arrive(sums[unit, 7])
    copy_out.wait()
    copy_in.wait()
    flush()
    assert used[0] <= TRANSFERS and local_count[0] <= 48, used


TRANSFERS = 416


def run_layer(*operands):
    anywhere = pl.BlockSpec(memory_space=pl.ANY)
    vmem = pltpu.VMEM
    return pl.pallas_call(
        layer_kernel,
        out_shape=(
            jax.ShapeDtypeStruct((TOK, D), BF16),
            jax.ShapeDtypeStruct((TOK, D), BF16),
            jax.ShapeDtypeStruct((2, 2, 4, 16, S_COLS), BF16),
        ),
        in_specs=[anywhere] * 9,
        out_specs=(anywhere,) * 3,
        scratch_shapes=[
            vmem((4, 4, 4, 16, WCOLS), BF16),
            vmem((4, 4, 4, 16, G_COLS), BF16),
            vmem((2, 4, 4, 16, 2560), BF16),
            vmem((2, 2, 4, 16, WCOLS), BF16),
            vmem((2, 4, 4, 16, WCOLS), BF16),
            vmem((3, 4, 16, WCOLS), BF16),
            vmem((3, 16, WCOLS), BF16),
            vmem((2, TOK, D), BF16),
            vmem((2, TOK, D), BF16),
            vmem((2, TOK, 256), F32),
            vmem((2, TOK, TOK), BF16),
            vmem((2, TOK, TOK), BF16),
            vmem((2, TOK, D), BF16),
            vmem((2 * TOK, 1536), BF16),
            vmem((12, 2 * TOK, HD), BF16),
            vmem((4, 2 * TOK, HD), BF16),
            vmem((2, 2 * TOK, 512), BF16),
            vmem((2, TOK, D), F32),
            vmem((TOK, D), F32),
            vmem((TOK, D), F32),
            vmem((TOK, D), F32),
            vmem((2, TOK, D), BF16),
            vmem((2 * TOK, 3072), BF16),
            vmem((3, 2 * TOK, 512), BF16),
            vmem((2, TOK, D), BF16),
            vmem((4, 4, 4, 16, 2 * TOK), BF16),
            vmem((2, 4, 4, 16, 2 * TOK), BF16),
            vmem((8, D), F32),
            pltpu.SemaphoreType.DMA((48,)),
            pltpu.SemaphoreType.DMA((TRANSFERS,)),
            pltpu.SemaphoreType.DMA((TRANSFERS,)),
        ],
        compiler_params=pltpu.CompilerParams(
            collective_id=0, has_side_effects=True, vmem_limit_bytes=64 * 2**20
        ),
        cost_estimate=pl.CostEstimate(flops=26 * 10**9, bytes_accessed=10**7, transcendentals=10**6),
    )(*operands)


def adamw(master, first, second, gradient, rate, decay):
    first_new = 0.9 * first + 0.1 * gradient
    second_new = 0.999 * second + 0.001 * gradient * gradient
    direction = first_new / (1.0 - 0.9**STEP) / (jnp.sqrt(second_new / (1.0 - 0.999**STEP)) + 1e-08)
    return (master - rate * (direction + decay * master), first_new, second_new)


def step_places():
    qkv = [(0, c * 1024, c, S_QKV, 1024) for c in range(2)]
    qkv += [(0, 2048 + c * 512, c, S_QKV + 1024, 512) for c in range(2)]
    qkv += [(0, 3072 + c * 512, c, S_QKV + 1536, 512) for c in range(2)]
    out = [(c, 0, c, S_OUT, 1024) for c in range(2)]
    gate_up = [
        (0, up * 3072 + c * 1536 + half * 768, c, S_GU + half * 1536 + up * 768, 768)
        for up in range(2)
        for c in range(2)
        for half in range(2)
    ]
    down = [(0, 0, 0, S_DN, 1024), (2, 0, 1, S_DN, 1024)]
    down += [(1, c * 512, c, S_DN + 1024, 512) for c in range(2)]
    return qkv, out, gate_up, down


def step_kernel(*refs):
    states, summed, news = refs[:12], refs[12], refs[13:]
    for index, places in enumerate(step_places()):
        master, first, second = states[3 * index : 3 * index + 3]
        for group, column, core, at, size in places:
            here = (group, slice(None), pl.ds(column, size))
            results = adamw(
                master[here],
                first[here],
                second[here],
                summed[core, :, pl.ds(at, size)].astype(F32),
                0.05,
                0.1,
            )
            for ref, value in zip(news[3 * index : 3 * index + 3], results):
                ref[here] = value


def step(masters, firsts, seconds, summed):
    rows = 16
    arrays, specs, shapes = [], [], []
    for state in zip(masters, firsts, seconds):
        for array in state:
            groups = array.shape[0] // 128
            arrays.append(array.reshape(groups, 128, -1))
            specs.append(pl.BlockSpec((groups, rows, array.shape[1]), lambda i: (0, i, 0)))
            shapes.append(jax.ShapeDtypeStruct(arrays[-1].shape, F32))
    results = pl.pallas_call(
        step_kernel,
        grid=(128 // rows,),
        out_shape=tuple(shapes),
        in_specs=specs + [pl.BlockSpec((2, rows, S_COLS), lambda i: (0, i, 0))],
        out_specs=tuple(specs),
        compiler_params=pltpu.CompilerParams(vmem_limit_bytes=62 * 2**20),
        cost_estimate=pl.CostEstimate(flops=3 * 10**7, bytes_accessed=5 * 10**7, transcendentals=10**6),
    )(*arrays, summed)
    results = [value.reshape(-1, value.shape[2]) for value in results]
    return [tuple(results[3 * index : 3 * index + 3]) for index in range(4)]


def per_device(
    tokens,
    cotangent,
    segment_ids,
    positions,
    master_qkv,
    master_out,
    master_gate_up,
    master_down,
    master_gains,
    first_qkv,
    first_out,
    first_gate_up,
    first_down,
    first_gains,
    second_qkv,
    second_out,
    second_gate_up,
    second_down,
    second_gains,
):
    me = coordinates()
    shard = lax.axis_index("shard")
    order = jnp.minimum((me["y"] % 2) * 4 + me["z"], 2)
    gains = lax.dynamic_slice(
        jnp.pad(master_gains, (2048, 6144)), (2048 + 2048 * order - 288 * shard,), (2048,)
    ).reshape(16, 128)

    freq = jnp.exp(jnp.arange(HD // 2).astype(F32) * (-2.0 * math.log(1000000.0) / HD))
    angle = positions[0].astype(F32)[:, None] * freq
    cosine = jnp.cos(angle)
    sine = jnp.sin(angle)
    tables = jnp.concatenate([cosine, sine], axis=-1)

    activations, input_grad, summed = run_layer(
        tokens,
        cotangent,
        tables,
        jnp.broadcast_to(segment_ids.astype(F32), (8, TOK)),
        gains,
        master_qkv,
        master_out,
        master_gate_up,
        master_down,
    )
    summed = summed.reshape(2, 128, S_COLS)
    gain_rows = summed[:, :32, S_GAIN : S_GAIN + 128].astype(F32).sum(axis=0).reshape(-1)
    grad_gains = lax.dynamic_slice(gain_rows, (288 * shard,), (288,))
    updated = step(
        (master_qkv, master_out, master_gate_up, master_down),
        (first_qkv, first_out, first_gate_up, first_down),
        (second_qkv, second_out, second_gate_up, second_down),
        summed,
    )
    updated.append(adamw(master_gains, first_gains, second_gains, grad_gains, 0.4, 0.0))
    return (
        activations,
        input_grad,
        *(new[0] for new in updated),
        *(new[1] for new in updated),
        *(new[2] for new in updated),
    )


def solution(mesh):
    rows = P(("rep", "shard"), None)
    state = (P("shard", None),) * 4 + (P("shard"),)
    return jax.shard_map(
        per_device,
        mesh=mesh,
        in_specs=(rows,) * 4 + state * 3,
        out_specs=(rows,) * 2 + state * 3,
        check_vma=False,
    )
```

```python
import math

import jax
import jax.numpy as jnp
from jax import lax
from jax.experimental import pallas as pl
from jax.experimental.pallas import tpu as pltpu
from jax.sharding import PartitionSpec as P

D = 1024
HEADS = 16
KV_HEADS = 8
HD = 128
FF = 3072
STEP = 10
Q_WIDTH = 2048
KV_WIDTH = 1024
TOK = 256
F32 = jnp.float32
BF16 = jnp.bfloat16
EPS = 1e-06
SCALE = HD ** (-0.5)

QKV0, GAIN0, OUT0, GU0, DN0, WCOLS = 0, 2048, 2176, 3200, 6272, 7808
G_OUT, G_DN, G_COLS = 0, 1024, 2560
S_GU, S_QKV, S_GAIN, S_DN, S_OUT, S_COLS = 0, 3072, 5120, 5632, 7168, 8192
LOG2E = 1.4426950408889634
ROTATIONS = (("x", "y", "z"), ("y", "z", "x"), ("z", "x", "y"))

SCHEDULE = {
    "start": ("W0", "W1", "W2",),
    "early": ("W0", "W1", "W0", "W2", "W1", "W0", "W2", "W1", "W0", "W1", "W2",),
    "mid": ("W2",),
    "gu0": ("G0",),
    "gu1": ("G1",),
    "mixed": ("G2", "G0",),
    "attend1": ("G1",),
    "key": ("G2", "G0",),
    "in": ("G3", "G1", "G2", "G4",),
    "end": tuple("G" + unit for unit in "05312405631204653120645310625413645"),
}
BY_NEIGHBOURS = (True, True, True, True, False, False, False)
WAYS = ("yz", "yz", "zy", "all", "zy", "yzd", "all")


def dot(left, right):
    return jnp.dot(left, right, preferred_element_type=F32)


def dot_nt(left, right):
    return lax.dot_general(left, right, (((1,), (1,)), ((), ())), preferred_element_type=F32)


def dot_tn(left, right):
    return lax.dot_general(left, right, (((0,), (0,)), ((), ())), preferred_element_type=F32)


def lanes(start, size, step=128):
    return pl.ds(start if isinstance(start, int) else pl.multiple_of(start, step), size)


def steps_of(count, body, first=0):
    for index in range(first, count):
        body(index, 0)


def coordinates():
    rep = lax.axis_index("rep")
    shard = lax.axis_index("shard")
    return {
        "x": shard // 2,
        "y": (shard % 2) * 2 + (rep // 2) % 2,
        "z": rep // 4,
        "c": rep % 2,
    }


def device(at):
    return {"rep": at["z"] * 4 + (at["y"] % 2) * 2 + at["c"], "shard": at["x"] * 2 + at["y"] // 2}


def moved(me, axis, by):
    return {**me, axis: (me[axis] + by + 4) % 4}


def view(ref, select, offset, size):
    where = tuple(select.get(axis, slice(None)) for axis in "xyz")
    return ref.at[where + (slice(None), lanes(offset, size))]


def layer_kernel(
    tokens,
    cotangent,
    segments,
    positions,
    gains,
    master_qkv,
    master_out,
    master_gate_up,
    master_down,
    activations,
    input_grad,
    summed,
    weights,
    grads,
    other_weights,
    got_far,
    got_near,
    got_two,
    got_three,
    toks,
    cots,
    rope,
    mask,
    mask_turned,
    hidden,
    raw,
    rotated,
    vals,
    mixed,
    part,
    got_part,
    got_down,
    numbers,
    middle,
    hidden_mid,
    gate_up,
    active,
    branch,
    turned_lhs,
    spare,
    gains_acc,
    local_sem,
    send_sem,
    recv_sem,
):
    me = coordinates()
    c = me["c"]
    sib = 1 - c
    x, y, z = me["x"], me["y"], me["z"]
    sibling = device({**me, "c": sib})
    used = [0]

    class Transfer:
        def __init__(self, source, there, here, target):
            self.index = used[0]
            used[0] += 1
            self.source, self.there, self.here, self.target = source, there, here, target
            self.copy(source, there).start()

        def copy(self, source, there):
            return pltpu.make_async_remote_copy(
                src_ref=source,
                dst_ref=there,
                send_sem=send_sem.at[self.index],
                recv_sem=recv_sem.at[self.index],
                device_id=self.target,
                device_id_type=pl.DeviceIdType.MESH,
            )

        def arrived(self):
            self.copy(self.here, self.here).wait_recv()

        def sent(self):
            self.copy(self.source, self.there).wait_send()

    pending = []

    def send(source, there, here, target):
        transfer = Transfer(source, there, here, target)
        pending.append(transfer)
        return transfer

    def flush():
        while pending:
            pending.pop(0).sent()

    def arrive(transfers):
        for transfer in transfers:
            transfer.arrived()

    row = 16 * ((y % 2) * 4 + z)

    def rows_of(ref, first, offset, size):
        return ref.at[pl.ds(pl.multiple_of(first, 16), 16), lanes(offset, size)]

    groups = [
        (rows_of(master_qkv, row, c * 1024, 1024), QKV0, 1024),
        (rows_of(master_qkv, row, 2048 + c * 512, 512), QKV0 + 1024, 512),
        (rows_of(master_qkv, row, 3072 + c * 512, 512), QKV0 + 1536, 512),
        (rows_of(master_out, c * 128 + row, 0, 1024), OUT0, 1024),
        (rows_of(master_gate_up, row, c * 1536, 768), GU0, 768),
        (rows_of(master_gate_up, row, 3072 + c * 1536, 768), GU0 + 768, 768),
        (rows_of(master_gate_up, row, c * 1536 + 768, 768), GU0 + 1536, 768),
        (rows_of(master_gate_up, row, 3072 + c * 1536 + 768, 768), GU0 + 2304, 768),
        (rows_of(master_down, c * 256 + row, 0, 1024), DN0, 1024),
        (rows_of(master_down, 128 + row, c * 512, 512), DN0 + 1024, 512),
    ]
    inward = [
        (source, got_part.at[pl.ds(16 * index, 16), pl.ds(0, size)])
        for index, (source, offset, size) in enumerate(groups)
    ]
    inward += [(gains, got_part.at[pl.ds(160, 16), pl.ds(0, 128)])]
    first_inward = len(inward)
    inward += [
        (segments, numbers.at[0]),
        (positions, numbers.at[1]),
        (tokens, toks.at[c]),
        (cotangent, cots.at[c]),
    ]
    inward = [pltpu.make_async_copy(*pair, local_sem.at[index]) for index, pair in enumerate(inward)]

    barrier = pltpu.get_barrier_semaphore()
    across_y = {**me, "y": y + 1 - 2 * (y % 2)}
    friends = [sibling] + [device(moved(me, axis, by)) for axis in "xyz" for by in (1, 2, 3)]
    friends += [device(moved(across_y, "z", by)) for by in (1, 2, 3)]
    for friend in friends:
        pl.semaphore_signal(barrier, inc=1, device_id=friend, device_id_type=pl.DeviceIdType.MESH)
    for copy in inward:
        copy.start()
    for copy in inward[:first_inward]:
        copy.wait()
    for index, (source, offset, size) in enumerate(groups):
        rows16 = got_part[16 * index : 16 * index + 16, 0:size]
        weights[x, y, z, :, offset : offset + size] = rows16.astype(BF16)
    weights[x, y, z, :, GAIN0 : GAIN0 + 128] = got_part[160:176, 0:128].astype(BF16)
    pl.semaphore_wait(barrier, len(friends))

    def gather_one(rotation, offset, size):
        first, second, third = rotation
        source = view(weights, {"x": x, "y": y, "z": z}, offset, size)
        out = []
        for by in (1, 2, 3):
            here = view(weights, {**{"x": x, "y": y, "z": z}, third: (me[third] - by + 4) % 4}, offset, size)
            out.append(send(source, source, here, device(moved(me, third, by))))
        return out

    def gather_two(rotation, offset, size):
        first, second, third = rotation
        source = view(weights, {first: me[first], second: me[second]}, offset, size)
        out = []
        for by in (1, 3):
            here = view(weights, {first: me[first], second: (me[second] - by + 4) % 4}, offset, size)
            out.append(send(source, source, here, device(moved(me, second, by))))
        return out

    def gather_on(rotation, offset, size):
        first, second, third = rotation
        out = []
        for by, half in ((1, 0), (3, 1)):
            spot = {first: me[first], third: pl.ds(2 * half, 2)}
            source = view(weights, {**spot, second: (me[second] - by + 4) % 4}, offset, size)
            here = view(weights, {**spot, second: (me[second] + 2) % 4}, offset, size)
            out.append(send(source, source, here, device(moved(me, second, by))))
        return out

    def gather_three(rotation, offset, size):
        first = rotation[0]
        source = view(weights, {first: me[first]}, offset, size)
        out = []
        for by in (1, 3):
            here = view(weights, {first: (me[first] - by + 4) % 4}, offset, size)
            out.append(send(source, source, here, device(moved(me, first, by))))
        return out

    def gather_four(rotation, offset, size):
        first, second = rotation[0], rotation[1]
        out = []
        for by, half in ((1, 0), (3, 1)):
            rows = pl.ds(2 * half, 2)
            source = view(weights, {first: (me[first] - by + 4) % 4, second: rows}, offset, size)
            here = view(weights, {first: (me[first] + 2) % 4, second: rows}, offset, size)
            out.append(send(source, source, here, device(moved(me, first, by))))
        return out

    chunks = (
        ((0, 1152), (1152, 1024), (OUT0, 1024)),
        ((GU0, 1024), (GU0 + 1024, 1024), (GU0 + 2048, 1024)),
        ((DN0, 512), (DN0 + 512, 512), (DN0 + 1024, 512)),
    )
    steps = (gather_one, gather_two, gather_on, gather_three, gather_four)
    flying = [[None] * 3 for _ in chunks]

    w_step = [0] * len(chunks)

    def pump(chunk):
        step = w_step[chunk]
        w_step[chunk] += 1
        for index, rotation in enumerate(ROTATIONS):
            if step:
                arrive(flying[chunk][index])
            if step < len(steps):
                flying[chunk][index] = steps[step](rotation, *chunks[chunk][index])

    def gathered(chunk):
        while w_step[chunk] <= len(steps):
            pump(chunk)

    def exchange(name):
        for item in SCHEDULE.get(name, ()):
            (pump if item[0] == "W" else reduce)(int(item[1]))

    exchange("start")
    for copy in inward[first_inward:]:
        copy.wait()
    order = lax.broadcasted_iota(jnp.int32, (64, 256), 0).astype(F32)
    angle = jnp.exp(order * (-2.0 * math.log(1000000.0) / HD)) * numbers[1].astype(F32)
    cosine = jnp.cos(angle)
    sine = jnp.sin(angle)
    rope[c, :, 0:128] = jnp.concatenate([cosine, cosine], axis=0).T
    rope[c, :, 128:256] = jnp.concatenate([-sine, sine], axis=0).T
    across_segments = jnp.broadcast_to(numbers[0].astype(F32), (256, 256))
    same = across_segments == across_segments.T
    earlier = lax.broadcasted_iota(jnp.int32, (256, 256), 1) <= lax.broadcasted_iota(
        jnp.int32, (256, 256), 0
    )
    mask[c] = jnp.where(same & earlier, 0.0, -1e30).astype(BF16)
    early = [
        send(toks.at[c], toks.at[c], toks.at[sib], sibling),
        send(rope.at[c], rope.at[c], rope.at[sib], sibling),
        send(mask.at[c], mask.at[c], mask.at[sib], sibling),
        send(cots.at[c], cots.at[c], cots.at[sib], sibling),
    ]
    exchange("early")
    arrive(early)
    for b in range(2):
        mask_turned[b] = mask[b].astype(F32).T.astype(BF16)
    exchange("late")
    gathered(0)

    def to_other(offset, size, at):
        return send(
            view(weights, {"x": pl.ds(2 * sib, 2)}, offset, size),
            view(other_weights, {}, at, size),
            view(other_weights, {}, at, size),
            sibling,
        )

    other_out = to_other(OUT0, 1024, 0)

    def weight(offset, size):
        return weights[:, :, :, :, lanes(offset, size)].reshape(1024, size)

    def weight_rows(row, offset, size):
        return weights[row, :, :, :, lanes(offset, size)].reshape(256, size)

    def weight_own(offset, size):
        return weights[pl.ds(2 * c, 2), :, :, :, lanes(offset, size)].reshape(512, size)

    def weight_other(offset, size):
        return other_weights[:, :, :, :, lanes(offset, size)].reshape(512, size)

    gain_rows = jnp.zeros((16, 128), F32)
    head_rows = jnp.zeros((16, 128), F32)
    for part_x in range(4):
        for part_y in (0, 2):
            gain_rows += weights[part_x, part_y, 0, :, pl.ds(GAIN0, 128)].astype(F32)
            head_rows += weights[part_x, part_y, 1, :, pl.ds(GAIN0, 128)].astype(F32)
    gain_in = jnp.concatenate([gain_rows[i : i + 1] for i in range(8)], axis=1)
    gain_mid = jnp.concatenate([gain_rows[i : i + 1] for i in range(8, 16)], axis=1)
    gain_query = head_rows[0:1]
    gain_key = head_rows[1:2]

    def unit_of(values):
        scale = lax.rsqrt(jnp.mean(values * values, axis=-1, keepdims=True) + EPS)
        return values * scale, scale

    def norm_back(upstream, gain, unit, scale):
        pushed = upstream * gain
        inner = jnp.mean(pushed * unit, axis=-1, keepdims=True)
        return scale * (pushed - unit * inner)

    for b in range(2):
        unit, _ = unit_of(toks[b].astype(F32))
        hidden[b] = (unit * gain_in).astype(BF16)

    def all_hidden():
        return hidden[...].reshape(512, 1024)

    mean_of = jnp.full((128, 128), 1.0 / 128, BF16)

    def head_mean(values):
        return dot(values.astype(BF16), mean_of)

    def project_heads(t, carry):
        values = dot(all_hidden(), weight(QKV0 + t * 256, 256))
        raw[:, lanes(t * 256, 256)] = values.astype(BF16)
        gain = gain_query if t < 4 else gain_key
        cosine = rope[:, :, 0:128].reshape(512, 128)
        sine = rope[:, :, 128:256].reshape(512, 128)
        for h in range(2):
            head = values[:, h * 128 : (h + 1) * 128]
            normal = head * lax.rsqrt(head_mean(head * head) + EPS) * gain
            rotated[2 * t + h] = (normal * cosine + pltpu.roll(normal, 64, 1) * sine).astype(BF16)
        return carry

    steps_of(6, project_heads)

    def project_values(t, carry):
        values = dot(all_hidden(), weight(QKV0 + 1536 + t * 256, 256)).astype(BF16)
        vals[2 * t] = values[:, :128]
        vals[2 * t + 1] = values[:, 128:]
        return carry

    steps_of(2, project_values)
    exchange("project")

    def heads_of(b, g):
        rows = pl.ds(pl.multiple_of(b * 256, 256), 256)
        query = rotated[pl.ds(2 * g, 2), rows, :].reshape(512, 128)
        return rows, query, rotated[8 + g, rows, :], vals[g, rows, :]

    def attend(step, carry):
        b, g = step // 4, step % 4
        rows, query, key, value = heads_of(b, g)
        scores = dot_nt(query, key).reshape(2, 256, 256) * (SCALE * LOG2E) + mask[b].astype(F32)[None]
        expo = jnp.exp2(scores).reshape(512, 256).astype(BF16)
        result = dot(expo, jnp.concatenate([value, jnp.ones((256, 128), BF16)], axis=1))
        result = (result[:, :128] / result[:, 128:]).astype(BF16)
        for h in range(2):
            mixed[h, rows, lanes(g * 128, 128)] = result[h * 256 : (h + 1) * 256]
        return carry

    lax.fori_loop(0, 8, attend, 0, unroll=4)

    exchange("attend")
    arrive([other_out])

    def two_parts(values, columns):
        part[0, :, columns] = values[:256]
        part[1, :, columns] = values[256:]

    def project_out(t, carry):
        values = dot(mixed[c], weight_own(OUT0 + t * 512, 512)) + dot(
            mixed[sib], weight_other(t * 512, 512)
        )
        two_parts(values, lanes(t * 512, 512))
        return carry

    steps_of(2, project_out)
    exchange("projected")
    across = send(part.at[sib], got_part, got_part, sibling)
    across.arrived()
    middle[...] = toks[c].astype(F32) + part[c] + got_part[...]
    unit_mid, _ = unit_of(middle[...])
    hidden_mid[c] = (unit_mid * gain_mid).astype(BF16)
    across_mid = send(hidden_mid.at[c], hidden_mid.at[c], hidden_mid.at[sib], sibling)
    across.sent()
    pending.remove(across)
    exchange("mid")
    gathered(1)
    arrive([across_mid])

    def all_mid():
        return hidden_mid[...].reshape(512, 1024)

    def feed_forward(t, carry):
        column = (t // 3) * 1536 + (t % 3) * 256
        gate = dot(all_mid(), weight(GU0 + column, 256))
        up = dot(all_mid(), weight(GU0 + column + 768, 256))
        gate_up[:, lanes(column, 256)] = gate.astype(BF16)
        gate_up[:, lanes(column + 768, 256)] = up.astype(BF16)
        result = (gate * jax.nn.sigmoid(gate) * up).astype(BF16)
        for h in range(2):
            block = 2 * t + h
            active[block % 3, :, lanes((block // 3) * 128, 128)] = result[:, h * 128 : (h + 1) * 128]
        return carry

    steps_of(3, feed_forward)
    exchange("feed0")
    steps_of(6, feed_forward, 3)
    exchange("feed1")

    def unit_of_parts(ref, offset, sizes, column):
        parts = []
        for size in sizes:
            parts.append((ref, offset, size, column))
            offset, column = offset + size, column + size
        return parts

    plans = (
        unit_of_parts(grads, G_DN, (512, 512, 512), S_DN),
        unit_of_parts(weights, GU0, (512, 512, 512), S_GU),
        unit_of_parts(weights, GU0 + 1536, (512, 512, 512), S_GU + 1536),
        unit_of_parts(grads, G_OUT, (256, 384, 384), S_OUT),
        unit_of_parts(weights, OUT0, (512, 256, 256), S_QKV),
        unit_of_parts(weights, DN0, (256, 384, 384), S_QKV + 1024),
        unit_of_parts(weights, DN0 + 1024, (128,), S_GAIN),
    )
    UNITS = len(plans)
    landing, at = {}, 0
    for unit in range(UNITS):
        for index in range(len(plans[unit])):
            landing[unit, index] = at
            at += plans[unit][index][2]

    def remaining(rotation):
        return [axis for axis in "xyz" if axis != rotation[0]]

    def add_blocks(blocks, target, size, shape):
        count = math.prod(shape)

        def body(k, carry):
            where = []
            left = k
            for extent in reversed(shape):
                where.insert(0, left % extent)
                left = left // extent
            total = blocks[0](where)
            for block in blocks[1:]:
                total = total + block(where)
            target(where, total.astype(BF16))
            return carry

        if count == 1:
            body(0, 0)
        else:
            lax.fori_loop(0, count, body, 0)

    def reader(ref, offset, size, locate):
        return lambda where: ref[locate(where) + (slice(None), lanes(offset, size))].astype(F32)

    def writer(ref, offset, size, locate):
        def store(where, value):
            ref[locate(where) + (slice(None), lanes(offset, size))] = value

        return store

    sums = {}

    def reduce_one(unit, index):
        ref, offset, size, to = plans[unit][index]
        rotation = ROTATIONS[index]
        first, other = rotation[0], remaining(rotation)[0]
        at = landing[unit, index]
        sums[unit, index, 1] = [
            send(
                view(ref, {first: (me[first] + 2) % 4, other: pl.ds(2 * half, 2)}, offset, size),
                got_far.at[half, :, :, :, lanes(at, size)],
                got_far.at[half, :, :, :, lanes(at, size)],
                device(moved(me, first, by)),
            )
            for by, half in ((1, 0), (3, 1))
        ]

    def reduce_two(unit, index):
        ref, offset, size, to = plans[unit][index]
        rotation = ROTATIONS[index]
        first, (other, last) = rotation[0], remaining(rotation)
        at = landing[unit, index]
        arrive(sums[unit, index, 1])
        out = []
        for by, half in ((1, 0), (3, 1)):
            block = (me[first] + by) % 4

            def locate(where, block=block, half=half):
                spot = {first: block, other: where[0] + 2 * half, last: where[1]}
                return tuple(spot[axis] for axis in "xyz")

            add_blocks(
                [
                    reader(ref, offset, size, locate),
                    reader(got_far, at, size, lambda where, half=half: (half, where[0], where[1])),
                ],
                writer(ref, offset, size, locate),
                size,
                (2, 4),
            )
            out.append(
                send(
                    view(ref, {first: block}, offset, size),
                    got_near.at[half, :, :, :, lanes(at, size)],
                    got_near.at[half, :, :, :, lanes(at, size)],
                    device(moved(me, first, by)),
                )
            )
        sums[unit, index, 2] = out

    def reduce_three(unit, index):
        ref, offset, size, to = plans[unit][index]
        rotation = ROTATIONS[index]
        first, second, third = rotation
        other, last = remaining(rotation)
        at = landing[unit, index]
        arrive(sums[unit, index, 2])

        def locate(where):
            spot = {first: me[first], other: where[0], last: where[1]}
            return tuple(spot[axis] for axis in "xyz")

        add_blocks(
            [reader(ref, offset, size, locate)]
            + [
                reader(got_near, at, size, lambda where, half=half: (half, where[0], where[1]))
                for half in range(2)
            ],
            writer(ref, offset, size, locate),
            size,
            (4, 4),
        )
        if not BY_NEIGHBOURS[unit]:
            sums[unit, index, 3] = [
                send(
                    view(ref, {first: me[first], second: (me[second] + by) % 4}, offset, size),
                    got_two.at[by - 1, :, :, lanes(at, size)],
                    got_two.at[by - 1, :, :, lanes(at, size)],
                    device(moved(me, second, by)),
                )
                for by in (1, 2, 3)
            ]
            return
        sums[unit, index, 3] = [
            send(
                view(
                    ref,
                    {first: me[first], second: (me[second] + 2) % 4, third: pl.ds(2 * half, 2)},
                    offset,
                    size,
                ),
                got_two.at[2, 2 * half : 2 * half + 2, :, lanes(at, size)],
                got_two.at[2, 2 * half : 2 * half + 2, :, lanes(at, size)],
                device(moved(me, second, by)),
            )
            for by, half in ((1, 0), (3, 1))
        ]

    def reduce_on(unit, index):
        ref, offset, size, to = plans[unit][index]
        first, second, third = ROTATIONS[index]
        at = landing[unit, index]
        arrive(sums[unit, index, 3])
        out = []
        for by, half in ((1, 0), (3, 1)):
            block = (me[second] + by) % 4

            def locate(where, block=block, half=half):
                spot = {first: me[first], second: block, third: where[0] + 2 * half}
                return tuple(spot[axis] for axis in "xyz")

            add_blocks(
                [
                    reader(ref, offset, size, locate),
                    reader(got_two, at, size, lambda where, half=half: (2, where[0] + 2 * half)),
                ],
                writer(ref, offset, size, locate),
                size,
                (2,),
            )
            out.append(
                send(
                    view(ref, {first: me[first], second: block}, offset, size),
                    got_two.at[half, :, :, lanes(at, size)],
                    got_two.at[half, :, :, lanes(at, size)],
                    device(moved(me, second, by)),
                )
            )
        sums[unit, index, 3] = out

    def reduce_four(unit, index):
        ref, offset, size, to = plans[unit][index]
        first, second, third = ROTATIONS[index]
        at = landing[unit, index]
        arrive(sums[unit, index, 3])

        def locate(where):
            spot = {first: me[first], second: me[second], third: where[0]}
            return tuple(spot[axis] for axis in "xyz")

        add_blocks(
            [reader(ref, offset, size, locate)]
            + [
                reader(got_two, at, size, lambda where, by=by: (by, where[0]))
                for by in range(2 if BY_NEIGHBOURS[unit] else 3)
            ],
            writer(ref, offset, size, locate),
            size,
            (4,),
        )
        sums[unit, index, 4] = [
            send(
                view(ref, {first: me[first], second: me[second], third: (me[third] + by) % 4}, offset, size),
                got_three.at[by - 1, :, lanes(at, size)],
                got_three.at[by - 1, :, lanes(at, size)],
                device(moved(me, third, by)),
            )
            for by in (1, 2, 3)
        ]

    y_low = y % 2
    local_count = [len(inward)]
    local_pending = {}

    def whole(unit):
        ref, offset, _, to = plans[unit][0]
        size = sum(part[2] for part in plans[unit])
        return ref.at[x, y, z, :, lanes(offset, size)], lanes(to, size)

    def along_z(unit, source, there, here, steps=(1, 2, 3)):
        sums[unit] = [
            send(source, there, here((z - by + 4) % 4), device(moved(me, "z", by))) for by in steps
        ]

    def landed(unit):
        arrive(sums[unit])
        if unit in local_pending:
            local_pending.pop(unit).wait()
        return whole(unit)[1]

    def reduce_five(unit):
        for index in range(len(plans[unit])):
            ref, offset, size, to = plans[unit][index]
            at = landing[unit, index]
            arrive(sums[unit, index, 4])
            here = (x, y, z)
            add_blocks(
                [reader(ref, offset, size, lambda where: here)]
                + [reader(got_three, at, size, lambda where, by=by: (by,)) for by in range(3)],
                writer(ref, offset, size, lambda where: here),
                size,
                (1,),
            )
        source, column = whole(unit)
        there = summed.at[c, y_low, z, :, column]
        local_pending[unit] = pltpu.make_async_copy(source, there, local_sem.at[local_count[0]])
        local_count[0] += 1
        local_pending[unit].start()
        way = WAYS[unit]
        if way in ("zy", "all"):
            along_z(unit, source, there, lambda at_z: summed.at[c, y_low, at_z, :, column])
        if way in ("yz", "yzd"):
            sums[unit] = [send(source, there, summed.at[c, 1 - y_low, z, :, column], device(across_y))]
        if way == "all":
            sums[unit] += [
                send(
                    source,
                    there,
                    summed.at[c, 1 - y_low, (z - by + 4) % 4, :, column],
                    device(moved(across_y, "z", by)),
                )
                for by in range(4)
            ]

    def spread_y(unit):
        column = landed(unit)
        source = summed.at[c, y_low, :, :, column]
        sums[unit] = [send(source, source, summed.at[c, 1 - y_low, :, :, column], device(across_y))]

    def spread_z(unit):
        column = landed(unit)
        source = summed.at[c, :, z, :, column]
        steps = (1, 2, 3) if WAYS[unit] == "yzd" else (1, 3)
        along_z(unit, source, source, lambda at_z: summed.at[c, :, at_z, :, column], steps)

    def spread_on(unit):
        column = landed(unit)
        out = []
        for by, half in ((1, 0), (3, 1)):
            source = summed.at[c, half, (z - by + 4) % 4, :, column]
            here = summed.at[c, half, (z + 2) % 4, :, column]
            out.append(send(source, source, here, device(moved(me, "z", by))))
        sums[unit] = out

    def spread_core(unit):
        column = landed(unit)
        source = summed.at[c, :, :, :, column]
        sums[unit] = [send(source, source, summed.at[sib, :, :, :, column], sibling)]

    spreads = {
        "yz": (spread_z, spread_on, spread_core),
        "yzd": (spread_z, spread_core),
        "zy": (spread_y, spread_core),
        "all": (spread_core,),
    }

    def stages_of(unit):
        sums_by_part = [reduce_one, reduce_two, reduce_three, reduce_four]
        if BY_NEIGHBOURS[unit]:
            sums_by_part.insert(3, reduce_on)

        def for_parts(stage):
            def run(unit):
                for index in range(len(plans[unit])):
                    stage(unit, index)

            return run

        return [for_parts(stage) for stage in sums_by_part] + [reduce_five, *spreads[WAYS[unit]]]

    stages = [stages_of(unit) for unit in range(UNITS)]

    def reduce(unit):
        stages[unit].pop(0)(unit)

    def all_cots():
        return cots[...].reshape(512, 1024)

    def cot_half(half):
        return cots[:, :, lanes(half * 512, 512, 512)].reshape(512, 512)

    def grads_own(offset, size, values):
        grads[pl.ds(2 * c, 2), :, :, :, lanes(offset, size)] = values.astype(BF16).reshape(2, 4, 4, 16, size)

    def grads_other(offset, size, values):
        weights[pl.ds(2 * sib, 2), :, :, :, lanes(offset, size)] = values.astype(BF16).reshape(2, 4, 4, 16, size)

    def turned(values, t):
        turned_lhs[pl.ds(2 * t, 2)] = values.astype(BF16).reshape(2, 4, 4, 16, 512)

    for t in range(2):
        columns = slice(t * 512, (t + 1) * 512)
        turned(dot_tn(active[2 * sib], cots[:, :, columns].reshape(512, 512)), t)
    spare[...] = dot_tn(active[1], cot_half(sib)).astype(BF16).reshape(2, 4, 4, 16, 512)
    to_sibling = [
        send(source, view(grads, {"x": pl.ds(2 * c, 2)}, at, 512), view(grads, {"x": pl.ds(2 * sib, 2)}, at, 512), sibling)
        for source, at in (
            (turned_lhs.at[0:2], G_DN),
            (turned_lhs.at[2:4], G_DN + 512),
            (spare, G_DN + 1024),
        )
    ]
    for t in range(2):
        values = dot_tn(active[2 * c], cots[:, :, t * 512 : (t + 1) * 512].reshape(512, 512))
        grads_own(G_DN + t * 512, 512, values)
    grads_own(G_DN + 1024, 512, dot_tn(active[1], cot_half(c)))
    exchange("down")
    arrive(to_sibling)
    reduce(0)
    gathered(2)
    other_down = to_other(DN0, 1536, 1024)
    flush()
    turned_lhs[...] = all_mid().T.reshape(4, 4, 4, 16, 512)
    arrive([other_down])

    def left():
        return turned_lhs[...].reshape(1024, 512)

    def back_active(kind, q):
        if kind == 0:
            group = 2 * c
            values = dot_nt(all_cots(), weight_rows(2 * c + q, DN0, 1024))
        elif kind == 1:
            group = 2 * sib
            values = dot_nt(all_cots(), other_weights[q, :, :, :, 1024:2048].reshape(256, 1024))
        else:
            group = 1
            values = dot_nt(cot_half(c), weight_rows(2 * c + q, DN0 + 1024, 512)) + dot_nt(
                cot_half(sib), other_weights[q, :, :, :, 2048:2560].reshape(256, 512)
            )
        for h in range(2):
            column = q * 1536 + (3 * h + group) * 128
            pulled = values[:, h * 128 : (h + 1) * 128]
            gate = gate_up[:, lanes(column, 128)].astype(F32)
            up = gate_up[:, lanes(column + 768, 128)].astype(F32)
            sigma = jax.nn.sigmoid(gate)
            back_gate = pulled * up * sigma * (1.0 + gate * (1.0 - sigma))
            gate_up[:, lanes(column, 128)] = back_gate.astype(BF16)
            gate_up[:, lanes(column + 768, 128)] = (pulled * gate * sigma).astype(BF16)

    def back_part(values, fresh):
        if fresh:
            part[0], part[1] = values[:256], values[256:]
        else:
            part[0] += values[:256]
            part[1] += values[256:]

    def back_mid(half):
        for piece in range(2):
            column = half * 1536 + piece * 768
            values = dot_nt(gate_up[:, column : column + 768], weight(GU0 + column, 768))
            back_part(values, half == 0 and piece == 0)

    def gate_up_grads(half):
        for t in range(3):
            column = half * 1536 + t * 512
            values = dot(left(), gate_up[:, column : column + 512])
            weights[:, :, :, :, GU0 + column : GU0 + column + 512] = values.astype(BF16).reshape(4, 4, 4, 16, 512)

    for kind in range(3):
        back_active(kind, 0)
    exchange("active0")
    back_mid(0)
    gate_up_grads(0)
    reduce(1)
    exchange("gu0")
    for kind in range(3):
        back_active(kind, 1)
    exchange("active1")
    back_mid(1)
    exchange("mid1")
    across = send(part.at[sib], got_part, got_part, sibling)
    gate_up_grads(1)
    reduce(2)
    exchange("gu1")
    arrive([across])
    back = part[c] + got_part[...]
    unit_mid, scale_mid = unit_of(middle[...])
    gains_acc[1:2, :] = jnp.sum(back * unit_mid, axis=0, keepdims=True)
    back_middle = cots[c].astype(F32) + norm_back(back, gain_mid, unit_mid, scale_mid)
    branch[c] = back_middle.astype(BF16)
    across.sent()
    pending.remove(across)
    across_branch = send(branch.at[c], branch.at[c], branch.at[sib], sibling)
    cots[c] = (back_middle - branch[c].astype(F32)).astype(BF16)

    down_rows = lambda t: (
        dot(active[2 * c], weight_own(DN0 + t * 256, 256))
        + dot(active[2 * sib], weight_other(1024 + t * 256, 256))
    )
    for t in range(4):
        values = down_rows(t)
        two_parts(values, pl.ds(t * 256, 256))
    for half, load in ((c, lambda: weight_own(DN0 + 1024, 512)), (sib, lambda: weight_other(2048, 512))):
        values = dot(active[1], load())
        columns = lanes(half * 512, 512, 512)
        part[0, :, columns] += values[:256]
        part[1, :, columns] += values[256:]
    across_down = send(part.at[sib], got_down, got_down, sibling)
    middle[...] += part[c]
    exchange("output")
    arrive([across_branch])

    def all_branch():
        return branch[...].reshape(512, 1024)

    for t in range(2):
        columns = slice(t * 512, (t + 1) * 512)
        turned(dot_tn(mixed[sib], branch[:, :, columns].reshape(512, 512)), t)
    to_sibling = [
        send(
            turned_lhs.at[2 * t : 2 * t + 2],
            view(grads, {"x": pl.ds(2 * c, 2)}, G_OUT + t * 512, 512),
            view(grads, {"x": pl.ds(2 * sib, 2)}, G_OUT + t * 512, 512),
            sibling,
        )
        for t in range(2)
    ]
    for t in range(2):
        columns = slice(t * 512, (t + 1) * 512)
        grads_own(G_OUT + t * 512, 512, dot_tn(mixed[c], branch[:, :, columns].reshape(512, 512)))
    mixed_back = (
        dot_nt(all_branch(), weight_own(OUT0, 1024)).astype(BF16),
        dot_nt(all_branch(), weight_other(0, 1024)).astype(BF16),
    )
    for h, values in ((c, mixed_back[0]), (sib, mixed_back[1])):
        hidden_mid[h, :, 0:512] = values[:256]
        hidden_mid[h, :, 512:1024] = values[256:]
    arrive(to_sibling)
    reduce(3)
    exchange("mixed")
    gains_acc[2:3, :] = jnp.zeros((1, 1024), F32)

    def attend_back(step, carry):
        b, g = step // 4, step % 4
        rows, query, key, value = heads_of(b, g)
        column = lanes(b * 512 + g * 128, 128)
        pulled = jnp.concatenate([hidden_mid[h, :, column] for h in range(2)], axis=0)
        bias = mask_turned[b].astype(F32)
        scores = dot_nt(key, query) * (SCALE * LOG2E) + jnp.concatenate([bias, bias], axis=1)
        expo = jnp.exp2(scores)
        probs = expo * (1.0 / jnp.sum(expo, axis=0, keepdims=True))
        back_probs = dot_nt(value, pulled)
        inner = jnp.sum(probs * back_probs, axis=0, keepdims=True)
        back_scores = (probs * (back_probs - inner) * SCALE).astype(BF16)
        back_query = dot_tn(back_scores, key)
        back_key = dot(back_scores, query)
        back_value = dot(probs.astype(BF16), pulled)
        cosine = rope[b, :, 0:128]
        sine = rope[b, :, 128:256]

        def through(upstream, column, gain):
            values = raw[rows, lanes(column, 128)].astype(F32)
            scale = lax.rsqrt(head_mean(values * values) + EPS)
            unit = values * scale
            plain = upstream * cosine - pltpu.roll(upstream, 64, 1) * sine
            term = plain * unit
            pushed = plain * gain
            result = scale * (pushed - unit * head_mean(term * gain))
            gate_up[rows, lanes(column, 128)] = result.astype(BF16)
            return jnp.sum(term, axis=0, keepdims=True)

        for h in range(2):
            gains_acc[2:3, 0:128] += through(
                back_query[h * 256 : (h + 1) * 256], (2 * g + h) * 128, gain_query
            )
        gains_acc[2:3, 128:256] += through(back_key, 1024 + g * 128, gain_key)
        gate_up[rows, lanes(1536 + g * 128, 128)] = back_value.astype(BF16)
        return carry

    lax.fori_loop(0, 4, attend_back, 0, unroll=2)
    exchange("attend0")
    lax.fori_loop(4, 8, attend_back, 0, unroll=2)
    exchange("attend1")
    for transfer in to_sibling:
        transfer.sent()
        pending.remove(transfer)
    turned_lhs[...] = all_hidden().T.reshape(4, 4, 4, 16, 512)

    def qkv_grads(t, column):
        values = dot(left(), gate_up[:, t * 512 : (t + 1) * 512])
        weights[:, :, :, :, column : column + 512] = values.astype(BF16).reshape(4, 4, 4, 16, 512)

    for t in range(2):
        qkv_grads(t, OUT0 + t * 512)
    reduce(4)
    exchange("query")
    for t in range(2, 4):
        qkv_grads(t, DN0 + (t - 2) * 512)
    reduce(5)
    exchange("key")
    across_down.sent()
    pending.remove(across_down)

    for t in range(2):
        columns = slice(t * 1024, (t + 1) * 1024)
        back_part(dot_nt(gate_up[:, columns], weight(QKV0 + t * 1024, 1024)), t == 0)
    across = send(part.at[sib], got_part, got_part, sibling)
    across_down.arrived()
    hidden_mid[c] = (middle[...] + got_down[...]).astype(BF16)
    copy_out = pltpu.make_async_copy(hidden_mid.at[c], activations, local_sem.at[0])
    copy_out.start()
    exchange("in")
    arrive([across])
    back = part[c] + got_part[...]
    unit_in, scale_in = unit_of(toks[c].astype(F32))
    gains_acc[0:1, :] = jnp.sum(back * unit_in, axis=0, keepdims=True)
    back_middle = branch[c].astype(F32) + cots[c].astype(F32)
    hidden_mid[sib] = (back_middle + norm_back(back, gain_in, unit_in, scale_in)).astype(BF16)
    copy_in = pltpu.make_async_copy(hidden_mid.at[sib], input_grad, local_sem.at[1])
    copy_in.start()

    low = jnp.concatenate(
        [gains_acc[r : r + 1, i * 128 : (i + 1) * 128] for r in range(2) for i in range(8)], axis=0
    ).astype(BF16)
    high = jnp.concatenate(
        [gains_acc[2:3, 0:128], gains_acc[2:3, 128:256], jnp.zeros((14, 128), F32)], axis=0
    ).astype(BF16)
    gains_at = slice(DN0 + 1024, DN0 + 1152)
    weights[:, :, :, :, gains_at] = jnp.zeros((4, 4, 4, 16, 128), BF16)
    for part_x in range(4):
        for part_y in (0, 2):
            weights[part_x, part_y, 0, :, gains_at] = low
            weights[part_x, part_y, 1, :, gains_at] = high
    reduce(6)
    exchange("end")
    assert not any(stages)
    for unit in range(UNITS):
        arrive(sums[unit])
    copy_out.wait()
    copy_in.wait()
    flush()
    assert used[0] <= TRANSFERS and local_count[0] <= 48, used


TRANSFERS = 416


def run_layer(*operands):
    anywhere = pl.BlockSpec(memory_space=pl.ANY)
    vmem = pltpu.VMEM
    return pl.pallas_call(
        layer_kernel,
        out_shape=(
            jax.ShapeDtypeStruct((TOK, D), BF16),
            jax.ShapeDtypeStruct((TOK, D), BF16),
            jax.ShapeDtypeStruct((2, 2, 4, 16, S_COLS), BF16),
        ),
        in_specs=[anywhere] * 9,
        out_specs=(anywhere,) * 3,
        scratch_shapes=[
            vmem((4, 4, 4, 16, WCOLS), BF16),
            vmem((4, 4, 4, 16, G_COLS), BF16),
            vmem((2, 4, 4, 16, 2560), BF16),
            vmem((2, 2, 4, 16, WCOLS), BF16),
            vmem((2, 4, 4, 16, WCOLS), BF16),
            vmem((3, 4, 16, WCOLS), BF16),
            vmem((3, 16, WCOLS), BF16),
            vmem((2, TOK, D), BF16),
            vmem((2, TOK, D), BF16),
            vmem((2, TOK, 256), F32),
            vmem((2, TOK, TOK), BF16),
            vmem((2, TOK, TOK), BF16),
            vmem((2, TOK, D), BF16),
            vmem((2 * TOK, 1536), BF16),
            vmem((12, 2 * TOK, HD), BF16),
            vmem((4, 2 * TOK, HD), BF16),
            vmem((2, 2 * TOK, 512), BF16),
            vmem((2, TOK, D), F32),
            vmem((TOK, D), F32),
            vmem((TOK, D), F32),
            vmem((2, 1, TOK), jnp.int32),
            vmem((TOK, D), F32),
            vmem((2, TOK, D), BF16),
            vmem((2 * TOK, 3072), BF16),
            vmem((3, 2 * TOK, 512), BF16),
            vmem((2, TOK, D), BF16),
            vmem((4, 4, 4, 16, 2 * TOK), BF16),
            vmem((2, 4, 4, 16, 2 * TOK), BF16),
            vmem((8, D), F32),
            pltpu.SemaphoreType.DMA((48,)),
            pltpu.SemaphoreType.DMA((TRANSFERS,)),
            pltpu.SemaphoreType.DMA((TRANSFERS,)),
        ],
        compiler_params=pltpu.CompilerParams(
            collective_id=0, has_side_effects=True, vmem_limit_bytes=64 * 2**20
        ),
        cost_estimate=pl.CostEstimate(flops=26 * 10**9, bytes_accessed=10**7, transcendentals=10**6),
    )(*operands)


def adamw(master, first, second, gradient, rate, decay):
    first_new = 0.9 * first + 0.1 * gradient
    second_new = 0.999 * second + 0.001 * gradient * gradient
    direction = first_new / (1.0 - 0.9**STEP) / (jnp.sqrt(second_new / (1.0 - 0.999**STEP)) + 1e-08)
    return (master - rate * (direction + decay * master), first_new, second_new)


def step_places():
    qkv = [(0, c * 1024, c, S_QKV, 1024) for c in range(2)]
    qkv += [(0, 2048 + c * 512, c, S_QKV + 1024, 512) for c in range(2)]
    qkv += [(0, 3072 + c * 512, c, S_QKV + 1536, 512) for c in range(2)]
    out = [(c, 0, c, S_OUT, 1024) for c in range(2)]
    gate_up = [
        (0, up * 3072 + c * 1536 + half * 768, c, S_GU + half * 1536 + up * 768, 768)
        for up in range(2)
        for c in range(2)
        for half in range(2)
    ]
    down = [(0, 0, 0, S_DN, 1024), (2, 0, 1, S_DN, 1024)]
    down += [(1, c * 512, c, S_DN + 1024, 512) for c in range(2)]
    return qkv, out, gate_up, down


def step_kernel(*refs):
    states, summed, news = refs[:12], refs[12], refs[13:]
    for index, places in enumerate(step_places()):
        master, first, second = states[3 * index : 3 * index + 3]
        for group, column, core, at, size in places:
            here = (group, slice(None), pl.ds(column, size))
            results = adamw(
                master[here],
                first[here],
                second[here],
                summed[core, :, pl.ds(at, size)].astype(F32),
                0.05,
                0.1,
            )
            for ref, value in zip(news[3 * index : 3 * index + 3], results):
                ref[here] = value


def step(masters, firsts, seconds, summed):
    rows = 32
    arrays, specs, shapes = [], [], []
    for state in zip(masters, firsts, seconds):
        for array in state:
            groups = array.shape[0] // 128
            arrays.append(array.reshape(groups, 128, -1))
            specs.append(pl.BlockSpec((groups, rows, array.shape[1]), lambda i: (0, i, 0)))
            shapes.append(jax.ShapeDtypeStruct(arrays[-1].shape, F32))
    results = pl.pallas_call(
        step_kernel,
        grid=(128 // rows,),
        out_shape=tuple(shapes),
        in_specs=specs + [pl.BlockSpec((2, rows, S_COLS), lambda i: (0, i, 0))],
        out_specs=tuple(specs),
        compiler_params=pltpu.CompilerParams(vmem_limit_bytes=62 * 2**20),
        cost_estimate=pl.CostEstimate(flops=3 * 10**7, bytes_accessed=5 * 10**7, transcendentals=10**6),
    )(*arrays, summed)
    results = [value.reshape(-1, value.shape[2]) for value in results]
    return [tuple(results[3 * index : 3 * index + 3]) for index in range(4)]


def per_device(
    tokens,
    cotangent,
    segment_ids,
    positions,
    master_qkv,
    master_out,
    master_gate_up,
    master_down,
    master_gains,
    first_qkv,
    first_out,
    first_gate_up,
    first_down,
    first_gains,
    second_qkv,
    second_out,
    second_gate_up,
    second_down,
    second_gains,
):
    me = coordinates()
    shard = lax.axis_index("shard")
    order = jnp.minimum((me["y"] % 2) * 4 + me["z"], 2)
    gains = lax.dynamic_slice(
        jnp.pad(master_gains, (2048, 6144)), (2048 + 2048 * order - 288 * shard,), (2048,)
    ).reshape(16, 128)

    activations, input_grad, summed = run_layer(
        tokens,
        cotangent,
        segment_ids,
        positions,
        gains,
        master_qkv,
        master_out,
        master_gate_up,
        master_down,
    )
    summed = summed.reshape(2, 128, S_COLS)
    gain_rows = summed[:, :32, S_GAIN : S_GAIN + 128].astype(F32).sum(axis=0).reshape(-1)
    grad_gains = lax.dynamic_slice(gain_rows, (288 * shard,), (288,))
    updated = step(
        (master_qkv, master_out, master_gate_up, master_down),
        (first_qkv, first_out, first_gate_up, first_down),
        (second_qkv, second_out, second_gate_up, second_down),
        summed,
    )
    updated.append(adamw(master_gains, first_gains, second_gains, grad_gains, 0.4, 0.0))
    return (
        activations,
        input_grad,
        *(new[0] for new in updated),
        *(new[1] for new in updated),
        *(new[2] for new in updated),
    )


def solution(mesh):
    rows = P(("rep", "shard"), None)
    state = (P("shard", None),) * 4 + (P("shard"),)
    return jax.shard_map(
        per_device,
        mesh=mesh,
        in_specs=(rows,) * 4 + state * 3,
        out_specs=(rows,) * 2 + state * 3,
        check_vma=False,
    )
```

```python
import math

import jax
import jax.numpy as jnp
from jax import lax
from jax.experimental import pallas as pl
from jax.experimental.pallas import tpu as pltpu
from jax.sharding import PartitionSpec as P

D = 1024
HEADS = 16
KV_HEADS = 8
HD = 128
FF = 3072
STEP = 10
Q_WIDTH = 2048
KV_WIDTH = 1024
TOK = 256
F32 = jnp.float32
BF16 = jnp.bfloat16
EPS = 1e-06
SCALE = HD ** (-0.5)

QKV0, GAIN0, OUT0, GU0, DN0, WCOLS = 0, 2048, 2176, 3200, 6272, 7808
G_OUT, G_DN, G_COLS = 0, 1024, 2560
S_GU, S_QKV, S_GAIN, S_DN, S_OUT, S_COLS = 0, 3072, 5120, 5632, 7168, 8192
LOG2E = 1.4426950408889634
ROTATIONS = (("x", "y", "z"), ("y", "z", "x"), ("z", "x", "y"))

SCHEDULE = {
    "start": ("W0", "W1", "W2",),
    "early": ("W0", "W1", "W0", "W2", "W1", "W0", "W1", "W2", "W0", "W1", "W2",),
    "mid": ("W2",),
    "mid0": ("G0",),
    "branch": ("G0",),
    "output": ("G1", "G2",),
    "mixed": ("G0",),
    "attend1": ("G1",),
    "query": ("G2",),
    "key": ("G3", "G0",),
    "in0": ("G2", "G1", "G4",),
    "in": ("G5",),
    "end": tuple("G" + unit for unit in "0321465031265403216543214652346453"),
}
BY_NEIGHBOURS = (False, False, True, True, False, True, False)
WAYS = ("yz", "yz", "yz", "zy", "yz", "all", "all")


def dot(left, right):
    return jnp.dot(left, right, preferred_element_type=F32)


def dot_nt(left, right):
    return lax.dot_general(left, right, (((1,), (1,)), ((), ())), preferred_element_type=F32)


def dot_tn(left, right):
    return lax.dot_general(left, right, (((0,), (0,)), ((), ())), preferred_element_type=F32)


def lanes(start, size, step=128):
    return pl.ds(start if isinstance(start, int) else pl.multiple_of(start, step), size)


def steps_of(count, body, first=0):
    for index in range(first, count):
        body(index, 0)


def coordinates():
    rep = lax.axis_index("rep")
    shard = lax.axis_index("shard")
    return {
        "x": shard // 2,
        "y": (shard % 2) * 2 + (rep // 2) % 2,
        "z": rep // 4,
        "c": rep % 2,
    }


def device(at):
    return {"rep": at["z"] * 4 + (at["y"] % 2) * 2 + at["c"], "shard": at["x"] * 2 + at["y"] // 2}


def moved(me, axis, by):
    return {**me, axis: (me[axis] + by + 4) % 4}


def view(ref, select, offset, size):
    where = tuple(select.get(axis, slice(None)) for axis in "xyz")
    return ref.at[where + (slice(None), lanes(offset, size))]


def layer_kernel(
    tokens,
    cotangent,
    segments,
    positions,
    gains,
    master_qkv,
    master_out,
    master_gate_up,
    master_down,
    activations,
    input_grad,
    summed,
    weights,
    grads,
    other_weights,
    got_far,
    got_near,
    got_two,
    got_three,
    toks,
    cots,
    rope,
    mask,
    mask_turned,
    hidden,
    raw,
    rotated,
    vals,
    mixed,
    part,
    got_part,
    got_down,
    numbers,
    middle,
    hidden_mid,
    gate_up,
    active,
    branch,
    turned_lhs,
    spare,
    gains_acc,
    local_sem,
    send_sem,
    recv_sem,
):
    me = coordinates()
    c = me["c"]
    sib = 1 - c
    x, y, z = me["x"], me["y"], me["z"]
    sibling = device({**me, "c": sib})
    used = [0]

    class Transfer:
        def __init__(self, source, there, here, target):
            self.index = used[0]
            used[0] += 1
            self.source, self.there, self.here, self.target = source, there, here, target
            self.copy(source, there).start()

        def copy(self, source, there):
            return pltpu.make_async_remote_copy(
                src_ref=source,
                dst_ref=there,
                send_sem=send_sem.at[self.index],
                recv_sem=recv_sem.at[self.index],
                device_id=self.target,
                device_id_type=pl.DeviceIdType.MESH,
            )

        def arrived(self):
            self.copy(self.here, self.here).wait_recv()

        def sent(self):
            self.copy(self.source, self.there).wait_send()

    pending = []

    def send(source, there, here, target):
        transfer = Transfer(source, there, here, target)
        pending.append(transfer)
        return transfer

    def flush():
        while pending:
            pending.pop(0).sent()

    def arrive(transfers):
        for transfer in transfers:
            transfer.arrived()

    row = 16 * ((y % 2) * 4 + z)

    def rows_of(ref, first, offset, size):
        return ref.at[pl.ds(pl.multiple_of(first, 16), 16), lanes(offset, size)]

    groups = [
        (rows_of(master_qkv, row, c * 1024, 1024), QKV0, 1024),
        (rows_of(master_qkv, row, 2048 + c * 512, 512), QKV0 + 1024, 512),
        (rows_of(master_qkv, row, 3072 + c * 512, 512), QKV0 + 1536, 512),
        (rows_of(master_out, c * 128 + row, 0, 1024), OUT0, 1024),
        (rows_of(master_gate_up, row, c * 1536, 768), GU0, 768),
        (rows_of(master_gate_up, row, 3072 + c * 1536, 768), GU0 + 768, 768),
        (rows_of(master_gate_up, row, c * 1536 + 768, 768), GU0 + 1536, 768),
        (rows_of(master_gate_up, row, 3072 + c * 1536 + 768, 768), GU0 + 2304, 768),
        (rows_of(master_down, c * 256 + row, 0, 1024), DN0, 1024),
        (rows_of(master_down, 128 + row, c * 512, 512), DN0 + 1024, 512),
    ]
    inward = [
        (source, got_part.at[pl.ds(16 * index, 16), pl.ds(0, size)])
        for index, (source, offset, size) in enumerate(groups)
    ]
    inward += [(gains, got_part.at[pl.ds(160, 16), pl.ds(0, 128)])]
    first_inward = len(inward)
    inward += [
        (segments, numbers.at[0]),
        (positions, numbers.at[1]),
        (tokens, toks.at[c]),
        (cotangent, cots.at[c]),
    ]
    inward = [pltpu.make_async_copy(*pair, local_sem.at[index]) for index, pair in enumerate(inward)]

    barrier = pltpu.get_barrier_semaphore()
    across_y = {**me, "y": y + 1 - 2 * (y % 2)}
    friends = [sibling] + [device(moved(me, axis, by)) for axis in "xyz" for by in (1, 2, 3)]
    friends += [device(moved(across_y, "z", by)) for by in (1, 2, 3)]
    for friend in friends:
        pl.semaphore_signal(barrier, inc=1, device_id=friend, device_id_type=pl.DeviceIdType.MESH)
    for copy in inward:
        copy.start()
    for copy in inward[:first_inward]:
        copy.wait()
    for index, (source, offset, size) in enumerate(groups):
        rows16 = got_part[16 * index : 16 * index + 16, 0:size]
        weights[x, y, z, :, offset : offset + size] = rows16.astype(BF16)
    weights[x, y, z, :, GAIN0 : GAIN0 + 128] = got_part[160:176, 0:128].astype(BF16)
    pl.semaphore_wait(barrier, len(friends))

    def gather_one(rotation, offset, size):
        first, second, third = rotation
        source = view(weights, {"x": x, "y": y, "z": z}, offset, size)
        out = []
        for by in (1, 2, 3):
            here = view(weights, {**{"x": x, "y": y, "z": z}, third: (me[third] - by + 4) % 4}, offset, size)
            out.append(send(source, source, here, device(moved(me, third, by))))
        return out

    def gather_two(rotation, offset, size):
        first, second, third = rotation
        source = view(weights, {first: me[first], second: me[second]}, offset, size)
        out = []
        for by in (1, 3):
            here = view(weights, {first: me[first], second: (me[second] - by + 4) % 4}, offset, size)
            out.append(send(source, source, here, device(moved(me, second, by))))
        return out

    def gather_on(rotation, offset, size):
        first, second, third = rotation
        out = []
        for by, half in ((1, 0), (3, 1)):
            spot = {first: me[first], third: pl.ds(2 * half, 2)}
            source = view(weights, {**spot, second: (me[second] - by + 4) % 4}, offset, size)
            here = view(weights, {**spot, second: (me[second] + 2) % 4}, offset, size)
            out.append(send(source, source, here, device(moved(me, second, by))))
        return out

    def gather_three(rotation, offset, size):
        first = rotation[0]
        source = view(weights, {first: me[first]}, offset, size)
        out = []
        for by in (1, 3):
            here = view(weights, {first: (me[first] - by + 4) % 4}, offset, size)
            out.append(send(source, source, here, device(moved(me, first, by))))
        return out

    def gather_four(rotation, offset, size):
        first, second = rotation[0], rotation[1]
        out = []
        for by, half in ((1, 0), (3, 1)):
            rows = pl.ds(2 * half, 2)
            source = view(weights, {first: (me[first] - by + 4) % 4, second: rows}, offset, size)
            here = view(weights, {first: (me[first] + 2) % 4, second: rows}, offset, size)
            out.append(send(source, source, here, device(moved(me, first, by))))
        return out

    chunks = (
        ((0, 1152), (1152, 1024), (OUT0, 1024)),
        ((GU0, 1024), (GU0 + 1024, 1024), (GU0 + 2048, 1024)),
        ((DN0, 512), (DN0 + 512, 512), (DN0 + 1024, 512)),
    )
    steps = (gather_one, gather_two, gather_on, gather_three, gather_four)
    flying = [[None] * 3 for _ in chunks]

    w_step = [0] * len(chunks)

    def pump(chunk):
        step = w_step[chunk]
        w_step[chunk] += 1
        for index, rotation in enumerate(ROTATIONS):
            if step:
                arrive(flying[chunk][index])
            if step < len(steps):
                flying[chunk][index] = steps[step](rotation, *chunks[chunk][index])

    def gathered(chunk):
        while w_step[chunk] <= len(steps):
            pump(chunk)

    def exchange(name):
        for item in SCHEDULE.get(name, ()):
            (pump if item[0] == "W" else reduce)(int(item[1]))

    exchange("start")
    for copy in inward[first_inward:]:
        copy.wait()
    order = lax.broadcasted_iota(jnp.int32, (64, 256), 0).astype(F32)
    angle = jnp.exp(order * (-2.0 * math.log(1000000.0) / HD)) * numbers[1].astype(F32)
    cosine = jnp.cos(angle)
    sine = jnp.sin(angle)
    rope[c, :, 0:128] = jnp.concatenate([cosine, cosine], axis=0).T
    rope[c, :, 128:256] = jnp.concatenate([-sine, sine], axis=0).T
    across_segments = jnp.broadcast_to(numbers[0].astype(F32), (256, 256))
    same = across_segments == across_segments.T
    earlier = lax.broadcasted_iota(jnp.int32, (256, 256), 1) <= lax.broadcasted_iota(
        jnp.int32, (256, 256), 0
    )
    mask[c] = jnp.where(same & earlier, 0.0, -1e30).astype(BF16)
    early = [
        send(toks.at[c], toks.at[c], toks.at[sib], sibling),
        send(rope.at[c], rope.at[c], rope.at[sib], sibling),
        send(mask.at[c], mask.at[c], mask.at[sib], sibling),
        send(cots.at[c], cots.at[c], cots.at[sib], sibling),
    ]
    exchange("early")
    arrive(early)
    for b in range(2):
        mask_turned[b] = mask[b].astype(F32).T.astype(BF16)
    exchange("late")
    gathered(0)

    def to_other(offset, size, at):
        return send(
            view(weights, {"x": pl.ds(2 * sib, 2)}, offset, size),
            view(other_weights, {}, at, size),
            view(other_weights, {}, at, size),
            sibling,
        )

    other_out = to_other(OUT0, 1024, 0)

    def weight(offset, size):
        return weights[:, :, :, :, lanes(offset, size)].reshape(1024, size)

    def weight_rows(row, offset, size):
        return weights[row, :, :, :, lanes(offset, size)].reshape(256, size)

    def weight_own(offset, size):
        return weights[pl.ds(2 * c, 2), :, :, :, lanes(offset, size)].reshape(512, size)

    def weight_other(offset, size):
        return other_weights[:, :, :, :, lanes(offset, size)].reshape(512, size)

    gain_rows = jnp.zeros((16, 128), F32)
    head_rows = jnp.zeros((16, 128), F32)
    for part_x in range(4):
        for part_y in (0, 2):
            gain_rows += weights[part_x, part_y, 0, :, pl.ds(GAIN0, 128)].astype(F32)
            head_rows += weights[part_x, part_y, 1, :, pl.ds(GAIN0, 128)].astype(F32)
    gain_in = jnp.concatenate([gain_rows[i : i + 1] for i in range(8)], axis=1)
    gain_mid = jnp.concatenate([gain_rows[i : i + 1] for i in range(8, 16)], axis=1)
    gain_query = head_rows[0:1]
    gain_key = head_rows[1:2]

    def unit_of(values):
        scale = lax.rsqrt(jnp.mean(values * values, axis=-1, keepdims=True) + EPS)
        return values * scale, scale

    def norm_back(upstream, gain, unit, scale):
        pushed = upstream * gain
        inner = jnp.mean(pushed * unit, axis=-1, keepdims=True)
        return scale * (pushed - unit * inner)

    for b in range(2):
        unit, _ = unit_of(toks[b].astype(F32))
        hidden[b] = (unit * gain_in).astype(BF16)

    def all_hidden():
        return hidden[...].reshape(512, 1024)

    mean_of = jnp.full((128, 128), 1.0 / 128, BF16)

    def head_mean(values):
        return dot(values.astype(BF16), mean_of)

    def project_heads(t, carry):
        values = dot(all_hidden(), weight(QKV0 + t * 256, 256))
        raw[:, lanes(t * 256, 256)] = values.astype(BF16)
        gain = gain_query if t < 4 else gain_key
        cosine = rope[:, :, 0:128].reshape(512, 128)
        sine = rope[:, :, 128:256].reshape(512, 128)
        for h in range(2):
            head = values[:, h * 128 : (h + 1) * 128]
            normal = head * lax.rsqrt(head_mean(head * head) + EPS) * gain
            rotated[2 * t + h] = (normal * cosine + pltpu.roll(normal, 64, 1) * sine).astype(BF16)
        return carry

    steps_of(6, project_heads)

    def project_values(t, carry):
        values = dot(all_hidden(), weight(QKV0 + 1536 + t * 256, 256)).astype(BF16)
        vals[2 * t] = values[:, :128]
        vals[2 * t + 1] = values[:, 128:]
        return carry

    steps_of(2, project_values)
    exchange("project")

    def heads_of(b, g):
        rows = pl.ds(pl.multiple_of(b * 256, 256), 256)
        query = rotated[pl.ds(2 * g, 2), rows, :].reshape(512, 128)
        return rows, query, rotated[8 + g, rows, :], vals[g, rows, :]

    def attend(step, carry):
        b, g = step // 4, step % 4
        rows, query, key, value = heads_of(b, g)
        scores = dot_nt(query, key).reshape(2, 256, 256) * (SCALE * LOG2E) + mask[b].astype(F32)[None]
        expo = jnp.exp2(scores).reshape(512, 256).astype(BF16)
        result = dot(expo, jnp.concatenate([value, jnp.ones((256, 128), BF16)], axis=1))
        result = (result[:, :128] / result[:, 128:]).astype(BF16)
        for h in range(2):
            mixed[h, rows, lanes(g * 128, 128)] = result[h * 256 : (h + 1) * 256]
        return carry

    lax.fori_loop(0, 8, attend, 0, unroll=4)

    exchange("attend")
    arrive([other_out])

    def two_parts(values, columns):
        part[0, :, columns] = values[:256]
        part[1, :, columns] = values[256:]

    def project_out(t, carry):
        values = dot(mixed[c], weight_own(OUT0 + t * 512, 512)) + dot(
            mixed[sib], weight_other(t * 512, 512)
        )
        two_parts(values, lanes(t * 512, 512))
        return carry

    steps_of(2, project_out)
    exchange("projected")
    across = send(part.at[sib], got_part, got_part, sibling)
    across.arrived()
    middle[...] = toks[c].astype(F32) + part[c] + got_part[...]
    unit_mid, _ = unit_of(middle[...])
    hidden_mid[c] = (unit_mid * gain_mid).astype(BF16)
    across_mid = send(hidden_mid.at[c], hidden_mid.at[c], hidden_mid.at[sib], sibling)
    across.sent()
    pending.remove(across)
    exchange("mid")
    gathered(1)
    arrive([across_mid])

    def all_mid():
        return hidden_mid[...].reshape(512, 1024)

    def feed_forward(t, carry):
        column = (t // 3) * 1536 + (t % 3) * 256
        gate = dot(all_mid(), weight(GU0 + column, 256))
        up = dot(all_mid(), weight(GU0 + column + 768, 256))
        gate_up[:, lanes(column, 256)] = gate.astype(BF16)
        gate_up[:, lanes(column + 768, 256)] = up.astype(BF16)
        result = (gate * jax.nn.sigmoid(gate) * up).astype(BF16)
        for h in range(2):
            block = 2 * t + h
            active[block % 3, :, lanes((block // 3) * 128, 128)] = result[:, h * 128 : (h + 1) * 128]
        return carry

    steps_of(3, feed_forward)
    exchange("feed0")
    steps_of(6, feed_forward, 3)
    exchange("feed1")

    def unit_of_parts(ref, offset, sizes, column):
        parts = []
        for size in sizes:
            parts.append((ref, offset, size, column))
            offset, column = offset + size, column + size
        return parts

    plans = (
        unit_of_parts(grads, G_DN, (512, 512, 512), S_DN),
        unit_of_parts(weights, GU0, (512, 512, 512), S_GU),
        unit_of_parts(weights, GU0 + 1536, (512, 512, 512), S_GU + 1536),
        unit_of_parts(grads, G_OUT, (512, 256, 256), S_OUT),
        unit_of_parts(weights, OUT0, (256, 384, 384), S_QKV),
        unit_of_parts(weights, DN0, (256, 384, 384), S_QKV + 1024),
        unit_of_parts(weights, DN0 + 1024, (128,), S_GAIN),
    )
    UNITS = len(plans)
    landing, at = {}, 0
    for unit in range(UNITS):
        for index in range(len(plans[unit])):
            landing[unit, index] = at
            at += plans[unit][index][2]

    def remaining(rotation):
        return [axis for axis in "xyz" if axis != rotation[0]]

    def add_blocks(blocks, target, size, shape):
        count = math.prod(shape)

        def body(k, carry):
            where = []
            left = k
            for extent in reversed(shape):
                where.insert(0, left % extent)
                left = left // extent
            total = blocks[0](where)
            for block in blocks[1:]:
                total = total + block(where)
            target(where, total.astype(BF16))
            return carry

        if count == 1:
            body(0, 0)
        else:
            lax.fori_loop(0, count, body, 0)

    def reader(ref, offset, size, locate):
        return lambda where: ref[locate(where) + (slice(None), lanes(offset, size))].astype(F32)

    def writer(ref, offset, size, locate):
        def store(where, value):
            ref[locate(where) + (slice(None), lanes(offset, size))] = value

        return store

    sums = {}

    def reduce_one(unit, index):
        ref, offset, size, to = plans[unit][index]
        rotation = ROTATIONS[index]
        first, other = rotation[0], remaining(rotation)[0]
        at = landing[unit, index]
        sums[unit, index, 1] = [
            send(
                view(ref, {first: (me[first] + 2) % 4, other: pl.ds(2 * half, 2)}, offset, size),
                got_far.at[half, :, :, :, lanes(at, size)],
                got_far.at[half, :, :, :, lanes(at, size)],
                device(moved(me, first, by)),
            )
            for by, half in ((1, 0), (3, 1))
        ]

    def reduce_two(unit, index):
        ref, offset, size, to = plans[unit][index]
        rotation = ROTATIONS[index]
        first, (other, last) = rotation[0], remaining(rotation)
        at = landing[unit, index]
        arrive(sums[unit, index, 1])
        out = []
        for by, half in ((1, 0), (3, 1)):
            block = (me[first] + by) % 4

            def locate(where, block=block, half=half):
                spot = {first: block, other: where[0] + 2 * half, last: where[1]}
                return tuple(spot[axis] for axis in "xyz")

            add_blocks(
                [
                    reader(ref, offset, size, locate),
                    reader(got_far, at, size, lambda where, half=half: (half, where[0], where[1])),
                ],
                writer(ref, offset, size, locate),
                size,
                (2, 4),
            )
            out.append(
                send(
                    view(ref, {first: block}, offset, size),
                    got_near.at[half, :, :, :, lanes(at, size)],
                    got_near.at[half, :, :, :, lanes(at, size)],
                    device(moved(me, first, by)),
                )
            )
        sums[unit, index, 2] = out

    def reduce_three(unit, index):
        ref, offset, size, to = plans[unit][index]
        rotation = ROTATIONS[index]
        first, second, third = rotation
        other, last = remaining(rotation)
        at = landing[unit, index]
        arrive(sums[unit, index, 2])

        def locate(where):
            spot = {first: me[first], other: where[0], last: where[1]}
            return tuple(spot[axis] for axis in "xyz")

        add_blocks(
            [reader(ref, offset, size, locate)]
            + [
                reader(got_near, at, size, lambda where, half=half: (half, where[0], where[1]))
                for half in range(2)
            ],
            writer(ref, offset, size, locate),
            size,
            (4, 4),
        )
        if not BY_NEIGHBOURS[unit]:
            sums[unit, index, 3] = [
                send(
                    view(ref, {first: me[first], second: (me[second] + by) % 4}, offset, size),
                    got_two.at[by - 1, :, :, lanes(at, size)],
                    got_two.at[by - 1, :, :, lanes(at, size)],
                    device(moved(me, second, by)),
                )
                for by in (1, 2, 3)
            ]
            return
        sums[unit, index, 3] = [
            send(
                view(
                    ref,
                    {first: me[first], second: (me[second] + 2) % 4, third: pl.ds(2 * half, 2)},
                    offset,
                    size,
                ),
                got_two.at[2, 2 * half : 2 * half + 2, :, lanes(at, size)],
                got_two.at[2, 2 * half : 2 * half + 2, :, lanes(at, size)],
                device(moved(me, second, by)),
            )
            for by, half in ((1, 0), (3, 1))
        ]

    def reduce_on(unit, index):
        ref, offset, size, to = plans[unit][index]
        first, second, third = ROTATIONS[index]
        at = landing[unit, index]
        arrive(sums[unit, index, 3])
        out = []
        for by, half in ((1, 0), (3, 1)):
            block = (me[second] + by) % 4

            def locate(where, block=block, half=half):
                spot = {first: me[first], second: block, third: where[0] + 2 * half}
                return tuple(spot[axis] for axis in "xyz")

            add_blocks(
                [
                    reader(ref, offset, size, locate),
                    reader(got_two, at, size, lambda where, half=half: (2, where[0] + 2 * half)),
                ],
                writer(ref, offset, size, locate),
                size,
                (2,),
            )
            out.append(
                send(
                    view(ref, {first: me[first], second: block}, offset, size),
                    got_two.at[half, :, :, lanes(at, size)],
                    got_two.at[half, :, :, lanes(at, size)],
                    device(moved(me, second, by)),
                )
            )
        sums[unit, index, 3] = out

    def reduce_four(unit, index):
        ref, offset, size, to = plans[unit][index]
        first, second, third = ROTATIONS[index]
        at = landing[unit, index]
        arrive(sums[unit, index, 3])

        def locate(where):
            spot = {first: me[first], second: me[second], third: where[0]}
            return tuple(spot[axis] for axis in "xyz")

        add_blocks(
            [reader(ref, offset, size, locate)]
            + [
                reader(got_two, at, size, lambda where, by=by: (by, where[0]))
                for by in range(2 if BY_NEIGHBOURS[unit] else 3)
            ],
            writer(ref, offset, size, locate),
            size,
            (4,),
        )
        sums[unit, index, 4] = [
            send(
                view(ref, {first: me[first], second: me[second], third: (me[third] + by) % 4}, offset, size),
                got_three.at[by - 1, :, lanes(at, size)],
                got_three.at[by - 1, :, lanes(at, size)],
                device(moved(me, third, by)),
            )
            for by in (1, 2, 3)
        ]

    y_low = y % 2
    local_count = [len(inward)]
    local_pending = {}

    def whole(unit):
        ref, offset, _, to = plans[unit][0]
        size = sum(part[2] for part in plans[unit])
        return ref.at[x, y, z, :, lanes(offset, size)], lanes(to, size)

    def along_z(unit, source, there, here, steps=(1, 2, 3)):
        sums[unit] = [
            send(source, there, here((z - by + 4) % 4), device(moved(me, "z", by))) for by in steps
        ]

    def landed(unit):
        arrive(sums[unit])
        if unit in local_pending:
            local_pending.pop(unit).wait()
        return whole(unit)[1]

    def reduce_five(unit):
        for index in range(len(plans[unit])):
            ref, offset, size, to = plans[unit][index]
            at = landing[unit, index]
            arrive(sums[unit, index, 4])
            here = (x, y, z)
            add_blocks(
                [reader(ref, offset, size, lambda where: here)]
                + [reader(got_three, at, size, lambda where, by=by: (by,)) for by in range(3)],
                writer(ref, offset, size, lambda where: here),
                size,
                (1,),
            )
        source, column = whole(unit)
        there = summed.at[c, y_low, z, :, column]
        local_pending[unit] = pltpu.make_async_copy(source, there, local_sem.at[local_count[0]])
        local_count[0] += 1
        local_pending[unit].start()
        way = WAYS[unit]
        if way in ("zy", "all"):
            along_z(unit, source, there, lambda at_z: summed.at[c, y_low, at_z, :, column])
        if way in ("yz", "yzd"):
            sums[unit] = [send(source, there, summed.at[c, 1 - y_low, z, :, column], device(across_y))]
        if way == "all":
            sums[unit] += [
                send(
                    source,
                    there,
                    summed.at[c, 1 - y_low, (z - by + 4) % 4, :, column],
                    device(moved(across_y, "z", by)),
                )
                for by in range(4)
            ]

    def spread_y(unit):
        column = landed(unit)
        source = summed.at[c, y_low, :, :, column]
        sums[unit] = [send(source, source, summed.at[c, 1 - y_low, :, :, column], device(across_y))]

    def spread_z(unit):
        column = landed(unit)
        source = summed.at[c, :, z, :, column]
        steps = (1, 2, 3) if WAYS[unit] == "yzd" else (1, 3)
        along_z(unit, source, source, lambda at_z: summed.at[c, :, at_z, :, column], steps)

    def spread_on(unit):
        column = landed(unit)
        out = []
        for by, half in ((1, 0), (3, 1)):
            source = summed.at[c, half, (z - by + 4) % 4, :, column]
            here = summed.at[c, half, (z + 2) % 4, :, column]
            out.append(send(source, source, here, device(moved(me, "z", by))))
        sums[unit] = out

    def spread_core(unit):
        column = landed(unit)
        source = summed.at[c, :, :, :, column]
        sums[unit] = [send(source, source, summed.at[sib, :, :, :, column], sibling)]

    spreads = {
        "yz": (spread_z, spread_on, spread_core),
        "yzd": (spread_z, spread_core),
        "zy": (spread_y, spread_core),
        "all": (spread_core,),
    }

    def stages_of(unit):
        sums_by_part = [reduce_one, reduce_two, reduce_three, reduce_four]
        if BY_NEIGHBOURS[unit]:
            sums_by_part.insert(3, reduce_on)

        def for_parts(stage):
            def run(unit):
                for index in range(len(plans[unit])):
                    stage(unit, index)

            return run

        return [for_parts(stage) for stage in sums_by_part] + [reduce_five, *spreads[WAYS[unit]]]

    stages = [stages_of(unit) for unit in range(UNITS)]

    def reduce(unit):
        stages[unit].pop(0)(unit)

    def all_cots():
        return cots[...].reshape(512, 1024)

    def cot_half(half):
        return cots[:, :, lanes(half * 512, 512, 512)].reshape(512, 512)

    def grads_own(offset, size, values):
        grads[pl.ds(2 * c, 2), :, :, :, lanes(offset, size)] = values.astype(BF16).reshape(2, 4, 4, 16, size)

    def grads_other(offset, size, values):
        weights[pl.ds(2 * sib, 2), :, :, :, lanes(offset, size)] = values.astype(BF16).reshape(2, 4, 4, 16, size)

    def turned(values, t):
        turned_lhs[pl.ds(2 * t, 2)] = values.astype(BF16).reshape(2, 4, 4, 16, 512)

    for t in range(2):
        columns = slice(t * 512, (t + 1) * 512)
        turned(dot_tn(active[2 * sib], cots[:, :, columns].reshape(512, 512)), t)
    spare[...] = dot_tn(active[1], cot_half(sib)).astype(BF16).reshape(2, 4, 4, 16, 512)
    to_sibling = [
        send(source, view(grads, {"x": pl.ds(2 * c, 2)}, at, 512), view(grads, {"x": pl.ds(2 * sib, 2)}, at, 512), sibling)
        for source, at in (
            (turned_lhs.at[0:2], G_DN),
            (turned_lhs.at[2:4], G_DN + 512),
            (spare, G_DN + 1024),
        )
    ]
    for t in range(2):
        values = dot_tn(active[2 * c], cots[:, :, t * 512 : (t + 1) * 512].reshape(512, 512))
        grads_own(G_DN + t * 512, 512, values)
    grads_own(G_DN + 1024, 512, dot_tn(active[1], cot_half(c)))
    exchange("down")
    arrive(to_sibling)
    reduce(0)
    gathered(2)
    other_down = to_other(DN0, 1536, 1024)
    flush()
    turned_lhs[...] = all_mid().T.reshape(4, 4, 4, 16, 512)
    arrive([other_down])
    exchange("x")

    def left():
        return turned_lhs[...].reshape(1024, 512)

    def back_active(kind, q):
        if kind == 0:
            group = 2 * c
            values = dot_nt(all_cots(), weight_rows(2 * c + q, DN0, 1024))
        elif kind == 1:
            group = 2 * sib
            values = dot_nt(all_cots(), other_weights[q, :, :, :, 1024:2048].reshape(256, 1024))
        else:
            group = 1
            values = dot_nt(cot_half(c), weight_rows(2 * c + q, DN0 + 1024, 512)) + dot_nt(
                cot_half(sib), other_weights[q, :, :, :, 2048:2560].reshape(256, 512)
            )
        for h in range(2):
            column = q * 1536 + (3 * h + group) * 128
            pulled = values[:, h * 128 : (h + 1) * 128]
            gate = gate_up[:, lanes(column, 128)].astype(F32)
            up = gate_up[:, lanes(column + 768, 128)].astype(F32)
            sigma = jax.nn.sigmoid(gate)
            back_gate = pulled * up * sigma * (1.0 + gate * (1.0 - sigma))
            gate_up[:, lanes(column, 128)] = back_gate.astype(BF16)
            gate_up[:, lanes(column + 768, 128)] = (pulled * gate * sigma).astype(BF16)

    def back_part(values, fresh):
        if fresh:
            part[0], part[1] = values[:256], values[256:]
        else:
            part[0] += values[:256]
            part[1] += values[256:]

    def back_mid(half):
        for piece in range(2):
            column = half * 1536 + piece * 768
            values = dot_nt(gate_up[:, column : column + 768], weight(GU0 + column, 768))
            back_part(values, half == 0 and piece == 0)

    def gate_up_grads(half):
        for t in range(3):
            column = half * 1536 + t * 512
            values = dot(left(), gate_up[:, column : column + 512])
            weights[:, :, :, :, GU0 + column : GU0 + column + 512] = values.astype(BF16).reshape(4, 4, 4, 16, 512)

    for kind in range(3):
        back_active(kind, 0)
    exchange("active0")
    back_mid(0)
    exchange("mid0")
    gate_up_grads(0)
    reduce(1)
    exchange("gu0")
    for kind in range(3):
        back_active(kind, 1)
    exchange("active1")
    back_mid(1)
    exchange("mid1")
    across = send(part.at[sib], got_part, got_part, sibling)
    gate_up_grads(1)
    reduce(2)
    exchange("gu1")
    arrive([across])
    back = part[c] + got_part[...]
    unit_mid, scale_mid = unit_of(middle[...])
    gains_acc[1:2, :] = jnp.sum(back * unit_mid, axis=0, keepdims=True)
    back_middle = cots[c].astype(F32) + norm_back(back, gain_mid, unit_mid, scale_mid)
    branch[c] = back_middle.astype(BF16)
    across.sent()
    pending.remove(across)
    across_branch = send(branch.at[c], branch.at[c], branch.at[sib], sibling)
    exchange("branch")
    cots[c] = (back_middle - branch[c].astype(F32)).astype(BF16)

    down_rows = lambda t: (
        dot(active[2 * c], weight_own(DN0 + t * 256, 256))
        + dot(active[2 * sib], weight_other(1024 + t * 256, 256))
    )
    for t in range(4):
        values = down_rows(t)
        two_parts(values, pl.ds(t * 256, 256))
    for half, load in ((c, lambda: weight_own(DN0 + 1024, 512)), (sib, lambda: weight_other(2048, 512))):
        values = dot(active[1], load())
        columns = lanes(half * 512, 512, 512)
        part[0, :, columns] += values[:256]
        part[1, :, columns] += values[256:]
    across_down = send(part.at[sib], got_down, got_down, sibling)
    middle[...] += part[c]
    exchange("output")
    arrive([across_branch])

    def all_branch():
        return branch[...].reshape(512, 1024)

    for t in range(2):
        columns = slice(t * 512, (t + 1) * 512)
        turned(dot_tn(mixed[sib], branch[:, :, columns].reshape(512, 512)), t)
    to_sibling = [
        send(
            turned_lhs.at[2 * t : 2 * t + 2],
            view(grads, {"x": pl.ds(2 * c, 2)}, G_OUT + t * 512, 512),
            view(grads, {"x": pl.ds(2 * sib, 2)}, G_OUT + t * 512, 512),
            sibling,
        )
        for t in range(2)
    ]
    for t in range(2):
        columns = slice(t * 512, (t + 1) * 512)
        grads_own(G_OUT + t * 512, 512, dot_tn(mixed[c], branch[:, :, columns].reshape(512, 512)))
    exchange("outs")
    mixed_back = (
        dot_nt(all_branch(), weight_own(OUT0, 1024)).astype(BF16),
        dot_nt(all_branch(), weight_other(0, 1024)).astype(BF16),
    )
    for h, values in ((c, mixed_back[0]), (sib, mixed_back[1])):
        hidden_mid[h, :, 0:512] = values[:256]
        hidden_mid[h, :, 512:1024] = values[256:]
    arrive(to_sibling)
    reduce(3)
    exchange("mixed")
    gains_acc[2:3, :] = jnp.zeros((1, 1024), F32)

    def attend_back(step, carry):
        b, g = step // 4, step % 4
        rows, query, key, value = heads_of(b, g)
        column = lanes(b * 512 + g * 128, 128)
        pulled = jnp.concatenate([hidden_mid[h, :, column] for h in range(2)], axis=0)
        bias = mask_turned[b].astype(F32)
        scores = dot_nt(key, query) * (SCALE * LOG2E) + jnp.concatenate([bias, bias], axis=1)
        expo = jnp.exp2(scores)
        probs = expo * (1.0 / jnp.sum(expo, axis=0, keepdims=True))
        back_probs = dot_nt(value, pulled)
        inner = jnp.sum(probs * back_probs, axis=0, keepdims=True)
        back_scores = (probs * (back_probs - inner) * SCALE).astype(BF16)
        back_query = dot_tn(back_scores, key)
        back_key = dot(back_scores, query)
        back_value = dot(probs.astype(BF16), pulled)
        cosine = rope[b, :, 0:128]
        sine = rope[b, :, 128:256]

        def through(upstream, column, gain):
            values = raw[rows, lanes(column, 128)].astype(F32)
            scale = lax.rsqrt(head_mean(values * values) + EPS)
            unit = values * scale
            plain = upstream * cosine - pltpu.roll(upstream, 64, 1) * sine
            term = plain * unit
            pushed = plain * gain
            result = scale * (pushed - unit * head_mean(term * gain))
            gate_up[rows, lanes(column, 128)] = result.astype(BF16)
            return jnp.sum(term, axis=0, keepdims=True)

        for h in range(2):
            gains_acc[2:3, 0:128] += through(
                back_query[h * 256 : (h + 1) * 256], (2 * g + h) * 128, gain_query
            )
        gains_acc[2:3, 128:256] += through(back_key, 1024 + g * 128, gain_key)
        gate_up[rows, lanes(1536 + g * 128, 128)] = back_value.astype(BF16)
        return carry

    for quarter in range(4):
        lax.fori_loop(2 * quarter, 2 * quarter + 2, attend_back, 0, unroll=True)
        exchange("attend%d" % quarter)
    for transfer in to_sibling:
        transfer.sent()
        pending.remove(transfer)
    turned_lhs[...] = all_hidden().T.reshape(4, 4, 4, 16, 512)

    def qkv_grads(t, column):
        values = dot(left(), gate_up[:, t * 512 : (t + 1) * 512])
        weights[:, :, :, :, column : column + 512] = values.astype(BF16).reshape(4, 4, 4, 16, 512)

    for t in range(2):
        qkv_grads(t, OUT0 + t * 512)
    reduce(4)
    exchange("query")
    for t in range(2, 4):
        qkv_grads(t, DN0 + (t - 2) * 512)
    reduce(5)
    exchange("key")
    across_down.sent()
    pending.remove(across_down)

    for t in range(2):
        columns = slice(t * 1024, (t + 1) * 1024)
        back_part(dot_nt(gate_up[:, columns], weight(QKV0 + t * 1024, 1024)), t == 0)
        if t == 0:
            exchange("in0")
    across = send(part.at[sib], got_part, got_part, sibling)
    across_down.arrived()
    hidden_mid[c] = (middle[...] + got_down[...]).astype(BF16)
    copy_out = pltpu.make_async_copy(hidden_mid.at[c], activations, local_sem.at[0])
    copy_out.start()
    exchange("in")
    arrive([across])
    back = part[c] + got_part[...]
    unit_in, scale_in = unit_of(toks[c].astype(F32))
    gains_acc[0:1, :] = jnp.sum(back * unit_in, axis=0, keepdims=True)
    back_middle = branch[c].astype(F32) + cots[c].astype(F32)
    hidden_mid[sib] = (back_middle + norm_back(back, gain_in, unit_in, scale_in)).astype(BF16)
    copy_in = pltpu.make_async_copy(hidden_mid.at[sib], input_grad, local_sem.at[1])
    copy_in.start()

    low = jnp.concatenate(
        [gains_acc[r : r + 1, i * 128 : (i + 1) * 128] for r in range(2) for i in range(8)], axis=0
    ).astype(BF16)
    high = jnp.concatenate(
        [gains_acc[2:3, 0:128], gains_acc[2:3, 128:256], jnp.zeros((14, 128), F32)], axis=0
    ).astype(BF16)
    gains_at = slice(DN0 + 1024, DN0 + 1152)
    weights[:, :, :, :, gains_at] = jnp.zeros((4, 4, 4, 16, 128), BF16)
    for part_x in range(4):
        for part_y in (0, 2):
            weights[part_x, part_y, 0, :, gains_at] = low
            weights[part_x, part_y, 1, :, gains_at] = high
    reduce(6)
    exchange("end")
    assert not any(stages)
    for unit in range(UNITS):
        arrive(sums[unit])
    copy_out.wait()
    copy_in.wait()
    flush()
    assert used[0] <= TRANSFERS and local_count[0] <= 48, used


TRANSFERS = 416


def run_layer(*operands):
    anywhere = pl.BlockSpec(memory_space=pl.ANY)
    vmem = pltpu.VMEM
    return pl.pallas_call(
        layer_kernel,
        out_shape=(
            jax.ShapeDtypeStruct((TOK, D), BF16),
            jax.ShapeDtypeStruct((TOK, D), BF16),
            jax.ShapeDtypeStruct((2, 2, 4, 16, S_COLS), BF16),
        ),
        in_specs=[anywhere] * 9,
        out_specs=(anywhere,) * 3,
        scratch_shapes=[
            vmem((4, 4, 4, 16, WCOLS), BF16),
            vmem((4, 4, 4, 16, G_COLS), BF16),
            vmem((2, 4, 4, 16, 2560), BF16),
            vmem((2, 2, 4, 16, WCOLS), BF16),
            vmem((2, 4, 4, 16, WCOLS), BF16),
            vmem((3, 4, 16, WCOLS), BF16),
            vmem((3, 16, WCOLS), BF16),
            vmem((2, TOK, D), BF16),
            vmem((2, TOK, D), BF16),
            vmem((2, TOK, 256), F32),
            vmem((2, TOK, TOK), BF16),
            vmem((2, TOK, TOK), BF16),
            vmem((2, TOK, D), BF16),
            vmem((2 * TOK, 1536), BF16),
            vmem((12, 2 * TOK, HD), BF16),
            vmem((4, 2 * TOK, HD), BF16),
            vmem((2, 2 * TOK, 512), BF16),
            vmem((2, TOK, D), F32),
            vmem((TOK, D), F32),
            vmem((TOK, D), F32),
            vmem((2, 1, TOK), jnp.int32),
            vmem((TOK, D), F32),
            vmem((2, TOK, D), BF16),
            vmem((2 * TOK, 3072), BF16),
            vmem((3, 2 * TOK, 512), BF16),
            vmem((2, TOK, D), BF16),
            vmem((4, 4, 4, 16, 2 * TOK), BF16),
            vmem((2, 4, 4, 16, 2 * TOK), BF16),
            vmem((8, D), F32),
            pltpu.SemaphoreType.DMA((48,)),
            pltpu.SemaphoreType.DMA((TRANSFERS,)),
            pltpu.SemaphoreType.DMA((TRANSFERS,)),
        ],
        compiler_params=pltpu.CompilerParams(
            collective_id=0, has_side_effects=True, vmem_limit_bytes=64 * 2**20
        ),
        cost_estimate=pl.CostEstimate(flops=26 * 10**9, bytes_accessed=10**7, transcendentals=10**6),
    )(*operands)


def adamw(master, first, second, gradient, rate, decay):
    first_new = 0.9 * first + 0.1 * gradient
    second_new = 0.999 * second + 0.001 * gradient * gradient
    direction = first_new / (1.0 - 0.9**STEP) / (jnp.sqrt(second_new / (1.0 - 0.999**STEP)) + 1e-08)
    return (master - rate * (direction + decay * master), first_new, second_new)


def step_places():
    qkv = [(0, c * 1024, c, S_QKV, 1024) for c in range(2)]
    qkv += [(0, 2048 + c * 512, c, S_QKV + 1024, 512) for c in range(2)]
    qkv += [(0, 3072 + c * 512, c, S_QKV + 1536, 512) for c in range(2)]
    out = [(c, 0, c, S_OUT, 1024) for c in range(2)]
    gate_up = [
        (0, up * 3072 + c * 1536 + half * 768, c, S_GU + half * 1536 + up * 768, 768)
        for up in range(2)
        for c in range(2)
        for half in range(2)
    ]
    down = [(0, 0, 0, S_DN, 1024), (2, 0, 1, S_DN, 1024)]
    down += [(1, c * 512, c, S_DN + 1024, 512) for c in range(2)]
    return qkv, out, gate_up, down


def step_kernel(*refs):
    states, summed, (made, pulled), news = refs[:12], refs[12], refs[13:15], refs[15:]
    news[12][...] = made[...]
    news[13][...] = pulled[...]
    for index, places in enumerate(step_places()):
        master, first, second = states[3 * index : 3 * index + 3]
        for group, column, core, at, size in places:
            here = (group, slice(None), pl.ds(column, size))
            results = adamw(
                master[here],
                first[here],
                second[here],
                summed[core, :, pl.ds(at, size)].astype(F32),
                0.05,
                0.1,
            )
            for ref, value in zip(news[3 * index : 3 * index + 3], results):
                ref[here] = value


def step(masters, firsts, seconds, summed, tokens_out):
    rows = 32
    arrays, specs, shapes = [], [], []
    for state in zip(masters, firsts, seconds):
        for array in state:
            groups = array.shape[0] // 128
            arrays.append(array.reshape(groups, 128, -1))
            specs.append(pl.BlockSpec((groups, rows, array.shape[1]), lambda i: (0, i, 0)))
            shapes.append(jax.ShapeDtypeStruct(arrays[-1].shape, F32))
    token_rows = pl.BlockSpec((TOK * rows // 128, D), lambda i: (i, 0))
    shapes += [jax.ShapeDtypeStruct((TOK, D), BF16)] * 2
    results = pl.pallas_call(
        step_kernel,
        grid=(128 // rows,),
        out_shape=tuple(shapes),
        in_specs=specs + [pl.BlockSpec((2, rows, S_COLS), lambda i: (0, i, 0))] + [token_rows] * 2,
        out_specs=tuple(specs) + (token_rows,) * 2,
        compiler_params=pltpu.CompilerParams(vmem_limit_bytes=62 * 2**20),
        cost_estimate=pl.CostEstimate(flops=3 * 10**7, bytes_accessed=5 * 10**7, transcendentals=10**6),
    )(*arrays, summed, *tokens_out)
    states = [value.reshape(-1, value.shape[2]) for value in results[:12]]
    return [tuple(states[3 * index : 3 * index + 3]) for index in range(4)], results[12:]


def per_device(
    tokens,
    cotangent,
    segment_ids,
    positions,
    master_qkv,
    master_out,
    master_gate_up,
    master_down,
    master_gains,
    first_qkv,
    first_out,
    first_gate_up,
    first_down,
    first_gains,
    second_qkv,
    second_out,
    second_gate_up,
    second_down,
    second_gains,
):
    me = coordinates()
    shard = lax.axis_index("shard")
    order = jnp.minimum((me["y"] % 2) * 4 + me["z"], 2)
    gains = lax.dynamic_slice(
        jnp.pad(master_gains, (2048, 6144)), (2048 + 2048 * order - 288 * shard,), (2048,)
    ).reshape(16, 128)

    activations, input_grad, summed = run_layer(
        tokens,
        cotangent,
        segment_ids,
        positions,
        gains,
        master_qkv,
        master_out,
        master_gate_up,
        master_down,
    )
    summed = summed.reshape(2, 128, S_COLS)
    gain_rows = summed[:, :32, S_GAIN : S_GAIN + 128].astype(F32).sum(axis=0).reshape(-1)
    grad_gains = lax.dynamic_slice(gain_rows, (288 * shard,), (288,))
    updated, (activations, input_grad) = step(
        (master_qkv, master_out, master_gate_up, master_down),
        (first_qkv, first_out, first_gate_up, first_down),
        (second_qkv, second_out, second_gate_up, second_down),
        summed,
        (activations, input_grad),
    )
    updated.append(adamw(master_gains, first_gains, second_gains, grad_gains, 0.4, 0.0))
    return (
        activations,
        input_grad,
        *(new[0] for new in updated),
        *(new[1] for new in updated),
        *(new[2] for new in updated),
    )


def solution(mesh):
    rows = P(("rep", "shard"), None)
    state = (P("shard", None),) * 4 + (P("shard"),)
    return jax.shard_map(
        per_device,
        mesh=mesh,
        in_specs=(rows,) * 4 + state * 3,
        out_specs=(rows,) * 2 + state * 3,
        check_vma=False,
    )
```

```python
import math

import jax
import jax.numpy as jnp
from jax import lax
from jax.experimental import pallas as pl
from jax.experimental.pallas import tpu as pltpu
from jax.sharding import PartitionSpec as P

D = 1024
HEADS = 16
KV_HEADS = 8
HD = 128
FF = 3072
STEP = 10
Q_WIDTH = 2048
KV_WIDTH = 1024
TOK = 256
F32 = jnp.float32
BF16 = jnp.bfloat16
EPS = 1e-06
SCALE = HD ** (-0.5)

QKV0, GAIN0, OUT0, GU0, DN0, WCOLS = 0, 2048, 2176, 3200, 6272, 7808
G_OUT, G_DN, G_COLS = 0, 1024, 2560
S_GU, S_QKV, S_GAIN, S_DN, S_OUT, S_COLS = 0, 3072, 5120, 5632, 7168, 8192
LOG2E = 1.4426950408889634
ROTATIONS = (("x", "y", "z"), ("y", "z", "x"), ("z", "x", "y"))

SCHEDULE = {
    "start": ("W0", "W1", "W2",),
    "early": ("W0", "W1", "W0", "W2", "W1", "W0", "W2", "W1", "W0", "W1", "W2",),
    "mid": ("W2",),
    "gu0": ("G0",),
    "gu1": ("G1",),
    "mixed": ("G2", "G0",),
    "attend1": ("G1",),
    "key": ("G2", "G0",),
    "in": ("G3", "G1", "G2", "G4",),
    "end": tuple("G" + unit for unit in "05312405631204653120645310625413645"),
}
BY_NEIGHBOURS = (True, True, True, True, False, False, False)
WAYS = ("yz", "yz", "zy", "all", "zy", "yzd", "all")


def dot(left, right):
    return jnp.dot(left, right, preferred_element_type=F32)


def dot_nt(left, right):
    return lax.dot_general(left, right, (((1,), (1,)), ((), ())), preferred_element_type=F32)


def dot_tn(left, right):
    return lax.dot_general(left, right, (((0,), (0,)), ((), ())), preferred_element_type=F32)


def lanes(start, size, step=128):
    return pl.ds(start if isinstance(start, int) else pl.multiple_of(start, step), size)


def coordinates():
    rep = lax.axis_index("rep")
    shard = lax.axis_index("shard")
    return {
        "x": shard // 2,
        "y": (shard % 2) * 2 + (rep // 2) % 2,
        "z": rep // 4,
        "c": rep % 2,
    }


def device(at):
    return {"rep": at["z"] * 4 + (at["y"] % 2) * 2 + at["c"], "shard": at["x"] * 2 + at["y"] // 2}


def moved(me, axis, by):
    return {**me, axis: (me[axis] + by + 4) % 4}


def view(ref, select, offset, size):
    where = tuple(select.get(axis, slice(None)) for axis in "xyz")
    return ref.at[where + (slice(None), lanes(offset, size))]


def layer_kernel(
    tokens,
    cotangent,
    segments,
    positions,
    gains,
    master_qkv,
    master_out,
    master_gate_up,
    master_down,
    activations,
    input_grad,
    summed,
    weights,
    grads,
    other_weights,
    got_far,
    got_near,
    got_two,
    got_three,
    toks,
    cots,
    rope,
    mask,
    mask_turned,
    hidden,
    raw,
    rotated,
    vals,
    mixed,
    part,
    got_part,
    got_down,
    numbers,
    middle,
    hidden_mid,
    gate_up,
    active,
    branch,
    turned_lhs,
    spare,
    gains_acc,
    local_sem,
    send_sem,
    recv_sem,
):
    me = coordinates()
    c = me["c"]
    sib = 1 - c
    x, y, z = me["x"], me["y"], me["z"]
    sibling = device({**me, "c": sib})
    used = [0]

    class Transfer:
        def __init__(self, source, there, here, target):
            self.index = used[0]
            used[0] += 1
            self.source, self.there, self.here, self.target = source, there, here, target
            self.copy(source, there).start()

        def copy(self, source, there):
            return pltpu.make_async_remote_copy(
                src_ref=source,
                dst_ref=there,
                send_sem=send_sem.at[self.index],
                recv_sem=recv_sem.at[self.index],
                device_id=self.target,
                device_id_type=pl.DeviceIdType.MESH,
            )

        def arrived(self):
            self.copy(self.here, self.here).wait_recv()

        def sent(self):
            self.copy(self.source, self.there).wait_send()

    pending = []

    def send(source, there, here, target):
        transfer = Transfer(source, there, here, target)
        pending.append(transfer)
        return transfer

    def flush():
        while pending:
            pending.pop(0).sent()

    def arrive(transfers):
        for transfer in transfers:
            transfer.arrived()

    row = 16 * ((y % 2) * 4 + z)

    def rows_of(ref, first, offset, size):
        return ref.at[pl.ds(pl.multiple_of(first, 16), 16), lanes(offset, size)]

    groups = [
        (rows_of(master_qkv, row, c * 1024, 1024), QKV0, 1024),
        (rows_of(master_qkv, row, 2048 + c * 512, 512), QKV0 + 1024, 512),
        (rows_of(master_qkv, row, 3072 + c * 512, 512), QKV0 + 1536, 512),
        (rows_of(master_out, c * 128 + row, 0, 1024), OUT0, 1024),
        (rows_of(master_gate_up, row, c * 1536, 768), GU0, 768),
        (rows_of(master_gate_up, row, 3072 + c * 1536, 768), GU0 + 768, 768),
        (rows_of(master_gate_up, row, c * 1536 + 768, 768), GU0 + 1536, 768),
        (rows_of(master_gate_up, row, 3072 + c * 1536 + 768, 768), GU0 + 2304, 768),
        (rows_of(master_down, c * 256 + row, 0, 1024), DN0, 1024),
        (rows_of(master_down, 128 + row, c * 512, 512), DN0 + 1024, 512),
    ]
    inward = [
        (source, got_part.at[pl.ds(16 * index, 16), pl.ds(0, size)])
        for index, (source, offset, size) in enumerate(groups)
    ]
    inward += [(gains, got_part.at[pl.ds(160, 16), pl.ds(0, 128)])]
    first_inward = len(inward)
    inward += [
        (segments, numbers.at[0]),
        (positions, numbers.at[1]),
        (tokens, toks.at[c]),
        (cotangent, cots.at[c]),
    ]
    inward = [pltpu.make_async_copy(*pair, local_sem.at[index]) for index, pair in enumerate(inward)]

    barrier = pltpu.get_barrier_semaphore()
    across_y = {**me, "y": y + 1 - 2 * (y % 2)}
    friends = [sibling] + [device(moved(me, axis, by)) for axis in "xyz" for by in (1, 2, 3)]
    friends += [device(moved(across_y, "z", by)) for by in (1, 2, 3)]
    for friend in friends:
        pl.semaphore_signal(barrier, inc=1, device_id=friend, device_id_type=pl.DeviceIdType.MESH)
    for copy in inward:
        copy.start()
    for copy in inward[:first_inward]:
        copy.wait()
    for index, (source, offset, size) in enumerate(groups):
        rows16 = got_part[16 * index : 16 * index + 16, 0:size]
        weights[x, y, z, :, offset : offset + size] = rows16.astype(BF16)
    weights[x, y, z, :, GAIN0 : GAIN0 + 128] = got_part[160:176, 0:128].astype(BF16)
    pl.semaphore_wait(barrier, len(friends))

    def gather_one(rotation, offset, size):
        first, second, third = rotation
        source = view(weights, {"x": x, "y": y, "z": z}, offset, size)
        out = []
        for by in (1, 2, 3):
            here = view(weights, {**{"x": x, "y": y, "z": z}, third: (me[third] - by + 4) % 4}, offset, size)
            out.append(send(source, source, here, device(moved(me, third, by))))
        return out

    def gather_two(rotation, offset, size):
        first, second, third = rotation
        source = view(weights, {first: me[first], second: me[second]}, offset, size)
        out = []
        for by in (1, 3):
            here = view(weights, {first: me[first], second: (me[second] - by + 4) % 4}, offset, size)
            out.append(send(source, source, here, device(moved(me, second, by))))
        return out

    def gather_on(rotation, offset, size):
        first, second, third = rotation
        out = []
        for by, half in ((1, 0), (3, 1)):
            spot = {first: me[first], third: pl.ds(2 * half, 2)}
            source = view(weights, {**spot, second: (me[second] - by + 4) % 4}, offset, size)
            here = view(weights, {**spot, second: (me[second] + 2) % 4}, offset, size)
            out.append(send(source, source, here, device(moved(me, second, by))))
        return out

    def gather_three(rotation, offset, size):
        first = rotation[0]
        source = view(weights, {first: me[first]}, offset, size)
        out = []
        for by in (1, 3):
            here = view(weights, {first: (me[first] - by + 4) % 4}, offset, size)
            out.append(send(source, source, here, device(moved(me, first, by))))
        return out

    def gather_four(rotation, offset, size):
        first, second = rotation[0], rotation[1]
        out = []
        for by, half in ((1, 0), (3, 1)):
            rows = pl.ds(2 * half, 2)
            source = view(weights, {first: (me[first] - by + 4) % 4, second: rows}, offset, size)
            here = view(weights, {first: (me[first] + 2) % 4, second: rows}, offset, size)
            out.append(send(source, source, here, device(moved(me, first, by))))
        return out

    chunks = (
        ((0, 1152), (1152, 1024), (OUT0, 1024)),
        ((GU0, 1024), (GU0 + 1024, 1024), (GU0 + 2048, 1024)),
        ((DN0, 512), (DN0 + 512, 512), (DN0 + 1024, 512)),
    )
    steps = (gather_one, gather_two, gather_on, gather_three, gather_four)
    flying = [[None] * 3 for _ in chunks]

    w_step = [0] * len(chunks)

    def pump(chunk):
        step = w_step[chunk]
        w_step[chunk] += 1
        for index, rotation in enumerate(ROTATIONS):
            if step:
                arrive(flying[chunk][index])
            if step < len(steps):
                flying[chunk][index] = steps[step](rotation, *chunks[chunk][index])

    def gathered(chunk):
        while w_step[chunk] <= len(steps):
            pump(chunk)

    def exchange(name):
        for item in SCHEDULE.get(name, ()):
            (pump if item[0] == "W" else reduce)(int(item[1]))

    exchange("start")
    for copy in inward[first_inward:]:
        copy.wait()
    order = lax.broadcasted_iota(jnp.int32, (64, 256), 0).astype(F32)
    angle = jnp.exp(order * (-2.0 * math.log(1000000.0) / HD)) * numbers[1].astype(F32)
    cosine = jnp.cos(angle)
    sine = jnp.sin(angle)
    rope[c, :, 0:128] = jnp.concatenate([cosine, cosine], axis=0).T
    rope[c, :, 128:256] = jnp.concatenate([-sine, sine], axis=0).T
    across_segments = jnp.broadcast_to(numbers[0].astype(F32), (256, 256))
    same = across_segments == across_segments.T
    earlier = lax.broadcasted_iota(jnp.int32, (256, 256), 1) <= lax.broadcasted_iota(
        jnp.int32, (256, 256), 0
    )
    mask[c] = jnp.where(same & earlier, 0.0, -1e30).astype(BF16)
    early = [
        send(toks.at[c], toks.at[c], toks.at[sib], sibling),
        send(rope.at[c], rope.at[c], rope.at[sib], sibling),
        send(mask.at[c], mask.at[c], mask.at[sib], sibling),
        send(cots.at[c], cots.at[c], cots.at[sib], sibling),
    ]
    exchange("early")
    arrive(early)
    for b in range(2):
        mask_turned[b] = mask[b].astype(F32).T.astype(BF16)
    exchange("late")
    gathered(0)

    def to_other(offset, size, at):
        return send(
            view(weights, {"x": pl.ds(2 * sib, 2)}, offset, size),
            view(other_weights, {}, at, size),
            view(other_weights, {}, at, size),
            sibling,
        )

    other_out = to_other(OUT0, 1024, 0)

    def weight(offset, size):
        return weights[:, :, :, :, lanes(offset, size)].reshape(1024, size)

    def weight_rows(row, offset, size):
        return weights[row, :, :, :, lanes(offset, size)].reshape(256, size)

    def weight_own(offset, size):
        return weights[pl.ds(2 * c, 2), :, :, :, lanes(offset, size)].reshape(512, size)

    def weight_other(offset, size):
        return other_weights[:, :, :, :, lanes(offset, size)].reshape(512, size)

    gain_rows = jnp.zeros((16, 128), F32)
    head_rows = jnp.zeros((16, 128), F32)
    for part_x in range(4):
        for part_y in (0, 2):
            gain_rows += weights[part_x, part_y, 0, :, pl.ds(GAIN0, 128)].astype(F32)
            head_rows += weights[part_x, part_y, 1, :, pl.ds(GAIN0, 128)].astype(F32)
    gain_in = jnp.concatenate([gain_rows[i : i + 1] for i in range(8)], axis=1)
    gain_mid = jnp.concatenate([gain_rows[i : i + 1] for i in range(8, 16)], axis=1)
    gain_query = head_rows[0:1]
    gain_key = head_rows[1:2]

    def unit_of(values):
        scale = lax.rsqrt(jnp.mean(values * values, axis=-1, keepdims=True) + EPS)
        return values * scale, scale

    def norm_back(upstream, gain, unit, scale):
        pushed = upstream * gain
        inner = jnp.mean(pushed * unit, axis=-1, keepdims=True)
        return scale * (pushed - unit * inner)

    for b in range(2):
        unit, _ = unit_of(toks[b].astype(F32))
        hidden[b] = (unit * gain_in).astype(BF16)

    def all_hidden():
        return hidden[...].reshape(512, 1024)

    mean_of = jnp.full((128, 128), 1.0 / 128, BF16)

    def head_mean(values):
        return dot(values.astype(BF16), mean_of)

    def project_heads(t, carry):
        values = dot(all_hidden(), weight(QKV0 + t * 256, 256))
        raw[:, lanes(t * 256, 256)] = values.astype(BF16)
        gain = jnp.where(t < 4, gain_query, gain_key)
        cosine = rope[:, :, 0:128].reshape(512, 128)
        sine = rope[:, :, 128:256].reshape(512, 128)
        for h in range(2):
            head = values[:, h * 128 : (h + 1) * 128]
            normal = head * lax.rsqrt(head_mean(head * head) + EPS) * gain
            rotated[2 * t + h] = (normal * cosine + pltpu.roll(normal, 64, 1) * sine).astype(BF16)
        return carry

    lax.fori_loop(0, 6, project_heads, 0)

    def project_values(t, carry):
        values = dot(all_hidden(), weight(QKV0 + 1536 + t * 256, 256)).astype(BF16)
        vals[2 * t] = values[:, :128]
        vals[2 * t + 1] = values[:, 128:]
        return carry

    lax.fori_loop(0, 2, project_values, 0)
    exchange("project")

    def heads_of(b, g):
        rows = pl.ds(pl.multiple_of(b * 256, 256), 256)
        query = rotated[pl.ds(2 * g, 2), rows, :].reshape(512, 128)
        return rows, query, rotated[8 + g, rows, :], vals[g, rows, :]

    def attend(step, carry):
        b, g = step // 4, step % 4
        rows, query, key, value = heads_of(b, g)
        scores = dot_nt(query, key).reshape(2, 256, 256) * (SCALE * LOG2E) + mask[b].astype(F32)[None]
        expo = jnp.exp2(scores).reshape(512, 256).astype(BF16)
        result = dot(expo, jnp.concatenate([value, jnp.ones((256, 128), BF16)], axis=1))
        result = (result[:, :128] / result[:, 128:]).astype(BF16)
        for h in range(2):
            mixed[h, rows, lanes(g * 128, 128)] = result[h * 256 : (h + 1) * 256]
        return carry

    lax.fori_loop(0, 8, attend, 0)

    exchange("attend")
    arrive([other_out])

    def two_parts(values, columns):
        part[0, :, columns] = values[:256]
        part[1, :, columns] = values[256:]

    def project_out(t, carry):
        values = dot(mixed[c], weight_own(OUT0 + t * 512, 512)) + dot(
            mixed[sib], weight_other(t * 512, 512)
        )
        two_parts(values, lanes(t * 512, 512))
        return carry

    lax.fori_loop(0, 2, project_out, 0)
    exchange("projected")
    across = send(part.at[sib], got_part, got_part, sibling)
    across.arrived()
    middle[...] = toks[c].astype(F32) + part[c] + got_part[...]
    unit_mid, _ = unit_of(middle[...])
    hidden_mid[c] = (unit_mid * gain_mid).astype(BF16)
    across_mid = send(hidden_mid.at[c], hidden_mid.at[c], hidden_mid.at[sib], sibling)
    across.sent()
    pending.remove(across)
    exchange("mid")
    gathered(1)
    arrive([across_mid])

    def all_mid():
        return hidden_mid[...].reshape(512, 1024)

    def feed_forward(t, carry):
        column = (t // 3) * 1536 + (t % 3) * 256
        gate = dot(all_mid(), weight(GU0 + column, 256))
        up = dot(all_mid(), weight(GU0 + column + 768, 256))
        gate_up[:, lanes(column, 256)] = gate.astype(BF16)
        gate_up[:, lanes(column + 768, 256)] = up.astype(BF16)
        result = (gate * jax.nn.sigmoid(gate) * up).astype(BF16)
        for h in range(2):
            block = 2 * t + h
            active[block % 3, :, lanes((block // 3) * 128, 128)] = result[:, h * 128 : (h + 1) * 128]
        return carry

    lax.fori_loop(0, 3, feed_forward, 0)
    exchange("feed0")
    lax.fori_loop(3, 6, feed_forward, 0)
    exchange("feed1")

    def unit_of_parts(ref, offset, sizes, column):
        parts = []
        for size in sizes:
            parts.append((ref, offset, size, column))
            offset, column = offset + size, column + size
        return parts

    plans = (
        unit_of_parts(grads, G_DN, (512, 512, 512), S_DN),
        unit_of_parts(weights, GU0, (512, 512, 512), S_GU),
        unit_of_parts(weights, GU0 + 1536, (512, 512, 512), S_GU + 1536),
        unit_of_parts(grads, G_OUT, (256, 384, 384), S_OUT),
        unit_of_parts(weights, OUT0, (512, 256, 256), S_QKV),
        unit_of_parts(weights, DN0, (256, 384, 384), S_QKV + 1024),
        unit_of_parts(weights, DN0 + 1024, (128,), S_GAIN),
    )
    UNITS = len(plans)
    landing, at = {}, 0
    for unit in range(UNITS):
        for index in range(len(plans[unit])):
            landing[unit, index] = at
            at += plans[unit][index][2]

    def remaining(rotation):
        return [axis for axis in "xyz" if axis != rotation[0]]

    def add_blocks(blocks, target, size, shape):
        count = math.prod(shape)

        def body(k, carry):
            where = []
            left = k
            for extent in reversed(shape):
                where.insert(0, left % extent)
                left = left // extent
            total = blocks[0](where)
            for block in blocks[1:]:
                total = total + block(where)
            target(where, total.astype(BF16))
            return carry

        if count == 1:
            body(0, 0)
        else:
            lax.fori_loop(0, count, body, 0)

    def reader(ref, offset, size, locate):
        return lambda where: ref[locate(where) + (slice(None), lanes(offset, size))].astype(F32)

    def writer(ref, offset, size, locate):
        def store(where, value):
            ref[locate(where) + (slice(None), lanes(offset, size))] = value

        return store

    sums = {}

    def reduce_one(unit, index):
        ref, offset, size, to = plans[unit][index]
        rotation = ROTATIONS[index]
        first, other = rotation[0], remaining(rotation)[0]
        at = landing[unit, index]
        sums[unit, index, 1] = [
            send(
                view(ref, {first: (me[first] + 2) % 4, other: pl.ds(2 * half, 2)}, offset, size),
                got_far.at[half, :, :, :, lanes(at, size)],
                got_far.at[half, :, :, :, lanes(at, size)],
                device(moved(me, first, by)),
            )
            for by, half in ((1, 0), (3, 1))
        ]

    def reduce_two(unit, index):
        ref, offset, size, to = plans[unit][index]
        rotation = ROTATIONS[index]
        first, (other, last) = rotation[0], remaining(rotation)
        at = landing[unit, index]
        arrive(sums[unit, index, 1])
        out = []
        for by, half in ((1, 0), (3, 1)):
            block = (me[first] + by) % 4

            def locate(where, block=block, half=half):
                spot = {first: block, other: where[0] + 2 * half, last: where[1]}
                return tuple(spot[axis] for axis in "xyz")

            add_blocks(
                [
                    reader(ref, offset, size, locate),
                    reader(got_far, at, size, lambda where, half=half: (half, where[0], where[1])),
                ],
                writer(ref, offset, size, locate),
                size,
                (2, 4),
            )
            out.append(
                send(
                    view(ref, {first: block}, offset, size),
                    got_near.at[half, :, :, :, lanes(at, size)],
                    got_near.at[half, :, :, :, lanes(at, size)],
                    device(moved(me, first, by)),
                )
            )
        sums[unit, index, 2] = out

    def reduce_three(unit, index):
        ref, offset, size, to = plans[unit][index]
        rotation = ROTATIONS[index]
        first, second, third = rotation
        other, last = remaining(rotation)
        at = landing[unit, index]
        arrive(sums[unit, index, 2])

        def locate(where):
            spot = {first: me[first], other: where[0], last: where[1]}
            return tuple(spot[axis] for axis in "xyz")

        add_blocks(
            [reader(ref, offset, size, locate)]
            + [
                reader(got_near, at, size, lambda where, half=half: (half, where[0], where[1]))
                for half in range(2)
            ],
            writer(ref, offset, size, locate),
            size,
            (4, 4),
        )
        if not BY_NEIGHBOURS[unit]:
            sums[unit, index, 3] = [
                send(
                    view(ref, {first: me[first], second: (me[second] + by) % 4}, offset, size),
                    got_two.at[by - 1, :, :, lanes(at, size)],
                    got_two.at[by - 1, :, :, lanes(at, size)],
                    device(moved(me, second, by)),
                )
                for by in (1, 2, 3)
            ]
            return
        sums[unit, index, 3] = [
            send(
                view(
                    ref,
                    {first: me[first], second: (me[second] + 2) % 4, third: pl.ds(2 * half, 2)},
                    offset,
                    size,
                ),
                got_two.at[2, 2 * half : 2 * half + 2, :, lanes(at, size)],
                got_two.at[2, 2 * half : 2 * half + 2, :, lanes(at, size)],
                device(moved(me, second, by)),
            )
            for by, half in ((1, 0), (3, 1))
        ]

    def reduce_on(unit, index):
        ref, offset, size, to = plans[unit][index]
        first, second, third = ROTATIONS[index]
        at = landing[unit, index]
        arrive(sums[unit, index, 3])
        out = []
        for by, half in ((1, 0), (3, 1)):
            block = (me[second] + by) % 4

            def locate(where, block=block, half=half):
                spot = {first: me[first], second: block, third: where[0] + 2 * half}
                return tuple(spot[axis] for axis in "xyz")

            add_blocks(
                [
                    reader(ref, offset, size, locate),
                    reader(got_two, at, size, lambda where, half=half: (2, where[0] + 2 * half)),
                ],
                writer(ref, offset, size, locate),
                size,
                (2,),
            )
            out.append(
                send(
                    view(ref, {first: me[first], second: block}, offset, size),
                    got_two.at[half, :, :, lanes(at, size)],
                    got_two.at[half, :, :, lanes(at, size)],
                    device(moved(me, second, by)),
                )
            )
        sums[unit, index, 3] = out

    def reduce_four(unit, index):
        ref, offset, size, to = plans[unit][index]
        first, second, third = ROTATIONS[index]
        at = landing[unit, index]
        arrive(sums[unit, index, 3])

        def locate(where):
            spot = {first: me[first], second: me[second], third: where[0]}
            return tuple(spot[axis] for axis in "xyz")

        add_blocks(
            [reader(ref, offset, size, locate)]
            + [
                reader(got_two, at, size, lambda where, by=by: (by, where[0]))
                for by in range(2 if BY_NEIGHBOURS[unit] else 3)
            ],
            writer(ref, offset, size, locate),
            size,
            (4,),
        )
        sums[unit, index, 4] = [
            send(
                view(ref, {first: me[first], second: me[second], third: (me[third] + by) % 4}, offset, size),
                got_three.at[by - 1, :, lanes(at, size)],
                got_three.at[by - 1, :, lanes(at, size)],
                device(moved(me, third, by)),
            )
            for by in (1, 2, 3)
        ]

    y_low = y % 2
    local_count = [len(inward)]
    local_pending = {}

    def whole(unit):
        ref, offset, _, to = plans[unit][0]
        size = sum(part[2] for part in plans[unit])
        return ref.at[x, y, z, :, lanes(offset, size)], lanes(to, size)

    def along_z(unit, source, there, here, steps=(1, 2, 3)):
        sums[unit] = [
            send(source, there, here((z - by + 4) % 4), device(moved(me, "z", by))) for by in steps
        ]

    def landed(unit):
        arrive(sums[unit])
        if unit in local_pending:
            local_pending.pop(unit).wait()
        return whole(unit)[1]

    def reduce_five(unit):
        for index in range(len(plans[unit])):
            ref, offset, size, to = plans[unit][index]
            at = landing[unit, index]
            arrive(sums[unit, index, 4])
            here = (x, y, z)
            add_blocks(
                [reader(ref, offset, size, lambda where: here)]
                + [reader(got_three, at, size, lambda where, by=by: (by,)) for by in range(3)],
                writer(ref, offset, size, lambda where: here),
                size,
                (1,),
            )
        source, column = whole(unit)
        there = summed.at[c, y_low, z, :, column]
        local_pending[unit] = pltpu.make_async_copy(source, there, local_sem.at[local_count[0]])
        local_count[0] += 1
        local_pending[unit].start()
        way = WAYS[unit]
        if way in ("zy", "all"):
            along_z(unit, source, there, lambda at_z: summed.at[c, y_low, at_z, :, column])
        if way in ("yz", "yzd"):
            sums[unit] = [send(source, there, summed.at[c, 1 - y_low, z, :, column], device(across_y))]
        if way == "all":
            sums[unit] += [
                send(
                    source,
                    there,
                    summed.at[c, 1 - y_low, (z - by + 4) % 4, :, column],
                    device(moved(across_y, "z", by)),
                )
                for by in range(4)
            ]

    def spread_y(unit):
        column = landed(unit)
        source = summed.at[c, y_low, :, :, column]
        sums[unit] = [send(source, source, summed.at[c, 1 - y_low, :, :, column], device(across_y))]

    def spread_z(unit):
        column = landed(unit)
        source = summed.at[c, :, z, :, column]
        steps = (1, 2, 3) if WAYS[unit] == "yzd" else (1, 3)
        along_z(unit, source, source, lambda at_z: summed.at[c, :, at_z, :, column], steps)

    def spread_on(unit):
        column = landed(unit)
        out = []
        for by, half in ((1, 0), (3, 1)):
            source = summed.at[c, half, (z - by + 4) % 4, :, column]
            here = summed.at[c, half, (z + 2) % 4, :, column]
            out.append(send(source, source, here, device(moved(me, "z", by))))
        sums[unit] = out

    def spread_core(unit):
        column = landed(unit)
        source = summed.at[c, :, :, :, column]
        sums[unit] = [send(source, source, summed.at[sib, :, :, :, column], sibling)]

    spreads = {
        "yz": (spread_z, spread_on, spread_core),
        "yzd": (spread_z, spread_core),
        "zy": (spread_y, spread_core),
        "all": (spread_core,),
    }

    def stages_of(unit):
        sums_by_part = [reduce_one, reduce_two, reduce_three, reduce_four]
        if BY_NEIGHBOURS[unit]:
            sums_by_part.insert(3, reduce_on)

        def for_parts(stage):
            def run(unit):
                for index in range(len(plans[unit])):
                    stage(unit, index)

            return run

        return [for_parts(stage) for stage in sums_by_part] + [reduce_five, *spreads[WAYS[unit]]]

    stages = [stages_of(unit) for unit in range(UNITS)]

    def reduce(unit):
        stages[unit].pop(0)(unit)

    def all_cots():
        return cots[...].reshape(512, 1024)

    def cot_half(half):
        return cots[:, :, lanes(half * 512, 512, 512)].reshape(512, 512)

    def grads_own(offset, size, values):
        grads[pl.ds(2 * c, 2), :, :, :, lanes(offset, size)] = values.astype(BF16).reshape(2, 4, 4, 16, size)

    def grads_other(offset, size, values):
        weights[pl.ds(2 * sib, 2), :, :, :, lanes(offset, size)] = values.astype(BF16).reshape(2, 4, 4, 16, size)

    def turned(values, t):
        turned_lhs[pl.ds(2 * t, 2)] = values.astype(BF16).reshape(2, 4, 4, 16, 512)

    for t in range(2):
        columns = slice(t * 512, (t + 1) * 512)
        turned(dot_tn(active[2 * sib], cots[:, :, columns].reshape(512, 512)), t)
    spare[...] = dot_tn(active[1], cot_half(sib)).astype(BF16).reshape(2, 4, 4, 16, 512)
    to_sibling = [
        send(source, view(grads, {"x": pl.ds(2 * c, 2)}, at, 512), view(grads, {"x": pl.ds(2 * sib, 2)}, at, 512), sibling)
        for source, at in (
            (turned_lhs.at[0:2], G_DN),
            (turned_lhs.at[2:4], G_DN + 512),
            (spare, G_DN + 1024),
        )
    ]
    for t in range(2):
        values = dot_tn(active[2 * c], cots[:, :, t * 512 : (t + 1) * 512].reshape(512, 512))
        grads_own(G_DN + t * 512, 512, values)
    grads_own(G_DN + 1024, 512, dot_tn(active[1], cot_half(c)))
    exchange("down")
    arrive(to_sibling)
    reduce(0)
    gathered(2)
    other_down = to_other(DN0, 1536, 1024)
    flush()
    turned_lhs[...] = all_mid().T.reshape(4, 4, 4, 16, 512)
    arrive([other_down])

    def left():
        return turned_lhs[...].reshape(1024, 512)

    def back_active(kind, q):
        if kind == 0:
            group = 2 * c
            values = dot_nt(all_cots(), weight_rows(2 * c + q, DN0, 1024))
        elif kind == 1:
            group = 2 * sib
            values = dot_nt(all_cots(), other_weights[q, :, :, :, 1024:2048].reshape(256, 1024))
        else:
            group = 1
            values = dot_nt(cot_half(c), weight_rows(2 * c + q, DN0 + 1024, 512)) + dot_nt(
                cot_half(sib), other_weights[q, :, :, :, 2048:2560].reshape(256, 512)
            )
        for h in range(2):
            column = q * 1536 + (3 * h + group) * 128
            pulled = values[:, h * 128 : (h + 1) * 128]
            gate = gate_up[:, lanes(column, 128)].astype(F32)
            up = gate_up[:, lanes(column + 768, 128)].astype(F32)
            sigma = jax.nn.sigmoid(gate)
            back_gate = pulled * up * sigma * (1.0 + gate * (1.0 - sigma))
            gate_up[:, lanes(column, 128)] = back_gate.astype(BF16)
            gate_up[:, lanes(column + 768, 128)] = (pulled * gate * sigma).astype(BF16)

    def back_mid(half):
        def body(row, carry):
            values = dot_nt(
                gate_up[:, half * 1536 : (half + 1) * 1536], weight_rows(row, GU0 + half * 1536, 1536)
            )
            columns = lanes(row * 256, 256)
            if half == 0:
                two_parts(values, columns)
            else:
                part[0, :, columns] += values[:256]
                part[1, :, columns] += values[256:]
            return carry

        lax.fori_loop(0, 4, body, 0)

    def gate_up_grads(half):
        def body(t, carry):
            column = half * 1536 + t * 512
            values = dot(left(), gate_up[:, lanes(column, 512)])
            weights[:, :, :, :, lanes(GU0 + column, 512)] = values.astype(BF16).reshape(4, 4, 4, 16, 512)
            return carry

        lax.fori_loop(0, 3, body, 0)

    for kind in range(3):
        back_active(kind, 0)
    exchange("active0")
    back_mid(0)
    gate_up_grads(0)
    reduce(1)
    exchange("gu0")
    for kind in range(3):
        back_active(kind, 1)
    exchange("active1")
    back_mid(1)
    exchange("mid1")
    across = send(part.at[sib], got_part, got_part, sibling)
    gate_up_grads(1)
    reduce(2)
    exchange("gu1")
    arrive([across])
    back = part[c] + got_part[...]
    unit_mid, scale_mid = unit_of(middle[...])
    gains_acc[1:2, :] = jnp.sum(back * unit_mid, axis=0, keepdims=True)
    back_middle = cots[c].astype(F32) + norm_back(back, gain_mid, unit_mid, scale_mid)
    branch[c] = back_middle.astype(BF16)
    across.sent()
    pending.remove(across)
    across_branch = send(branch.at[c], branch.at[c], branch.at[sib], sibling)
    cots[c] = (back_middle - branch[c].astype(F32)).astype(BF16)

    down_rows = lambda t: (
        dot(active[2 * c], weight_own(DN0 + t * 256, 256))
        + dot(active[2 * sib], weight_other(1024 + t * 256, 256))
    )
    for t in range(4):
        values = down_rows(t)
        two_parts(values, pl.ds(t * 256, 256))
    for half, load in ((c, lambda: weight_own(DN0 + 1024, 512)), (sib, lambda: weight_other(2048, 512))):
        values = dot(active[1], load())
        columns = lanes(half * 512, 512, 512)
        part[0, :, columns] += values[:256]
        part[1, :, columns] += values[256:]
    across_down = send(part.at[sib], got_down, got_down, sibling)
    middle[...] += part[c]
    exchange("output")
    arrive([across_branch])

    def all_branch():
        return branch[...].reshape(512, 1024)

    for t in range(2):
        columns = slice(t * 512, (t + 1) * 512)
        turned(dot_tn(mixed[sib], branch[:, :, columns].reshape(512, 512)), t)
    to_sibling = [
        send(
            turned_lhs.at[2 * t : 2 * t + 2],
            view(grads, {"x": pl.ds(2 * c, 2)}, G_OUT + t * 512, 512),
            view(grads, {"x": pl.ds(2 * sib, 2)}, G_OUT + t * 512, 512),
            sibling,
        )
        for t in range(2)
    ]
    for t in range(2):
        columns = slice(t * 512, (t + 1) * 512)
        grads_own(G_OUT + t * 512, 512, dot_tn(mixed[c], branch[:, :, columns].reshape(512, 512)))
    mixed_back = (
        dot_nt(all_branch(), weight_own(OUT0, 1024)).astype(BF16),
        dot_nt(all_branch(), weight_other(0, 1024)).astype(BF16),
    )
    for h, values in ((c, mixed_back[0]), (sib, mixed_back[1])):
        hidden_mid[h, :, 0:512] = values[:256]
        hidden_mid[h, :, 512:1024] = values[256:]
    arrive(to_sibling)
    reduce(3)
    exchange("mixed")
    gains_acc[2:3, :] = jnp.zeros((1, 1024), F32)

    def attend_back(step, carry):
        b, g = step // 4, step % 4
        rows, query, key, value = heads_of(b, g)
        column = lanes(b * 512 + g * 128, 128)
        pulled = jnp.concatenate([hidden_mid[h, :, column] for h in range(2)], axis=0)
        bias = mask_turned[b].astype(F32)
        scores = dot_nt(key, query) * (SCALE * LOG2E) + jnp.concatenate([bias, bias], axis=1)
        expo = jnp.exp2(scores)
        probs = expo * (1.0 / jnp.sum(expo, axis=0, keepdims=True))
        back_probs = dot_nt(value, pulled)
        inner = jnp.sum(probs * back_probs, axis=0, keepdims=True)
        back_scores = (probs * (back_probs - inner) * SCALE).astype(BF16)
        back_query = dot_tn(back_scores, key)
        back_key = dot(back_scores, query)
        back_value = dot(probs.astype(BF16), pulled)
        cosine = rope[b, :, 0:128]
        sine = rope[b, :, 128:256]

        def through(upstream, column, gain):
            values = raw[rows, lanes(column, 128)].astype(F32)
            scale = lax.rsqrt(head_mean(values * values) + EPS)
            unit = values * scale
            plain = upstream * cosine - pltpu.roll(upstream, 64, 1) * sine
            term = plain * unit
            pushed = plain * gain
            result = scale * (pushed - unit * head_mean(term * gain))
            gate_up[rows, lanes(column, 128)] = result.astype(BF16)
            return jnp.sum(term, axis=0, keepdims=True)

        for h in range(2):
            gains_acc[2:3, 0:128] += through(
                back_query[h * 256 : (h + 1) * 256], (2 * g + h) * 128, gain_query
            )
        gains_acc[2:3, 128:256] += through(back_key, 1024 + g * 128, gain_key)
        gate_up[rows, lanes(1536 + g * 128, 128)] = back_value.astype(BF16)
        return carry

    lax.fori_loop(0, 4, attend_back, 0)
    exchange("attend0")
    lax.fori_loop(4, 8, attend_back, 0)
    exchange("attend1")
    for transfer in to_sibling:
        transfer.sent()
        pending.remove(transfer)
    turned_lhs[...] = all_hidden().T.reshape(4, 4, 4, 16, 512)

    def qkv_grads(t, carry):
        values = dot(left(), gate_up[:, lanes(t * 512, 512)])
        column = t * 512 + jnp.where(t < 2, OUT0, DN0 - 1024)
        weights[:, :, :, :, lanes(column, 512)] = values.astype(BF16).reshape(4, 4, 4, 16, 512)
        return carry

    lax.fori_loop(0, 2, qkv_grads, 0)
    reduce(4)
    exchange("query")
    lax.fori_loop(2, 4, qkv_grads, 0)
    reduce(5)
    exchange("key")
    across_down.sent()
    pending.remove(across_down)

    def back_in(row, carry):
        values = dot_nt(gate_up[:, 0:2048], weight_rows(row, QKV0, 2048))
        two_parts(values, lanes(row * 256, 256))
        return carry

    lax.fori_loop(0, 4, back_in, 0)
    across = send(part.at[sib], got_part, got_part, sibling)
    across_down.arrived()
    hidden_mid[c] = (middle[...] + got_down[...]).astype(BF16)
    copy_out = pltpu.make_async_copy(hidden_mid.at[c], activations, local_sem.at[0])
    copy_out.start()
    exchange("in")
    arrive([across])
    back = part[c] + got_part[...]
    unit_in, scale_in = unit_of(toks[c].astype(F32))
    gains_acc[0:1, :] = jnp.sum(back * unit_in, axis=0, keepdims=True)
    back_middle = branch[c].astype(F32) + cots[c].astype(F32)
    hidden_mid[sib] = (back_middle + norm_back(back, gain_in, unit_in, scale_in)).astype(BF16)
    copy_in = pltpu.make_async_copy(hidden_mid.at[sib], input_grad, local_sem.at[1])
    copy_in.start()

    low = jnp.concatenate(
        [gains_acc[r : r + 1, i * 128 : (i + 1) * 128] for r in range(2) for i in range(8)], axis=0
    ).astype(BF16)
    high = jnp.concatenate(
        [gains_acc[2:3, 0:128], gains_acc[2:3, 128:256], jnp.zeros((14, 128), F32)], axis=0
    ).astype(BF16)
    gains_at = slice(DN0 + 1024, DN0 + 1152)
    weights[:, :, :, :, gains_at] = jnp.zeros((4, 4, 4, 16, 128), BF16)
    for part_x in range(4):
        for part_y in (0, 2):
            weights[part_x, part_y, 0, :, gains_at] = low
            weights[part_x, part_y, 1, :, gains_at] = high
    reduce(6)
    exchange("end")
    assert not any(stages)
    for unit in range(UNITS):
        arrive(sums[unit])
    copy_out.wait()
    copy_in.wait()
    flush()
    assert used[0] <= TRANSFERS and local_count[0] <= 48, used


TRANSFERS = 416


def run_layer(*operands):
    anywhere = pl.BlockSpec(memory_space=pl.ANY)
    vmem = pltpu.VMEM
    return pl.pallas_call(
        layer_kernel,
        out_shape=(
            jax.ShapeDtypeStruct((TOK, D), BF16),
            jax.ShapeDtypeStruct((TOK, D), BF16),
            jax.ShapeDtypeStruct((2, 2, 4, 16, S_COLS), BF16),
        ),
        in_specs=[anywhere] * 9,
        out_specs=(anywhere,) * 3,
        scratch_shapes=[
            vmem((4, 4, 4, 16, WCOLS), BF16),
            vmem((4, 4, 4, 16, G_COLS), BF16),
            vmem((2, 4, 4, 16, 2560), BF16),
            vmem((2, 2, 4, 16, WCOLS), BF16),
            vmem((2, 4, 4, 16, WCOLS), BF16),
            vmem((3, 4, 16, WCOLS), BF16),
            vmem((3, 16, WCOLS), BF16),
            vmem((2, TOK, D), BF16),
            vmem((2, TOK, D), BF16),
            vmem((2, TOK, 256), F32),
            vmem((2, TOK, TOK), BF16),
            vmem((2, TOK, TOK), BF16),
            vmem((2, TOK, D), BF16),
            vmem((2 * TOK, 1536), BF16),
            vmem((12, 2 * TOK, HD), BF16),
            vmem((4, 2 * TOK, HD), BF16),
            vmem((2, 2 * TOK, 512), BF16),
            vmem((2, TOK, D), F32),
            vmem((TOK, D), F32),
            vmem((TOK, D), F32),
            vmem((2, 1, TOK), jnp.int32),
            vmem((TOK, D), F32),
            vmem((2, TOK, D), BF16),
            vmem((2 * TOK, 3072), BF16),
            vmem((3, 2 * TOK, 512), BF16),
            vmem((2, TOK, D), BF16),
            vmem((4, 4, 4, 16, 2 * TOK), BF16),
            vmem((2, 4, 4, 16, 2 * TOK), BF16),
            vmem((8, D), F32),
            pltpu.SemaphoreType.DMA((48,)),
            pltpu.SemaphoreType.DMA((TRANSFERS,)),
            pltpu.SemaphoreType.DMA((TRANSFERS,)),
        ],
        compiler_params=pltpu.CompilerParams(
            collective_id=0, has_side_effects=True, vmem_limit_bytes=64 * 2**20
        ),
        cost_estimate=pl.CostEstimate(flops=26 * 10**9, bytes_accessed=10**7, transcendentals=10**6),
    )(*operands)


def adamw(master, first, second, gradient, rate, decay):
    first_new = 0.9 * first + 0.1 * gradient
    second_new = 0.999 * second + 0.001 * gradient * gradient
    direction = first_new / (1.0 - 0.9**STEP) / (jnp.sqrt(second_new / (1.0 - 0.999**STEP)) + 1e-08)
    return (master - rate * (direction + decay * master), first_new, second_new)


def step_places():
    qkv = [(0, c * 1024, c, S_QKV, 1024) for c in range(2)]
    qkv += [(0, 2048 + c * 512, c, S_QKV + 1024, 512) for c in range(2)]
    qkv += [(0, 3072 + c * 512, c, S_QKV + 1536, 512) for c in range(2)]
    out = [(c, 0, c, S_OUT, 1024) for c in range(2)]
    gate_up = [
        (0, up * 3072 + c * 1536 + half * 768, c, S_GU + half * 1536 + up * 768, 768)
        for up in range(2)
        for c in range(2)
        for half in range(2)
    ]
    down = [(0, 0, 0, S_DN, 1024), (2, 0, 1, S_DN, 1024)]
    down += [(1, c * 512, c, S_DN + 1024, 512) for c in range(2)]
    return qkv, out, gate_up, down


def step_kernel(*refs):
    states, summed, (made, pulled), news = refs[:12], refs[12], refs[13:15], refs[15:]
    news[12][...] = made[...]
    news[13][...] = pulled[...]
    for index, places in enumerate(step_places()):
        master, first, second = states[3 * index : 3 * index + 3]
        for group, column, core, at, size in places:
            here = (group, slice(None), pl.ds(column, size))
            results = adamw(
                master[here],
                first[here],
                second[here],
                summed[core, :, pl.ds(at, size)].astype(F32),
                0.05,
                0.1,
            )
            for ref, value in zip(news[3 * index : 3 * index + 3], results):
                ref[here] = value


def step(masters, firsts, seconds, summed, tokens_out):
    rows = 32
    arrays, specs, shapes = [], [], []
    for state in zip(masters, firsts, seconds):
        for array in state:
            groups = array.shape[0] // 128
            arrays.append(array.reshape(groups, 128, -1))
            specs.append(pl.BlockSpec((groups, rows, array.shape[1]), lambda i: (0, i, 0)))
            shapes.append(jax.ShapeDtypeStruct(arrays[-1].shape, F32))
    token_rows = pl.BlockSpec((TOK * rows // 128, D), lambda i: (i, 0))
    shapes += [jax.ShapeDtypeStruct((TOK, D), BF16)] * 2
    results = pl.pallas_call(
        step_kernel,
        grid=(128 // rows,),
        out_shape=tuple(shapes),
        in_specs=specs + [pl.BlockSpec((2, rows, S_COLS), lambda i: (0, i, 0))] + [token_rows] * 2,
        out_specs=tuple(specs) + (token_rows,) * 2,
        compiler_params=pltpu.CompilerParams(vmem_limit_bytes=62 * 2**20),
        cost_estimate=pl.CostEstimate(flops=3 * 10**7, bytes_accessed=5 * 10**7, transcendentals=10**6),
    )(*arrays, summed, *tokens_out)
    states = [value.reshape(-1, value.shape[2]) for value in results[:12]]
    return [tuple(states[3 * index : 3 * index + 3]) for index in range(4)], results[12:]


def per_device(
    tokens,
    cotangent,
    segment_ids,
    positions,
    master_qkv,
    master_out,
    master_gate_up,
    master_down,
    master_gains,
    first_qkv,
    first_out,
    first_gate_up,
    first_down,
    first_gains,
    second_qkv,
    second_out,
    second_gate_up,
    second_down,
    second_gains,
):
    me = coordinates()
    shard = lax.axis_index("shard")
    order = jnp.minimum((me["y"] % 2) * 4 + me["z"], 2)
    gains = lax.dynamic_slice(
        jnp.pad(master_gains, (2048, 6144)), (2048 + 2048 * order - 288 * shard,), (2048,)
    ).reshape(16, 128)

    activations, input_grad, summed = run_layer(
        tokens,
        cotangent,
        segment_ids,
        positions,
        gains,
        master_qkv,
        master_out,
        master_gate_up,
        master_down,
    )
    summed = summed.reshape(2, 128, S_COLS)
    gain_rows = summed[:, :32, S_GAIN : S_GAIN + 128].astype(F32).sum(axis=0).reshape(-1)
    grad_gains = lax.dynamic_slice(gain_rows, (288 * shard,), (288,))
    updated, (activations, input_grad) = step(
        (master_qkv, master_out, master_gate_up, master_down),
        (first_qkv, first_out, first_gate_up, first_down),
        (second_qkv, second_out, second_gate_up, second_down),
        summed,
        (activations, input_grad),
    )
    updated.append(adamw(master_gains, first_gains, second_gains, grad_gains, 0.4, 0.0))
    return (
        activations,
        input_grad,
        *(new[0] for new in updated),
        *(new[1] for new in updated),
        *(new[2] for new in updated),
    )


def solution(mesh):
    rows = P(("rep", "shard"), None)
    state = (P("shard", None),) * 4 + (P("shard"),)
    return jax.shard_map(
        per_device,
        mesh=mesh,
        in_specs=(rows,) * 4 + state * 3,
        out_specs=(rows,) * 2 + state * 3,
        check_vma=False,
    )
```
